512 devices in a mesh: mic: 16 (over y, core), tm: 32 (over x, z).
Axes of the slice: x: 4, y: 8, z: 8, core: 2. Of those that a mesh axis runs over, the one named last changes fastest.
Arguments:
- frames_in: bfloat16 [16, 4096, 768], P('mic', 'tm'), may hold values from -6 to 6
- cotangent: bfloat16 [16, 4096, 768], P('mic', 'tm'), may hold values from -6 to 6
- norm_gain: float32 [768], replicated, may hold values from 0.25 to 1.75
- w_qkv: bfloat16 [768, 2304], P('tm'), may hold values from -0.21875 to 0.21875
- w_out: bfloat16 [768, 768], P('tm'), may hold values from -0.21875 to 0.21875
- lengths: int32 [2], replicated, may hold values from 512 to 2048, as said below
Outputs:
- output: bfloat16 [16, 4096, 768], P('mic', 'tm')
- grad_input: bfloat16 [16, 4096, 768], P('mic', 'tm')
- grad_wout: float32 [768, 768], P('tm')
The draws below stay inside these ranges and needn't reach their ends.
Inputs may be any that keep to these rules, and one draw needn't show every extreme that they name: Session lengths are between a quarter of a session's 4096 / 2 slots and all of them; at least one session fills all its slots.
All inputs are finite; a program needn't handle non-finite values.
Results may differ from the reference program's by a relative error of at most 0.025.
Values may be sent and summed in bfloat16 or wider, within the bound.
No kernel may reach another device: no remote copies, remote signals or barrier semaphores. Data moves between devices by JAX's collectives and lax.ppermute only.
A program may use at most 64 MiB of HBM per device.

```python
import math
import jax
import jax.numpy as jnp
from jax import lax

D = 768
HD = 64
SESS = 2
MICS = 16
FRAMES = 4096


def draw_lengths(key, part):
    key = jax.random.fold_in(key, 7)
    slot_len = FRAMES // SESS
    first_key, second_key = jax.random.split(key)
    drawn = jax.random.randint(first_key, (SESS,), slot_len // 4, slot_len + 1)
    full_one = jax.random.randint(second_key, (), 0, SESS)
    return jnp.where(jnp.arange(SESS) == full_one, slot_len, drawn).astype(jnp.int32)


def level_of(key, shape, pieces, low, top_value):
    factor_of = 1.0
    for axis_at, blocks in pieces:
        draws = jax.random.uniform(jax.random.fold_in(jax.random.fold_in(key, 6), axis_at), (blocks,), jnp.float32, low / len(pieces), top_value / len(pieces))
        factor_of = factor_of * jnp.repeat(jnp.exp(draws), shape[axis_at] // blocks).reshape((-1,) + (1,) * (len(shape) - 1 - axis_at))
    return factor_of


def gaussian(stream_key, shape, spread, limit, cuts=(), held_as=jnp.bfloat16):
    factor_of = level_of(stream_key, shape, cuts, -0.22, 0.18) if cuts else 1.0
    result = jax.random.normal(stream_key, shape, jnp.float32) * spread * factor_of
    return jnp.minimum(jnp.maximum(result, -limit), limit).astype(held_as)


def setup_inputs(seed: int = 0) -> dict:
    key_list = jax.random.split(jax.random.key(seed), 7)
    return {
        "frames_in": gaussian(key_list[0], (MICS, FRAMES, D), 1.0, 6.0, ((0, 16), (1, 32))),
        "cotangent": gaussian(key_list[1], (MICS, FRAMES, D), 1.0, 6.0, ((0, 16), (1, 32))),
        "norm_gain": jnp.clip(1.0 + 0.15 * jax.random.normal(key_list[2], (D,), jnp.float32), 0.25, 1.75),
        "w_qkv": gaussian(key_list[3], (D, 3 * D), D ** -0.5, 0.21875, ((0, 32),)),
        "w_out": gaussian(key_list[4], (D, D), D ** -0.5, 0.21875, ((0, 32),)),
        "lengths": draw_lengths(jax.random.fold_in(key_list[6], 71), 0),
    }


def contract(form, left, right):
    left = lax.optimization_barrier(left)
    right = lax.optimization_barrier(right)
    return jnp.einsum(form, left.astype(jnp.float32), right.astype(jnp.float32))

def frame_valid(frame_ids, lengths, slot_len):
    session = frame_ids // slot_len
    offset = frame_ids - session * slot_len
    session_hit = (session[:, None] == jnp.arange(lengths.shape[0], dtype=jnp.int32)[None, :]).astype(jnp.int32)
    valid_len = lax.optimization_barrier(jnp.sum(session_hit * lengths[None, :], axis=1))
    return (offset < valid_len).astype(jnp.float32)

def block_math(x_block, g_block, valid_rows, norm_gain, w_qkv, w_out):
    mic_count, frame_count, model_width = x_block.shape
    head_count = model_width // HD
    row_total = mic_count * frame_count
    x_float = x_block.astype(jnp.float32)
    inv_rms = lax.rsqrt(lax.optimization_barrier(jnp.mean(x_float * x_float, axis=-1, keepdims=True)) + 1e-05)
    normed = (x_float * inv_rms * norm_gain).astype(jnp.bfloat16)
    rows_qkv = jnp.dot(normed.reshape(row_total, model_width), w_qkv, preferred_element_type=jnp.float32).astype(jnp.bfloat16)
    split_rows = rows_qkv.reshape(mic_count, frame_count, 3, head_count, HD)
    queries = split_rows[:, :, 0]
    key_part = split_rows[:, :, 1]
    values_part = split_rows[:, :, 2]
    scores = contract('mfhd,nfhd->fhmn', queries, key_part) * HD ** (-0.5)
    softmax_probs = jax.nn.softmax(scores, axis=-1)
    probs_low = softmax_probs.astype(jnp.bfloat16)
    attended = contract('fhmn,nfhd->mfhd', probs_low, values_part).astype(jnp.bfloat16).reshape(row_total, model_width)
    mixed_out = jnp.dot(attended, w_out, preferred_element_type=jnp.float32).reshape(mic_count, frame_count, model_width)
    valid_wide = valid_rows[None, :, None]
    output = (valid_wide * (x_float + mixed_out)).astype(jnp.bfloat16)
    grad_y = g_block.astype(jnp.float32) * valid_wide
    grad_z = grad_y.astype(jnp.bfloat16).reshape(row_total, model_width)
    grad_att = jnp.dot(grad_z, w_out.T, preferred_element_type=jnp.float32).astype(jnp.bfloat16)
    grad_att = grad_att.reshape(mic_count, frame_count, head_count, HD)
    grad_probs = contract('mfhd,nfhd->fhmn', grad_att, values_part)
    grad_scores = softmax_probs * (grad_probs - lax.optimization_barrier(jnp.sum(softmax_probs * grad_probs, axis=-1, keepdims=True))) * HD ** (-0.5)
    grad_low = grad_scores.astype(jnp.bfloat16)
    grad_query = contract('fhmn,nfhd->mfhd', grad_low, key_part)
    grad_key = contract('fhmn,mfhd->nfhd', grad_low, queries)
    grad_value = contract('fhmn,mfhd->nfhd', probs_low, grad_att)
    grad_qkv = jnp.stack([grad_query, grad_key, grad_value], axis=2).astype(jnp.bfloat16).reshape(row_total, 3 * model_width)
    grad_normed = jnp.dot(grad_qkv, w_qkv.T, preferred_element_type=jnp.float32).reshape(mic_count, frame_count, model_width)
    grad_hat = grad_normed * norm_gain
    inner = lax.optimization_barrier(jnp.mean(grad_hat * x_float, axis=-1, keepdims=True))
    grad_x = grad_y + inv_rms * (grad_hat - x_float * inv_rms * inv_rms * inner)
    return (output, grad_x.astype(jnp.bfloat16), attended, grad_z)

def reference(frames_in, cotangent, norm_gain, w_qkv, w_out, lengths):
    mic_count, frame_total, model_width = frames_in.shape
    block_len = math.gcd(frame_total, 256)
    block_count = frame_total // block_len
    x_blocks = frames_in.reshape(mic_count, block_count, block_len, model_width).transpose(1, 0, 2, 3)
    g_blocks = cotangent.reshape(mic_count, block_count, block_len, model_width).transpose(1, 0, 2, 3)
    block_starts = jnp.arange(block_count, dtype=jnp.int32) * block_len

    def scan_step(grad_total, scan_item):
        x_block, g_block, block_start = scan_item
        frame_ids = block_start + jnp.arange(block_len, dtype=jnp.int32)
        valid_rows = frame_valid(frame_ids, lengths, frame_total // SESS)
        output, grad_x, attended, grad_z = block_math(x_block, g_block, valid_rows, norm_gain, w_qkv, w_out)
        grad_total = grad_total + jnp.dot(attended.T, grad_z, preferred_element_type=jnp.float32)
        return (grad_total, (output, grad_x))
    grad_total, (outputs, grads) = lax.scan(scan_step, jnp.zeros((model_width, model_width), jnp.float32), (x_blocks, g_blocks, block_starts))
    outputs = outputs.transpose(1, 0, 2, 3).reshape(mic_count, frame_total, model_width)
    grads = grads.transpose(1, 0, 2, 3).reshape(mic_count, frame_total, model_width)
    return (outputs, grads, grad_total)
```

```python
import jax
import jax.numpy as jnp
from jax import lax
from jax.experimental import pallas as pl
from jax.experimental.pallas import tpu as pltpu
from jax.sharding import Mesh, PartitionSpec as P

HD = 64
SESS = 2
MIC = ("y", "core")
TM = ("x", "z")
NEG = -1e30
VMEM_LIMIT = 56 * 1024 * 1024


def dot_nn(a, b):
    return lax.dot_general(a, b, (((1,), (0,)), ((), ())), preferred_element_type=jnp.float32)


def dot_nt(a, b):
    return lax.dot_general(a, b, (((1,), (1,)), ((), ())), preferred_element_type=jnp.float32)


def dot_tn(a, b):
    return lax.dot_general(a, b, (((0,), (0,)), ((), ())), preferred_element_type=jnp.float32)


def low_half(rows):
    return lax.broadcasted_iota(jnp.int32, (rows, 2 * HD), 1) < HD


def fwd_kernel(frames, xp_ref, gain_ref, w_ref, g_ref, valid_ref, qkv_ref, p_ref, att_ref, gw_ref):
    rows, width = xp_ref.shape
    cores, half = w_ref.shape[1], w_ref.shape[3]
    xf = xp_ref[...].astype(jnp.float32)
    inv = lax.rsqrt(jnp.mean(xf * xf, axis=-1, keepdims=True) + 1e-05)
    normed = (xf * inv * gain_ref[...]).astype(jnp.bfloat16)
    for c in range(cores):
        part = dot_nn(normed, w_ref[:, c].reshape(width, half))
        qkv_ref[:, c * half : (c + 1) * half] = part.astype(jnp.bfloat16)
    row_at = lax.broadcasted_iota(jnp.int32, (rows, rows), 0)
    col_at = lax.broadcasted_iota(jnp.int32, (rows, rows), 1)
    same = lax.rem(row_at, frames) == lax.rem(col_at, frames)
    low = low_half(rows)
    for pair in range(width // (2 * HD)):
        at = pair * 2 * HD
        q = qkv_ref[:, at : at + 2 * HD]
        k = qkv_ref[:, width + at : width + at + 2 * HD]
        v = qkv_ref[:, 2 * width + at : 2 * width + at + 2 * HD]
        mixed = []
        for i in range(2):
            qi = jnp.where(low == (i == 0), q, jnp.zeros_like(q))
            s = jnp.where(same, dot_nt(qi, k) * HD ** (-0.5), NEG)
            e = jnp.exp(s - jnp.max(s, axis=-1, keepdims=True))
            p = e / jnp.sum(e, axis=-1, keepdims=True)
            p_ref[2 * pair + i] = p
            mixed.append(dot_nn(p.astype(jnp.bfloat16), v))
        att_ref[:, at : at + 2 * HD] = jnp.where(low, mixed[0], mixed[1]).astype(jnp.bfloat16)
    gz = (g_ref[...].astype(jnp.float32) * valid_ref[...]).astype(jnp.bfloat16)
    cut = width // cores
    for c in range(cores):
        gw_ref[c] = dot_tn(att_ref[...], gz[:, c * cut : (c + 1) * cut])


def out_kernel(x_ref, att_ref, wo_ref, valid_ref, out_ref):
    cores, _, cut = wo_ref.shape
    for c in range(cores):
        mixed = dot_nn(att_ref[...], wo_ref[c])
        x = x_ref[:, c * cut : (c + 1) * cut].astype(jnp.float32)
        out_ref[:, c * cut : (c + 1) * cut] = (valid_ref[...] * (x + mixed)).astype(jnp.bfloat16)


def bwd_kernel(
    g_ref, valid_ref, wo_ref, qkv_ref, p_ref, xp_ref, gp_ref, gain_ref, w_ref, perm_ref, dx_ref, gqkv_ref
):
    rows, width = xp_ref.shape
    cores, _, cut = wo_ref.shape
    half = w_ref.shape[3]
    valid = valid_ref[...]
    gz = (g_ref[...].astype(jnp.float32) * valid).astype(jnp.bfloat16)
    ga_all = sum(dot_nt(gz[:, c * cut : (c + 1) * cut], wo_ref[c]) for c in range(cores))
    ga_all = ga_all.astype(jnp.bfloat16)
    low = low_half(rows)
    for pair in range(width // (2 * HD)):
        at = pair * 2 * HD
        q = qkv_ref[:, at : at + 2 * HD]
        k = qkv_ref[:, width + at : width + at + 2 * HD]
        v = qkv_ref[:, 2 * width + at : 2 * width + at + 2 * HD]
        ga = ga_all[:, at : at + 2 * HD]
        dq, dk, dv = [], [], []
        for i in range(2):
            gi = jnp.where(low == (i == 0), ga, jnp.zeros_like(ga))
            p = p_ref[2 * pair + i]
            gp = dot_nt(gi, v)
            ds = p * (gp - jnp.sum(p * gp, axis=-1, keepdims=True)) * HD ** (-0.5)
            ds = ds.astype(jnp.bfloat16)
            dq.append(dot_nn(ds, k))
            dk.append(dot_tn(ds, q))
            dv.append(dot_tn(p.astype(jnp.bfloat16), ga))
        for j, grad in enumerate((dq, dk, dv)):
            gqkv_ref[:, j * width + at : j * width + at + 2 * HD] = jnp.where(
                low, grad[0], grad[1]
            ).astype(jnp.bfloat16)
    gh = sum(
        dot_nt(gqkv_ref[:, c * half : (c + 1) * half], w_ref[:, c].reshape(width, half))
        for c in range(cores)
    )
    gh = gh * gain_ref[...]
    xf = xp_ref[...].astype(jnp.float32)
    inv = lax.rsqrt(jnp.mean(xf * xf, axis=-1, keepdims=True) + 1e-05)
    inner = jnp.mean(gh * xf, axis=-1, keepdims=True)
    gy = gp_ref[...].astype(jnp.float32) * valid
    dx = (gy + inv * (gh - xf * inv * inv * inner)).astype(jnp.bfloat16)
    dx_ref[...] = dot_nt(dx, perm_ref[...]).astype(jnp.bfloat16)


def call(kernel, outs, scratch, flops, *operands):
    size = sum(o.size * o.dtype.itemsize for o in outs + operands)
    return pl.pallas_call(
        kernel,
        out_shape=outs,
        scratch_shapes=scratch,
        compiler_params=pltpu.CompilerParams(vmem_limit_bytes=VMEM_LIMIT),
        cost_estimate=pl.CostEstimate(flops=flops, bytes_accessed=size, transcendentals=0),
    )(*operands)


def swap(v, axis):
    return lax.ppermute(v, axis, [(0, 1), (1, 0)])


def exchange(v, axes):
    return lax.all_to_all(v, axes, split_axis=0, concat_axis=0, tiled=True)


def after(v, first):
    return lax.optimization_barrier((v, first))[0]


def per_device(frames_in, cotangent, norm_gain, w_qkv, w_out, lengths):
    bf, f32 = jnp.bfloat16, jnp.float32
    y_at, core_at = lax.axis_index("y"), lax.axis_index("core")
    ys, cores, tms = lax.axis_size("y"), lax.axis_size("core"), lax.axis_size("x") * lax.axis_size("z")
    mics = ys * cores
    frame_dev, width = frames_in.shape[1:]
    frames = frame_dev // mics
    rows = mics * frames
    piece, wide = w_qkv.shape
    rows_y, half, cut = piece // ys, wide // cores, width // cores

    mine = lax.dynamic_slice(w_qkv, (y_at * rows_y, core_at * half), (rows_y, half))
    mine = exchange(jnp.broadcast_to(mine[None], (tms, rows_y, half)), TM).reshape(tms * rows_y, half)
    w_full = lax.all_gather(mine, MIC, axis=0, tiled=False).reshape(ys, cores, tms * rows_y, half)

    both = jnp.concatenate(
        [frames_in.reshape(mics, frames, width), cotangent.reshape(mics, frames, width)], axis=1
    )
    both = exchange(after(both, mine), MIC)

    wo_mine = lax.dynamic_slice(w_out, (0, core_at * cut), (piece, cut))
    wo_mine = after(jnp.broadcast_to(wo_mine[None], (tms, piece, cut)), both)
    wo_mine = exchange(wo_mine, TM).reshape(width, cut)
    wo_other = swap(wo_mine, "core")
    first = core_at == 0
    wo = jnp.stack([jnp.where(first, wo_mine, wo_other), jnp.where(first, wo_other, wo_mine)])

    spot = jnp.arange(width, dtype=jnp.int32)
    block = tms * rows_y
    feature = (spot % block) // rows_y * piece + spot // block * rows_y + spot % rows_y
    perm = (spot[:, None] == feature[None, :]).astype(bf)
    both_p = jnp.dot(both.reshape(2 * rows, width), perm, preferred_element_type=f32).astype(bf)
    both_p = both_p.reshape(mics, 2, frames, width)
    both = both.reshape(mics, 2, frames, width)
    x, g = both[:, 0].reshape(rows, width), both[:, 1].reshape(rows, width)
    xp, gp = both_p[:, 0].reshape(rows, width), both_p[:, 1].reshape(rows, width)
    gain = norm_gain[feature].reshape(1, width)

    first_frame = (lax.axis_index(TM) * mics + lax.axis_index(MIC)) * frames
    frame_ids = first_frame + jnp.arange(frames, dtype=jnp.int32)
    slot_len = frame_dev * tms // SESS
    session = frame_ids // slot_len
    hit = session[:, None] == jnp.arange(lengths.shape[0], dtype=jnp.int32)[None, :]
    valid_len = jnp.sum(jnp.where(hit, lengths[None, :], 0), axis=1)
    valid = (frame_ids - session * slot_len < valid_len).astype(f32)
    valid = jnp.tile(valid, mics).reshape(rows, 1)

    def shape(dims, dtype):
        return jax.ShapeDtypeStruct(dims, dtype)

    heads = width // HD
    big = 2 * rows * width * wide
    qkv, probs, att, gw = call(
        lambda *refs: fwd_kernel(frames, *refs),
        (
            shape((rows, wide), bf),
            shape((heads, rows, rows), f32),
            shape((rows, width), bf),
            shape((cores, width, cut), f32),
        ),
        (),
        2 * big,
        xp, gain, w_full, g, valid,
    )

    keep = lax.dynamic_index_in_dim(gw, core_at, 0, keepdims=False)
    give = lax.dynamic_index_in_dim(gw, 1 - core_at, 0, keepdims=False).astype(bf)
    term = (keep + swap(give, "core").astype(f32)).astype(bf)
    term = exchange(term.reshape(tms, piece, cut), TM)
    term = jnp.sum(term.astype(f32), axis=0).astype(bf)
    term = exchange(jnp.broadcast_to(term[None], (mics, piece, cut)), MIC)
    term = jnp.sum(term.astype(f32).reshape(ys, cores, piece, cut), axis=0)
    grad_wout = term.transpose(1, 0, 2).reshape(piece, width)

    (out,) = call(out_kernel, (shape((rows, width), bf),), (), big // 3, x, att, wo, valid)
    out = exchange(out.reshape(mics, frames, width), MIC).reshape(1, frame_dev, width)
    (dx,) = call(
        bwd_kernel,
        (shape((rows, width), bf),),
        (pltpu.VMEM((rows, wide), bf),),
        3 * big,
        g, valid, wo, qkv, probs, xp, gp, gain, w_full, perm,
    )
    dx = exchange(dx.reshape(mics, frames, width), MIC).reshape(1, frame_dev, width)
    return (out, dx, grad_wout)


def solution(mesh):
    grid = Mesh(mesh.devices.reshape(-1, 2, 4, mesh.devices.shape[1] // 4), ("y", "core", "x", "z"))
    return jax.shard_map(
        per_device,
        mesh=grid,
        in_specs=(P(MIC, TM, None), P(MIC, TM, None), P(), P(TM, None), P(TM, None), P()),
        out_specs=(P(MIC, TM, None), P(MIC, TM, None), P(TM, None)),
        check_vma=False,
    )
```

```python
import jax
import jax.numpy as jnp
from jax import lax
from jax.experimental import pallas as pl
from jax.experimental.pallas import tpu as pltpu
from jax.sharding import Mesh, PartitionSpec as P

HD = 64
SESS = 2
MIC = ("y", "core")
TM = ("x", "z")
NEG = -1e30
VMEM_LIMIT = 56 * 1024 * 1024
FWD_COST, BWD_COST, END_COST = 8_000_000_000, 10_000_000_000, 2_000_000_000


def dot_nn(a, b):
    return lax.dot_general(a, b, (((1,), (0,)), ((), ())), preferred_element_type=jnp.float32)


def dot_nt(a, b):
    return lax.dot_general(a, b, (((1,), (1,)), ((), ())), preferred_element_type=jnp.float32)


def dot_tn(a, b):
    return lax.dot_general(a, b, (((0,), (0,)), ((), ())), preferred_element_type=jnp.float32)


def low_half(rows):
    return lax.broadcasted_iota(jnp.int32, (rows, 2 * HD), 1) < HD


def same_frame(rows, frames):
    row_at = lax.broadcasted_iota(jnp.int32, (rows, rows), 0)
    col_at = lax.broadcasted_iota(jnp.int32, (rows, rows), 1)
    return lax.rem(row_at, frames) == lax.rem(col_at, frames)


def pairs_of(rows, width):
    at = 0
    for start in (0, rows):
        for col in range(0, width, 2 * HD):
            yield start, col, at
            at += 2


def fwd_kernel(
    frames, core_ref, xp_ref, gain_ref, w_ref, g_ref, valid_ref, qkv_ref, p_ref, att_ref, keep_ref, give_ref
):
    width = xp_ref.shape[1]
    rows, mine = xp_ref.shape[0] // 2, att_ref.shape[1]
    xf = xp_ref[...].astype(jnp.float32)
    inv = lax.rsqrt(jnp.mean(xf * xf, axis=-1, keepdims=True) + 1e-05)
    normed = (xf * inv * gain_ref[...]).astype(jnp.bfloat16)
    qkv_ref[...] = dot_nn(normed, w_ref[...].reshape(width, 3 * mine)).astype(jnp.bfloat16)
    same = same_frame(rows, frames)
    low = low_half(rows)
    for start, at, index in pairs_of(rows, mine):
        here = pl.ds(start, rows)
        q = qkv_ref[here, at : at + 2 * HD]
        k = qkv_ref[here, mine + at : mine + at + 2 * HD]
        v = qkv_ref[here, 2 * mine + at : 2 * mine + at + 2 * HD]
        mixed = []
        for i in range(2):
            qi = jnp.where(low == (i == 0), q, jnp.zeros_like(q))
            s = jnp.where(same, dot_nt(qi, k) * HD ** (-0.5), NEG)
            e = jnp.exp(s - jnp.max(s, axis=-1, keepdims=True))
            p = e / jnp.sum(e, axis=-1, keepdims=True)
            p_ref[index + i] = p
            mixed.append(dot_nn(p.astype(jnp.bfloat16), v))
        att_ref[here, at : at + 2 * HD] = jnp.where(low, mixed[0], mixed[1]).astype(jnp.bfloat16)
    gz = (g_ref[...].astype(jnp.float32) * valid_ref[...]).astype(jnp.bfloat16)
    cut = width // 2
    low_cut, high_cut = gz[:, :cut], gz[:, cut:]
    first = core_ref[0] == 0
    att = att_ref[...]
    keep_ref[...] = dot_tn(att, jnp.where(first, low_cut, high_cut)).astype(jnp.bfloat16)
    give_ref[...] = dot_tn(att, jnp.where(first, high_cut, low_cut)).astype(jnp.bfloat16)


def bwd_kernel(
    g_ref, valid_ref, wo_ref, att_ref, qkv_ref, p_ref, w_ref, _, own_ref, other_ref, gqkv_ref
):
    width = g_ref.shape[1]
    rows, mine = g_ref.shape[0] // 2, att_ref.shape[1]
    cut = wo_ref.shape[2]
    att = att_ref[...]
    for c in range(2):
        part = dot_nn(att, wo_ref[c])
        own_ref[:, c * cut : (c + 1) * cut] = part[:rows]
        other_ref[:, c * cut : (c + 1) * cut] = part[rows:].astype(jnp.bfloat16)
    gz = (g_ref[...].astype(jnp.float32) * valid_ref[...]).astype(jnp.bfloat16)
    ga_all = dot_nt(gz[:, :cut], wo_ref[0]) + dot_nt(gz[:, cut:], wo_ref[1])
    ga_all = ga_all.astype(jnp.bfloat16)
    low = low_half(rows)
    for start, at, index in pairs_of(rows, mine):
        here = pl.ds(start, rows)
        q = qkv_ref[here, at : at + 2 * HD]
        k = qkv_ref[here, mine + at : mine + at + 2 * HD]
        v = qkv_ref[here, 2 * mine + at : 2 * mine + at + 2 * HD]
        ga = ga_all[start : start + rows, at : at + 2 * HD]
        dq, dk, dv = [], [], []
        for i in range(2):
            gi = jnp.where(low == (i == 0), ga, jnp.zeros_like(ga))
            p = p_ref[index + i]
            gp = dot_nt(gi, v)
            ds = p * (gp - jnp.sum(p * gp, axis=-1, keepdims=True)) * HD ** (-0.5)
            ds = ds.astype(jnp.bfloat16)
            dq.append(dot_nn(ds, k))
            dk.append(dot_tn(ds, q))
            dv.append(dot_tn(p.astype(jnp.bfloat16), ga))
        for j, grad in enumerate((dq, dk, dv)):
            gqkv_ref[here, j * mine + at : j * mine + at + 2 * HD] = jnp.where(
                low, grad[0], grad[1]
            ).astype(jnp.bfloat16)
    gh = dot_nt(gqkv_ref[...], w_ref[...].reshape(width, 3 * mine))
    own_ref[:, width:] = gh[:rows]
    other_ref[:, width:] = gh[rows:].astype(jnp.bfloat16)


def end_kernel(x_ref, valid_ref, xp_ref, gp_ref, gain_ref, own_ref, got_ref, perm_ref, both_ref):
    width = x_ref.shape[1]
    valid = valid_ref[...]
    mixed = own_ref[:, :width] + got_ref[:, :width].astype(jnp.float32)
    out = valid * (x_ref[...].astype(jnp.float32) + mixed)
    both_ref[:, :width] = out.astype(jnp.bfloat16)
    gh = (own_ref[:, width:] + got_ref[:, width:].astype(jnp.float32)) * gain_ref[...]
    xf = xp_ref[...].astype(jnp.float32)
    inv = lax.rsqrt(jnp.mean(xf * xf, axis=-1, keepdims=True) + 1e-05)
    inner = jnp.mean(gh * xf, axis=-1, keepdims=True)
    gy = gp_ref[...].astype(jnp.float32) * valid
    dx = (gy + inv * (gh - xf * inv * inv * inner)).astype(jnp.bfloat16)
    both_ref[:, width:] = dot_nt(dx, perm_ref[...]).astype(jnp.bfloat16)


def call(kernel, outs, scratch, flops, *operands, behind=()):
    size = sum(o.size * o.dtype.itemsize for o in outs + operands)
    return pl.pallas_call(
        kernel,
        out_shape=outs,
        in_specs=[
            pl.BlockSpec(memory_space=pltpu.SMEM if o.dtype == jnp.int32 else pltpu.VMEM)
            for o in operands
        ]
        + [pl.BlockSpec(memory_space=pl.ANY)] * len(behind),
        scratch_shapes=scratch,
        compiler_params=pltpu.CompilerParams(vmem_limit_bytes=VMEM_LIMIT),
        cost_estimate=pl.CostEstimate(flops=flops, bytes_accessed=size, transcendentals=0),
    )(*operands, *behind)


def swap(v, axis):
    return lax.ppermute(v, axis, [(0, 1), (1, 0)])


def exchange(v, axes):
    return lax.all_to_all(v, axes, split_axis=0, concat_axis=0, tiled=True)


def after(v, first):
    t = first[(0,) * first.ndim]
    return jnp.where(t == t, v, jnp.zeros_like(v))


def valid_of(first_frame, frames, slot_len, lengths):
    frame_ids = first_frame + jnp.arange(frames, dtype=jnp.int32)
    session = frame_ids // slot_len
    hit = session[:, None] == jnp.arange(lengths.shape[0], dtype=jnp.int32)[None, :]
    valid_len = jnp.sum(jnp.where(hit, lengths[None, :], 0), axis=1)
    return (frame_ids - session * slot_len < valid_len).astype(jnp.float32)


def per_device(frames_in, cotangent, norm_gain, w_qkv, w_out, lengths):
    bf, f32 = jnp.bfloat16, jnp.float32
    y_at, core_at = lax.axis_index("y"), lax.axis_index("core")
    ys, cores, tms = lax.axis_size("y"), lax.axis_size("core"), lax.axis_size("x") * lax.axis_size("z")
    mics = ys * cores
    frame_dev, width = frames_in.shape[1:]
    frames = frame_dev // mics
    rows = mics * frames
    piece, wide = w_qkv.shape
    rows_y, half, cut = piece // ys, wide // cores, width // cores
    first = core_at == 0

    mine = jnp.concatenate(
        [
            lax.dynamic_slice(w_qkv, (y_at * rows_y, j * width + core_at * cut), (rows_y, cut))
            for j in range(3)
        ],
        axis=1,
    )
    mine = exchange(jnp.broadcast_to(mine[None], (tms, rows_y, half)), TM)
    w_mine = lax.all_gather(mine.reshape(tms * rows_y, half), "y", axis=0, tiled=False)

    both = jnp.concatenate(
        [frames_in.reshape(mics, frames, width), cotangent.reshape(mics, frames, width)], axis=1
    )
    both = exchange(after(both, mine), MIC)
    next_both = swap(both, "core")

    wo_part = lax.dynamic_slice(w_out, (0, core_at * cut), (piece, cut))
    wo_part = after(jnp.broadcast_to(wo_part[None], (tms, piece, cut)), both)
    wo_part = exchange(wo_part, TM).reshape(cores, cut, cut)
    wo_keep = lax.dynamic_index_in_dim(wo_part, core_at, 0, keepdims=False)
    wo_got = swap(lax.dynamic_index_in_dim(wo_part, 1 - core_at, 0, keepdims=False), "core")
    wo = jnp.stack([jnp.where(first, wo_keep, wo_got), jnp.where(first, wo_got, wo_keep)])

    spot = jnp.arange(width, dtype=jnp.int32)
    block = tms * rows_y
    feature = (spot % block) // rows_y * piece + spot // block * rows_y + spot % rows_y
    perm = (spot[:, None] == feature[None, :]).astype(bf)
    gain = norm_gain[feature].reshape(1, width)
    own, near = both.reshape(mics, 2, frames, width), next_both.reshape(mics, 2, frames, width)
    x, g = own[:, 0].reshape(rows, width), own[:, 1].reshape(rows, width)
    near_x, near_g = near[:, 0].reshape(rows, width), near[:, 1].reshape(rows, width)
    placed = jnp.dot(
        jnp.concatenate([x, near_x, g]), perm, preferred_element_type=f32
    ).astype(bf)
    xp, gp = placed[: 2 * rows], placed[2 * rows :]
    g_all = jnp.concatenate([g, near_g])

    slot_len = frame_dev * tms // SESS
    start = (lax.axis_index(TM) * mics + y_at * cores) * frames
    valid = [
        jnp.tile(valid_of(start + c * frames, frames, slot_len, lengths), mics)
        for c in (core_at, 1 - core_at)
    ]
    valid_own = valid[0].reshape(rows, 1)
    valid_all = jnp.concatenate(valid).reshape(2 * rows, 1)

    def shape(dims, dtype):
        return jax.ShapeDtypeStruct(dims, dtype)

    heads = width // HD
    qkv, probs, att, keep, give = call(
        lambda *refs: fwd_kernel(frames, *refs),
        (
            shape((2 * rows, half), bf),
            shape((heads, rows, rows), f32),
            shape((2 * rows, cut), bf),
            shape((cut, cut), bf),
            shape((cut, cut), bf),
        ),
        (),
        FWD_COST,
        core_at.reshape(1).astype(jnp.int32), xp, gain, w_mine, g_all, valid_all,
    )

    got = swap(give, "core")
    term = jnp.where(first, jnp.concatenate([keep, got]), jnp.concatenate([got, keep]))
    own_part, other_part = call(
        bwd_kernel,
        (shape((rows, 2 * width), f32), shape((rows, 2 * width), bf)),
        (pltpu.VMEM((2 * rows, half), bf),),
        BWD_COST,
        g_all, valid_all, wo, att, qkv, probs, w_mine, behind=(term,),
    )
    term = exchange(term.reshape(tms, piece, cut), TM)
    term = jnp.sum(term.astype(f32), axis=0).astype(bf)
    got_part = swap(other_part, "core")
    (done,) = call(
        end_kernel,
        (shape((rows, 2 * width), bf),),
        (),
        END_COST,
        x, valid_own, xp[:rows], gp, gain, own_part, got_part, perm,
    )

    low = piece // frames
    term = term.reshape(low, frames, cut).transpose(1, 0, 2).reshape(frames, low * cut)
    term = jnp.broadcast_to(term[None], (mics, frames, low * cut))
    sent = jnp.concatenate([done.reshape(mics, frames, 2 * width), term], axis=2)
    sent = exchange(sent, MIC)
    out = sent[:, :, :width].reshape(1, frame_dev, width)
    dx = sent[:, :, width : 2 * width].reshape(1, frame_dev, width)
    term = jnp.sum(sent[:, :, 2 * width :].astype(f32).reshape(ys, cores, frames, low, cut), axis=0)
    grad_wout = term.transpose(2, 1, 0, 3).reshape(piece, width)
    return (out, dx, grad_wout)


def solution(mesh):
    grid = Mesh(mesh.devices.reshape(-1, 2, 4, mesh.devices.shape[1] // 4), ("y", "core", "x", "z"))
    return jax.shard_map(
        per_device,
        mesh=grid,
        in_specs=(P(MIC, TM, None), P(MIC, TM, None), P(), P(TM, None), P(TM, None), P()),
        out_specs=(P(MIC, TM, None), P(MIC, TM, None), P(TM, None)),
        check_vma=False,
    )
```

```python
import jax
import jax.numpy as jnp
from jax import lax
from jax.experimental import pallas as pl
from jax.experimental.pallas import tpu as pltpu
from jax.sharding import Mesh, PartitionSpec as P

HD = 64
SESS = 2
MIC = ("y", "core")
TM = ("x", "z")
NEG = -1e30
VMEM_LIMIT = 56 * 1024 * 1024
FWD_COST, BWD_COST, END_COST = 8_000_000_000, 10_000_000_000, 2_000_000_000


def dot_nn(a, b):
    return lax.dot_general(a, b, (((1,), (0,)), ((), ())), preferred_element_type=jnp.float32)


def dot_nt(a, b):
    return lax.dot_general(a, b, (((1,), (1,)), ((), ())), preferred_element_type=jnp.float32)


def dot_tn(a, b):
    return lax.dot_general(a, b, (((0,), (0,)), ((), ())), preferred_element_type=jnp.float32)


def low_half(rows):
    return lax.broadcasted_iota(jnp.int32, (rows, 2 * HD), 1) < HD


def same_frame(rows, frames):
    row_at = lax.broadcasted_iota(jnp.int32, (rows, rows), 0)
    col_at = lax.broadcasted_iota(jnp.int32, (rows, rows), 1)
    return lax.rem(row_at, frames) == lax.rem(col_at, frames)


def pairs_of(rows, width):
    at = 0
    for start in (0, rows):
        for col in range(0, width, 2 * HD):
            yield start, col, at
            at += 2


def fwd_kernel(
    frames, core_ref, xp_ref, gain_ref, w_ref, g_ref, valid_ref, qkv_ref, p_ref, att_ref, keep_ref, give_ref
):
    width = xp_ref.shape[1]
    rows, mine = xp_ref.shape[0] // 2, att_ref.shape[1]
    xf = xp_ref[...].astype(jnp.float32)
    inv = lax.rsqrt(jnp.mean(xf * xf, axis=-1, keepdims=True) + 1e-05)
    normed = (xf * inv * gain_ref[...]).astype(jnp.bfloat16)
    qkv_ref[...] = dot_nn(normed, w_ref[...].reshape(width, 3 * mine)).astype(jnp.bfloat16)
    same = same_frame(rows, frames)
    low = low_half(rows)
    for start, at, index in pairs_of(rows, mine):
        here = pl.ds(start, rows)
        q = qkv_ref[here, at : at + 2 * HD]
        k = qkv_ref[here, mine + at : mine + at + 2 * HD]
        v = qkv_ref[here, 2 * mine + at : 2 * mine + at + 2 * HD]
        mixed = []
        for i in range(2):
            qi = jnp.where(low == (i == 0), q, jnp.zeros_like(q))
            s = jnp.where(same, dot_nt(qi, k) * HD ** (-0.5), NEG)
            e = jnp.exp(s - jnp.max(s, axis=-1, keepdims=True))
            p = e / jnp.sum(e, axis=-1, keepdims=True)
            p_ref[index + i] = p
            mixed.append(dot_nn(p.astype(jnp.bfloat16), v))
        att_ref[here, at : at + 2 * HD] = jnp.where(low, mixed[0], mixed[1]).astype(jnp.bfloat16)
    gz = (g_ref[...].astype(jnp.float32) * valid_ref[...]).astype(jnp.bfloat16)
    cut = width // 2
    low_cut, high_cut = gz[:, :cut], gz[:, cut:]
    first = core_ref[0] == 0
    att = att_ref[...]
    keep_ref[...] = dot_tn(att, jnp.where(first, low_cut, high_cut)).astype(jnp.bfloat16)
    give_ref[...] = dot_tn(att, jnp.where(first, high_cut, low_cut)).astype(jnp.bfloat16)


def bwd_kernel(
    g_ref, valid_ref, wo_ref, att_ref, qkv_ref, p_ref, w_ref, _, own_ref, other_ref, gqkv_ref
):
    width = g_ref.shape[1]
    rows, mine = g_ref.shape[0] // 2, att_ref.shape[1]
    cut = wo_ref.shape[2]
    att = att_ref[...]
    for c in range(2):
        part = dot_nn(att, wo_ref[c])
        own_ref[:, c * cut : (c + 1) * cut] = part[:rows]
        other_ref[:, c * cut : (c + 1) * cut] = part[rows:].astype(jnp.bfloat16)
    gz = (g_ref[...].astype(jnp.float32) * valid_ref[...]).astype(jnp.bfloat16)
    ga_all = dot_nt(gz[:, :cut], wo_ref[0]) + dot_nt(gz[:, cut:], wo_ref[1])
    ga_all = ga_all.astype(jnp.bfloat16)
    low = low_half(rows)
    for start, at, index in pairs_of(rows, mine):
        here = pl.ds(start, rows)
        q = qkv_ref[here, at : at + 2 * HD]
        k = qkv_ref[here, mine + at : mine + at + 2 * HD]
        v = qkv_ref[here, 2 * mine + at : 2 * mine + at + 2 * HD]
        ga = ga_all[start : start + rows, at : at + 2 * HD]
        dq, dk, dv = [], [], []
        for i in range(2):
            gi = jnp.where(low == (i == 0), ga, jnp.zeros_like(ga))
            p = p_ref[index + i]
            gp = dot_nt(gi, v)
            ds = p * (gp - jnp.sum(p * gp, axis=-1, keepdims=True)) * HD ** (-0.5)
            ds = ds.astype(jnp.bfloat16)
            dq.append(dot_nn(ds, k))
            dk.append(dot_tn(ds, q))
            dv.append(dot_tn(p.astype(jnp.bfloat16), ga))
        for j, grad in enumerate((dq, dk, dv)):
            gqkv_ref[here, j * mine + at : j * mine + at + 2 * HD] = jnp.where(
                low, grad[0], grad[1]
            ).astype(jnp.bfloat16)
    gh = dot_nt(gqkv_ref[...], w_ref[...].reshape(width, 3 * mine))
    own_ref[:, width:] = gh[:rows]
    other_ref[:, width:] = gh[rows:].astype(jnp.bfloat16)


def end_kernel(x_ref, valid_ref, xp_ref, gp_ref, gain_ref, own_ref, got_ref, perm_ref, both_ref):
    width = x_ref.shape[1]
    valid = valid_ref[...]
    mixed = own_ref[:, :width] + got_ref[:, :width].astype(jnp.float32)
    out = valid * (x_ref[...].astype(jnp.float32) + mixed)
    both_ref[:, :width] = out.astype(jnp.bfloat16)
    gh = (own_ref[:, width:] + got_ref[:, width:].astype(jnp.float32)) * gain_ref[...]
    xf = xp_ref[...].astype(jnp.float32)
    inv = lax.rsqrt(jnp.mean(xf * xf, axis=-1, keepdims=True) + 1e-05)
    inner = jnp.mean(gh * xf, axis=-1, keepdims=True)
    gy = gp_ref[...].astype(jnp.float32) * valid
    dx = (gy + inv * (gh - xf * inv * inv * inner)).astype(jnp.bfloat16)
    both_ref[:, width:] = dot_nt(dx, perm_ref[...]).astype(jnp.bfloat16)


def call(kernel, outs, scratch, flops, *operands, behind=()):
    size = sum(o.size * o.dtype.itemsize for o in outs + operands)
    return pl.pallas_call(
        kernel,
        out_shape=outs,
        in_specs=[
            pl.BlockSpec(memory_space=pltpu.SMEM if o.dtype == jnp.int32 else pltpu.VMEM)
            for o in operands
        ]
        + [pl.BlockSpec(memory_space=pl.ANY)] * len(behind),
        scratch_shapes=scratch,
        compiler_params=pltpu.CompilerParams(vmem_limit_bytes=VMEM_LIMIT),
        cost_estimate=pl.CostEstimate(flops=flops, bytes_accessed=size, transcendentals=0),
    )(*operands, *behind)


def swap(v, axis):
    return lax.ppermute(v, axis, [(0, 1), (1, 0)])


def exchange(v, axes):
    return lax.all_to_all(v, axes, split_axis=0, concat_axis=0, tiled=True)


def after(v, first):
    return lax.optimization_barrier((v, first))[0]


def valid_of(first_frame, frames, slot_len, lengths):
    frame_ids = first_frame + jnp.arange(frames, dtype=jnp.int32)
    session = frame_ids // slot_len
    hit = session[:, None] == jnp.arange(lengths.shape[0], dtype=jnp.int32)[None, :]
    valid_len = jnp.sum(jnp.where(hit, lengths[None, :], 0), axis=1)
    return (frame_ids - session * slot_len < valid_len).astype(jnp.float32)


def per_device(frames_in, cotangent, norm_gain, w_qkv, w_out, lengths):
    bf, f32 = jnp.bfloat16, jnp.float32
    y_at, core_at = lax.axis_index("y"), lax.axis_index("core")
    ys, cores = lax.axis_size("y"), lax.axis_size("core")
    xs, zs = lax.axis_size("x"), lax.axis_size("z")
    tms = xs * zs
    mics = ys * cores
    frame_dev, width = frames_in.shape[1:]
    frames = frame_dev // mics
    rows = mics * frames
    piece, wide = w_qkv.shape
    half, cut = wide // cores, width // cores
    first = core_at == 0

    mine = jnp.concatenate(
        [lax.dynamic_slice(w_qkv, (0, j * width + core_at * cut), (piece, cut)) for j in range(3)], axis=1
    )
    mine = exchange(jnp.broadcast_to(mine[None], (xs, piece, half)), "x")
    w_mine = lax.all_gather(mine.reshape(xs * piece, half), "z", axis=0, tiled=False)

    both = jnp.concatenate(
        [frames_in.reshape(mics, frames, width), cotangent.reshape(mics, frames, width)], axis=1
    )
    both = exchange(after(both, mine), MIC)
    next_both = swap(both, "core")

    wo_part = lax.dynamic_slice(w_out, (0, core_at * cut), (piece, cut))
    wo_part = after(jnp.broadcast_to(wo_part[None], (tms, piece, cut)), both)
    wo_part = exchange(wo_part, TM).reshape(cores, cut, cut)

    spot = jnp.arange(width, dtype=jnp.int32)
    feature = (spot // piece % xs * zs + spot // (piece * xs)) * piece + spot % piece
    perm = (spot[:, None] == feature[None, :]).astype(bf)
    gain = norm_gain[feature].reshape(1, width)
    own, near = both.reshape(mics, 2, frames, width), next_both.reshape(mics, 2, frames, width)
    x, g = own[:, 0].reshape(rows, width), own[:, 1].reshape(rows, width)
    near_x, near_g = near[:, 0].reshape(rows, width), near[:, 1].reshape(rows, width)
    placed = jnp.dot(
        jnp.concatenate([x, near_x, g]), perm, preferred_element_type=f32
    ).astype(bf)
    xp, gp = placed[: 2 * rows], placed[2 * rows :]
    g_all = jnp.concatenate([g, near_g])

    slot_len = frame_dev * tms // SESS
    start = (lax.axis_index(TM) * mics + y_at * cores) * frames
    valid = [
        jnp.tile(valid_of(start + c * frames, frames, slot_len, lengths), mics)
        for c in (core_at, 1 - core_at)
    ]
    valid_own = valid[0].reshape(rows, 1)
    valid_all = jnp.concatenate(valid).reshape(2 * rows, 1)

    def shape(dims, dtype):
        return jax.ShapeDtypeStruct(dims, dtype)

    heads = width // HD
    qkv, probs, att, keep, give = call(
        lambda *refs: fwd_kernel(frames, *refs),
        (
            shape((2 * rows, half), bf),
            shape((heads, rows, rows), f32),
            shape((2 * rows, cut), bf),
            shape((cut, cut), bf),
            shape((cut, cut), bf),
        ),
        (),
        FWD_COST,
        core_at.reshape(1).astype(jnp.int32), xp, gain, w_mine, g_all, valid_all,
    )

    wo_part = after(wo_part, keep)
    wo_keep = lax.dynamic_index_in_dim(wo_part, core_at, 0, keepdims=False)
    wo_got = swap(lax.dynamic_index_in_dim(wo_part, 1 - core_at, 0, keepdims=False), "core")
    wo = jnp.stack([jnp.where(first, wo_keep, wo_got), jnp.where(first, wo_got, wo_keep)])

    got = swap(give, "core")
    term = jnp.where(first, jnp.concatenate([keep, got]), jnp.concatenate([got, keep]))
    own_part, other_part = call(
        bwd_kernel,
        (shape((rows, 2 * width), f32), shape((rows, 2 * width), bf)),
        (pltpu.VMEM((2 * rows, half), bf),),
        BWD_COST,
        g_all, valid_all, wo, att, qkv, probs, w_mine, behind=(term,),
    )
    term = exchange(term.reshape(tms, piece, cut), TM)
    term = jnp.sum(term.astype(f32), axis=0).astype(bf)
    got_part = swap(other_part, "core")
    (done,) = call(
        end_kernel,
        (shape((rows, 2 * width), bf),),
        (),
        END_COST,
        x, valid_own, xp[:rows], gp, gain, own_part, got_part, perm,
    )

    low = piece // frames
    term = term.reshape(low, frames, cut).transpose(1, 0, 2).reshape(frames, low * cut)
    term = jnp.broadcast_to(term[None], (mics, frames, low * cut))
    sent = jnp.concatenate([done.reshape(mics, frames, 2 * width), term], axis=2)
    sent = exchange(sent, MIC)
    out = sent[:, :, :width].reshape(1, frame_dev, width)
    dx = sent[:, :, width : 2 * width].reshape(1, frame_dev, width)
    term = jnp.sum(sent[:, :, 2 * width :].astype(f32).reshape(ys, cores, frames, low, cut), axis=0)
    grad_wout = term.transpose(2, 1, 0, 3).reshape(piece, width)
    return (out, dx, grad_wout)


def solution(mesh):
    grid = Mesh(mesh.devices.reshape(-1, 2, 4, mesh.devices.shape[1] // 4), ("y", "core", "x", "z"))
    return jax.shard_map(
        per_device,
        mesh=grid,
        in_specs=(P(MIC, TM, None), P(MIC, TM, None), P(), P(TM, None), P(TM, None), P()),
        out_specs=(P(MIC, TM, None), P(MIC, TM, None), P(TM, None)),
        check_vma=False,
    )
```

```python
import jax
import jax.numpy as jnp
from jax import lax
from jax.experimental import pallas as pl
from jax.experimental.pallas import tpu as pltpu
from jax.sharding import Mesh, PartitionSpec as P

HD = 64
SESS = 2
MIC = ("y", "core")
TM = ("x", "z")
NEG = -1e30
VMEM_LIMIT = 56 * 1024 * 1024
FWD_COST, BWD_COST, END_COST = 8_000_000_000, 1000, 1000


def dot_nn(a, b):
    return lax.dot_general(a, b, (((1,), (0,)), ((), ())), preferred_element_type=jnp.float32)


def dot_nt(a, b):
    return lax.dot_general(a, b, (((1,), (1,)), ((), ())), preferred_element_type=jnp.float32)


def dot_tn(a, b):
    return lax.dot_general(a, b, (((0,), (0,)), ((), ())), preferred_element_type=jnp.float32)


def low_half(rows):
    return lax.broadcasted_iota(jnp.int32, (rows, 2 * HD), 1) < HD


def same_frame(rows, frames):
    row_at = lax.broadcasted_iota(jnp.int32, (rows, rows), 0)
    col_at = lax.broadcasted_iota(jnp.int32, (rows, rows), 1)
    return lax.rem(row_at, frames) == lax.rem(col_at, frames)


def pairs_of(rows, width):
    at = 0
    for start in (0, rows):
        for col in range(0, width, 2 * HD):
            yield start, col, at
            at += 2


def fwd_kernel(
    frames, core_ref, xp_ref, gain_ref, w_ref, g_ref, valid_ref, qkv_ref, p_ref, att_ref, keep_ref, give_ref
):
    width = xp_ref.shape[1]
    rows, mine = xp_ref.shape[0] // 2, att_ref.shape[1]
    xf = xp_ref[...].astype(jnp.float32)
    inv = lax.rsqrt(jnp.mean(xf * xf, axis=-1, keepdims=True) + 1e-05)
    normed = (xf * inv * gain_ref[...]).astype(jnp.bfloat16)
    qkv_ref[...] = dot_nn(normed, w_ref[...].reshape(width, 3 * mine)).astype(jnp.bfloat16)
    same = same_frame(rows, frames)
    low = low_half(rows)
    for start, at, index in pairs_of(rows, mine):
        here = pl.ds(start, rows)
        q = qkv_ref[here, at : at + 2 * HD]
        k = qkv_ref[here, mine + at : mine + at + 2 * HD]
        v = qkv_ref[here, 2 * mine + at : 2 * mine + at + 2 * HD]
        mixed = []
        for i in range(2):
            qi = jnp.where(low == (i == 0), q, jnp.zeros_like(q))
            s = jnp.where(same, dot_nt(qi, k) * HD ** (-0.5), NEG)
            e = jnp.exp(s - jnp.max(s, axis=-1, keepdims=True))
            p = e / jnp.sum(e, axis=-1, keepdims=True)
            p_ref[index + i] = p
            mixed.append(dot_nn(p.astype(jnp.bfloat16), v))
        att_ref[here, at : at + 2 * HD] = jnp.where(low, mixed[0], mixed[1]).astype(jnp.bfloat16)
    gz = (g_ref[...].astype(jnp.float32) * valid_ref[...]).astype(jnp.bfloat16)
    cut = width // 2
    low_cut, high_cut = gz[:, :cut], gz[:, cut:]
    first = core_ref[0] == 0
    att = att_ref[...]
    keep_ref[...] = dot_tn(att, jnp.where(first, low_cut, high_cut)).astype(jnp.bfloat16)
    give_ref[...] = dot_tn(att, jnp.where(first, high_cut, low_cut)).astype(jnp.bfloat16)


def bwd_kernel(
    core_ref, g_ref, valid_ref, wo_ref, att_ref, order_ref, qkv_ref, p_ref, w_ref, _, own_ref, other_ref, gqkv_ref
):
    width = g_ref.shape[1]
    rows, mine = g_ref.shape[0] // 2, att_ref.shape[1]
    wo = wo_ref[:, core_ref[0]].reshape(mine, width)
    part = dot_nn(att_ref[...], wo)
    own_ref[:, :width] = part[:rows]
    other_ref[:, :width] = part[rows:].astype(jnp.bfloat16)
    gz = (g_ref[...].astype(jnp.float32) * valid_ref[...]).astype(jnp.bfloat16)
    ga_all = dot_nt(gz, wo).astype(jnp.bfloat16)
    ga_all = dot_nt(ga_all, order_ref[...]).astype(jnp.bfloat16)
    low = low_half(rows)
    for start, at, index in pairs_of(rows, mine):
        here = pl.ds(start, rows)
        q = qkv_ref[here, at : at + 2 * HD]
        k = qkv_ref[here, mine + at : mine + at + 2 * HD]
        v = qkv_ref[here, 2 * mine + at : 2 * mine + at + 2 * HD]
        ga = ga_all[start : start + rows, at : at + 2 * HD]
        dq, dk, dv = [], [], []
        for i in range(2):
            gi = jnp.where(low == (i == 0), ga, jnp.zeros_like(ga))
            p = p_ref[index + i]
            gp = dot_nt(gi, v)
            ds = p * (gp - jnp.sum(p * gp, axis=-1, keepdims=True)) * HD ** (-0.5)
            ds = ds.astype(jnp.bfloat16)
            dq.append(dot_nn(ds, k))
            dk.append(dot_tn(ds, q))
            dv.append(dot_tn(p.astype(jnp.bfloat16), ga))
        for j, grad in enumerate((dq, dk, dv)):
            gqkv_ref[here, j * mine + at : j * mine + at + 2 * HD] = jnp.where(
                low, grad[0], grad[1]
            ).astype(jnp.bfloat16)
    gh = dot_nt(gqkv_ref[...], w_ref[...].reshape(width, 3 * mine))
    own_ref[:, width:] = gh[:rows]
    other_ref[:, width:] = gh[rows:].astype(jnp.bfloat16)


def end_kernel(x_ref, valid_ref, xp_ref, gp_ref, gain_ref, own_ref, got_ref, perm_ref, both_ref):
    width = x_ref.shape[1]
    valid = valid_ref[...]
    mixed = own_ref[:, :width] + got_ref[:, :width].astype(jnp.float32)
    out = valid * (x_ref[...].astype(jnp.float32) + mixed)
    both_ref[:, :width] = out.astype(jnp.bfloat16)
    gh = (own_ref[:, width:] + got_ref[:, width:].astype(jnp.float32)) * gain_ref[...]
    xf = xp_ref[...].astype(jnp.float32)
    inv = lax.rsqrt(jnp.mean(xf * xf, axis=-1, keepdims=True) + 1e-05)
    inner = jnp.mean(gh * xf, axis=-1, keepdims=True)
    gy = gp_ref[...].astype(jnp.float32) * valid
    dx = (gy + inv * (gh - xf * inv * inv * inner)).astype(jnp.bfloat16)
    both_ref[:, width:] = dot_nt(dx, perm_ref[...]).astype(jnp.bfloat16)


def call(kernel, outs, scratch, flops, *operands, behind=()):
    size = sum(o.size * o.dtype.itemsize for o in outs + operands)
    return pl.pallas_call(
        kernel,
        out_shape=outs,
        in_specs=[
            pl.BlockSpec(memory_space=pltpu.SMEM if o.dtype == jnp.int32 else pltpu.VMEM)
            for o in operands
        ]
        + [pl.BlockSpec(memory_space=pl.ANY)] * len(behind),
        scratch_shapes=scratch,
        compiler_params=pltpu.CompilerParams(vmem_limit_bytes=VMEM_LIMIT),
        cost_estimate=pl.CostEstimate(flops=flops, bytes_accessed=size, transcendentals=0),
    )(*operands, *behind)


def swap(v, axis):
    return lax.ppermute(v, axis, [(0, 1), (1, 0)])


def exchange(v, axes):
    return lax.all_to_all(v, axes, split_axis=0, concat_axis=0, tiled=True)


def after(v, first):
    return lax.optimization_barrier((v, first))[0]


def valid_of(first_frame, frames, slot_len, lengths):
    frame_ids = first_frame + jnp.arange(frames, dtype=jnp.int32)
    session = frame_ids // slot_len
    hit = session[:, None] == jnp.arange(lengths.shape[0], dtype=jnp.int32)[None, :]
    valid_len = jnp.sum(jnp.where(hit, lengths[None, :], 0), axis=1)
    return (frame_ids - session * slot_len < valid_len).astype(jnp.float32)


def per_device(frames_in, cotangent, norm_gain, w_qkv, w_out, lengths):
    bf, f32 = jnp.bfloat16, jnp.float32
    y_at, core_at = lax.axis_index("y"), lax.axis_index("core")
    ys, cores = lax.axis_size("y"), lax.axis_size("core")
    xs, zs = lax.axis_size("x"), lax.axis_size("z")
    tms = xs * zs
    mics = ys * cores
    frame_dev, width = frames_in.shape[1:]
    frames = frame_dev // mics
    rows = mics * frames
    piece, wide = w_qkv.shape
    half, cut = wide // cores, width // cores
    first = core_at == 0
    core = core_at.reshape(1).astype(jnp.int32)

    mine = jnp.concatenate(
        [lax.dynamic_slice(w_qkv, (0, j * width + core_at * cut), (piece, cut)) for j in range(3)], axis=1
    )
    mine = exchange(jnp.broadcast_to(mine[None], (xs, piece, half)), "x")
    w_mine = lax.all_gather(mine.reshape(xs * piece, half), "z", axis=0, tiled=False)

    both = jnp.concatenate(
        [frames_in.reshape(mics, frames, width), cotangent.reshape(mics, frames, width)], axis=1
    )
    both = exchange(after(both, mine), MIC)
    next_both = swap(both, "core")

    wo_part = exchange(after(jnp.broadcast_to(w_out[None], (xs, piece, width)), both), "x")
    wo = lax.all_gather(wo_part.reshape(xs * piece, width), "z", axis=0, tiled=False)
    wo = wo.reshape(zs, cores, xs // cores * piece, width)

    spot = jnp.arange(width, dtype=jnp.int32)
    feature = (spot // piece % xs * zs + spot // (piece * xs)) * piece + spot % piece
    perm = (spot[:, None] == feature[None, :]).astype(bf)
    gain = norm_gain[feature].reshape(1, width)
    own, near = both.reshape(mics, 2, frames, width), next_both.reshape(mics, 2, frames, width)
    x, g = own[:, 0].reshape(rows, width), own[:, 1].reshape(rows, width)
    near_x, near_g = near[:, 0].reshape(rows, width), near[:, 1].reshape(rows, width)
    placed = jnp.dot(
        jnp.concatenate([x, near_x, g]), perm, preferred_element_type=f32
    ).astype(bf)
    xp, gp = placed[: 2 * rows], placed[2 * rows :]
    g_all = jnp.concatenate([g, near_g])

    slot_len = frame_dev * tms // SESS
    start = (lax.axis_index(TM) * mics + y_at * cores) * frames
    valid = [
        jnp.tile(valid_of(start + c * frames, frames, slot_len, lengths), mics)
        for c in (core_at, 1 - core_at)
    ]
    valid_own = valid[0].reshape(rows, 1)
    valid_all = jnp.concatenate(valid).reshape(2 * rows, 1)

    def shape(dims, dtype):
        return jax.ShapeDtypeStruct(dims, dtype)

    heads = width // HD
    qkv, probs, att, keep, give = call(
        lambda *refs: fwd_kernel(frames, *refs),
        (
            shape((2 * rows, half), bf),
            shape((heads, rows, rows), f32),
            shape((2 * rows, cut), bf),
            shape((cut, cut), bf),
            shape((cut, cut), bf),
        ),
        (),
        FWD_COST,
        core, xp, gain, w_mine, g_all, valid_all,
    )

    got = swap(give, "core")
    term = jnp.where(first, jnp.concatenate([keep, got]), jnp.concatenate([got, keep]))
    spot = jnp.arange(cut, dtype=jnp.int32)
    near_xs = xs // cores
    row = (spot // piece % near_xs * zs + spot // (piece * near_xs)) * piece + spot % piece
    order = (spot[:, None] == row[None, :]).astype(bf)
    att = jnp.dot(att, order, preferred_element_type=f32).astype(bf)

    own_part, other_part = call(
        bwd_kernel,
        (shape((rows, 2 * width), f32), shape((rows, 2 * width), bf)),
        (pltpu.VMEM((2 * rows, half), bf),),
        BWD_COST,
        core, g_all, valid_all, after(wo, term), att, order, qkv, probs, w_mine, behind=(term,),
    )
    term = exchange(term.reshape(tms, piece, cut), TM)
    term = jnp.sum(term.astype(f32), axis=0).astype(bf)
    got_part = swap(other_part, "core")
    (done,) = call(
        end_kernel,
        (shape((rows, 2 * width), bf),),
        (),
        END_COST,
        x, valid_own, xp[:rows], gp, gain, own_part, got_part, perm,
    )

    low = piece // frames
    term = term.reshape(low, frames, cut).transpose(1, 0, 2).reshape(frames, low * cut)
    term = jnp.broadcast_to(term[None], (mics, frames, low * cut))
    sent = jnp.concatenate([done.reshape(mics, frames, 2 * width), term], axis=2)
    sent = exchange(sent, MIC)
    out = sent[:, :, :width].reshape(1, frame_dev, width)
    dx = sent[:, :, width : 2 * width].reshape(1, frame_dev, width)
    term = jnp.sum(sent[:, :, 2 * width :].astype(f32).reshape(ys, cores, frames, low, cut), axis=0)
    grad_wout = term.transpose(2, 1, 0, 3).reshape(piece, width)
    return (out, dx, grad_wout)


def solution(mesh):
    grid = Mesh(mesh.devices.reshape(-1, 2, 4, mesh.devices.shape[1] // 4), ("y", "core", "x", "z"))
    return jax.shard_map(
        per_device,
        mesh=grid,
        in_specs=(P(MIC, TM, None), P(MIC, TM, None), P(), P(TM, None), P(TM, None), P()),
        out_specs=(P(MIC, TM, None), P(MIC, TM, None), P(TM, None)),
        check_vma=False,
    )
```

```python
import jax
import jax.numpy as jnp
from jax import lax
from jax.experimental import pallas as pl
from jax.experimental.pallas import tpu as pltpu
from jax.sharding import Mesh, PartitionSpec as P

HD = 64
SESS = 2
MIC = ("y", "core")
TM = ("x", "z")
NEG = -1e30
VMEM_LIMIT = 56 * 1024 * 1024
FWD_COST, BWD_COST, END_COST = 8_000_000_000, 1000, 1000


def dot_nn(a, b):
    return lax.dot_general(a, b, (((1,), (0,)), ((), ())), preferred_element_type=jnp.float32)


def dot_nt(a, b):
    return lax.dot_general(a, b, (((1,), (1,)), ((), ())), preferred_element_type=jnp.float32)


def dot_tn(a, b):
    return lax.dot_general(a, b, (((0,), (0,)), ((), ())), preferred_element_type=jnp.float32)


def low_half(rows):
    return lax.broadcasted_iota(jnp.int32, (rows, 2 * HD), 1) < HD


def same_frame(rows, frames):
    row_at = lax.broadcasted_iota(jnp.int32, (rows, rows), 0)
    col_at = lax.broadcasted_iota(jnp.int32, (rows, rows), 1)
    return lax.rem(row_at, frames) == lax.rem(col_at, frames)


def pairs_of(rows, width):
    at = 0
    for start in (0, rows):
        for col in range(0, width, 2 * HD):
            yield start, col, at
            at += 2


def fwd_kernel(frames, zs, core_ref, xp_ref, gain_ref, g_ref, valid_ref, *refs):
    blocks, (qkv_ref, p_ref, att_ref, keep_ref, give_ref, w_ref) = refs[:zs], refs[zs:]
    rows, mine = xp_ref.shape[0] // 2, att_ref.shape[1]
    width, deep = xp_ref.shape[1], blocks[0].shape[0]
    for i, block in enumerate(blocks):
        w_ref[i * deep : (i + 1) * deep, :] = block[:, : 3 * mine]
    xf = xp_ref[...].astype(jnp.float32)
    inv = lax.rsqrt(jnp.mean(xf * xf, axis=-1, keepdims=True) + 1e-05)
    normed = (xf * inv * gain_ref[...]).astype(jnp.bfloat16)
    qkv_ref[...] = dot_nn(normed, w_ref[...]).astype(jnp.bfloat16)
    same = same_frame(rows, frames)
    low = low_half(rows)
    for start, at, index in pairs_of(rows, mine):
        here = pl.ds(start, rows)
        q = qkv_ref[here, at : at + 2 * HD]
        k = qkv_ref[here, mine + at : mine + at + 2 * HD]
        v = qkv_ref[here, 2 * mine + at : 2 * mine + at + 2 * HD]
        mixed = []
        for i in range(2):
            qi = jnp.where(low == (i == 0), q, jnp.zeros_like(q))
            s = jnp.where(same, dot_nt(qi, k) * HD ** (-0.5), NEG)
            e = jnp.exp(s - jnp.max(s, axis=-1, keepdims=True))
            p = e / jnp.sum(e, axis=-1, keepdims=True)
            p_ref[index + i] = p
            mixed.append(dot_nn(p.astype(jnp.bfloat16), v))
        att_ref[here, at : at + 2 * HD] = jnp.where(low, mixed[0], mixed[1]).astype(jnp.bfloat16)
    gz = (g_ref[...].astype(jnp.float32) * valid_ref[...]).astype(jnp.bfloat16)
    cut = width // 2
    low_cut, high_cut = gz[:, :cut], gz[:, cut:]
    first = core_ref[0] == 0
    att = att_ref[...]
    keep_ref[...] = dot_tn(att, jnp.where(first, low_cut, high_cut)).astype(jnp.bfloat16)
    give_ref[...] = dot_tn(att, jnp.where(first, high_cut, low_cut)).astype(jnp.bfloat16)


def bwd_kernel(zs, g_ref, valid_ref, att_ref, order_ref, qkv_ref, p_ref, *refs):
    blocks, (_, own_ref, other_ref, gqkv_ref, w_ref, wo_ref) = refs[:zs], refs[zs:]
    rows, mine = g_ref.shape[0] // 2, att_ref.shape[1]
    width, deep = g_ref.shape[1], blocks[0].shape[0]
    for i, block in enumerate(blocks):
        w_ref[i * deep : (i + 1) * deep, :] = block[:, : 3 * mine]
        here = pl.ds(i * deep // 2, deep // 2)
        wo_ref[here, :mine] = block[: deep // 2, 3 * mine :]
        wo_ref[here, mine:] = block[deep // 2 :, 3 * mine :]
    wo = wo_ref[...]
    part = dot_nn(att_ref[...], wo)
    own_ref[:, :width] = part[:rows]
    other_ref[:, :width] = part[rows:].astype(jnp.bfloat16)
    gz = (g_ref[...].astype(jnp.float32) * valid_ref[...]).astype(jnp.bfloat16)
    ga_all = dot_nt(gz, wo).astype(jnp.bfloat16)
    ga_all = dot_nt(ga_all, order_ref[...]).astype(jnp.bfloat16)
    low = low_half(rows)
    for start, at, index in pairs_of(rows, mine):
        here = pl.ds(start, rows)
        q = qkv_ref[here, at : at + 2 * HD]
        k = qkv_ref[here, mine + at : mine + at + 2 * HD]
        v = qkv_ref[here, 2 * mine + at : 2 * mine + at + 2 * HD]
        ga = ga_all[start : start + rows, at : at + 2 * HD]
        dq, dk, dv = [], [], []
        for i in range(2):
            gi = jnp.where(low == (i == 0), ga, jnp.zeros_like(ga))
            p = p_ref[index + i]
            gp = dot_nt(gi, v)
            ds = p * (gp - jnp.sum(p * gp, axis=-1, keepdims=True)) * HD ** (-0.5)
            ds = ds.astype(jnp.bfloat16)
            dq.append(dot_nn(ds, k))
            dk.append(dot_tn(ds, q))
            dv.append(dot_tn(p.astype(jnp.bfloat16), ga))
        for j, grad in enumerate((dq, dk, dv)):
            gqkv_ref[here, j * mine + at : j * mine + at + 2 * HD] = jnp.where(
                low, grad[0], grad[1]
            ).astype(jnp.bfloat16)
    gh = dot_nt(gqkv_ref[...], w_ref[...])
    own_ref[:, width:] = gh[:rows]
    other_ref[:, width:] = gh[rows:].astype(jnp.bfloat16)


def end_kernel(x_ref, valid_ref, xp_ref, gp_ref, gain_ref, own_ref, got_ref, perm_ref, both_ref):
    width = x_ref.shape[1]
    valid = valid_ref[...]
    mixed = own_ref[:, :width] + got_ref[:, :width].astype(jnp.float32)
    out = valid * (x_ref[...].astype(jnp.float32) + mixed)
    both_ref[:, :width] = out.astype(jnp.bfloat16)
    gh = (own_ref[:, width:] + got_ref[:, width:].astype(jnp.float32)) * gain_ref[...]
    xf = xp_ref[...].astype(jnp.float32)
    inv = lax.rsqrt(jnp.mean(xf * xf, axis=-1, keepdims=True) + 1e-05)
    inner = jnp.mean(gh * xf, axis=-1, keepdims=True)
    gy = gp_ref[...].astype(jnp.float32) * valid
    dx = (gy + inv * (gh - xf * inv * inv * inner)).astype(jnp.bfloat16)
    both_ref[:, width:] = dot_nt(dx, perm_ref[...]).astype(jnp.bfloat16)


def call(kernel, outs, scratch, flops, *operands, behind=()):
    size = sum(o.size * o.dtype.itemsize for o in outs + operands)
    return pl.pallas_call(
        kernel,
        out_shape=outs,
        in_specs=[
            pl.BlockSpec(memory_space=pltpu.SMEM if o.dtype == jnp.int32 else pltpu.VMEM)
            for o in operands
        ]
        + [pl.BlockSpec(memory_space=pl.ANY)] * len(behind),
        scratch_shapes=scratch,
        compiler_params=pltpu.CompilerParams(vmem_limit_bytes=VMEM_LIMIT),
        cost_estimate=pl.CostEstimate(flops=flops, bytes_accessed=size, transcendentals=0),
    )(*operands, *behind)


def swap(v, axis):
    return lax.ppermute(v, axis, [(0, 1), (1, 0)])


def ring(v, axis, shift, steps):
    size = lax.axis_size(axis)
    got = []
    for _ in range(steps):
        v = lax.ppermute(v, axis, [(i, (i + shift) % size) for i in range(size)])
        got.append(v)
    return got


def exchange(v, axes):
    return lax.all_to_all(v, axes, split_axis=0, concat_axis=0, tiled=True)


def after(v, first):
    return lax.optimization_barrier((v, first))[0]


def valid_of(first_frame, frames, slot_len, lengths):
    frame_ids = first_frame + jnp.arange(frames, dtype=jnp.int32)
    session = frame_ids // slot_len
    hit = session[:, None] == jnp.arange(lengths.shape[0], dtype=jnp.int32)[None, :]
    valid_len = jnp.sum(jnp.where(hit, lengths[None, :], 0), axis=1)
    return (frame_ids - session * slot_len < valid_len).astype(jnp.float32)


def per_device(frames_in, cotangent, norm_gain, w_qkv, w_out, lengths):
    bf, f32 = jnp.bfloat16, jnp.float32
    y_at, core_at = lax.axis_index("y"), lax.axis_index("core")
    ys, cores = lax.axis_size("y"), lax.axis_size("core")
    xs, zs = lax.axis_size("x"), lax.axis_size("z")
    tms = xs * zs
    mics = ys * cores
    frame_dev, width = frames_in.shape[1:]
    frames = frame_dev // mics
    rows = mics * frames
    piece, wide = w_qkv.shape
    half, cut = wide // cores, width // cores
    first = core_at == 0
    core = core_at.reshape(1).astype(jnp.int32)

    mine = jnp.concatenate(
        [lax.dynamic_slice(w_qkv, (0, j * width + core_at * cut), (piece, cut)) for j in range(3)]
        + [w_out],
        axis=1,
    )
    mine = exchange(jnp.broadcast_to(mine[None], (xs, piece, half + width)), "x")
    near_xs = xs // cores
    wo_mine = lax.dynamic_slice_in_dim(mine[:, :, half:], core_at * near_xs, near_xs)
    wo_mine = wo_mine.reshape(near_xs * piece, width)
    wo_mine = jnp.concatenate([wo_mine[:, :cut], wo_mine[:, cut:]])
    block = jnp.concatenate([mine[:, :, :half].reshape(xs * piece, half), wo_mine], axis=1)
    ups, downs = zs // 2, zs - 1 - zs // 2
    blocks = [block] + ring(block, "z", 1, ups) + ring(block, "z", -1, downs)

    both = jnp.concatenate(
        [frames_in.reshape(mics, frames, width), cotangent.reshape(mics, frames, width)], axis=1
    )
    both = exchange(after(both, mine), MIC)
    next_both = swap(both, "core")

    z_at = lax.axis_index("z")

    def order_of(size, block_rows):
        spot = jnp.arange(size, dtype=jnp.int32)
        step, x_of = spot // block_rows, spot % block_rows // piece
        z_of = (z_at + jnp.where(step <= ups, -step, step - ups) + zs) % zs
        return (x_of * zs + z_of) * piece + spot % piece

    feature = order_of(width, xs * piece)
    hit = jnp.arange(width, dtype=jnp.int32)[:, None] == feature[None, :]
    perm = hit.astype(bf)
    gain = jnp.sum(jnp.where(hit, norm_gain[:, None], 0.0), axis=0, keepdims=True)
    own, near = both.reshape(mics, 2, frames, width), next_both.reshape(mics, 2, frames, width)
    x, g = own[:, 0].reshape(rows, width), own[:, 1].reshape(rows, width)
    near_x, near_g = near[:, 0].reshape(rows, width), near[:, 1].reshape(rows, width)
    placed = jnp.dot(
        jnp.concatenate([x, near_x, g]), perm, preferred_element_type=f32
    ).astype(bf)
    xp, gp = placed[: 2 * rows], placed[2 * rows :]
    g_all = jnp.concatenate([g, near_g])

    slot_len = frame_dev * tms // SESS
    start = (lax.axis_index(TM) * mics + y_at * cores) * frames
    valid = [
        jnp.tile(valid_of(start + c * frames, frames, slot_len, lengths), mics)
        for c in (core_at, 1 - core_at)
    ]
    valid_own = valid[0].reshape(rows, 1)
    valid_all = jnp.concatenate(valid).reshape(2 * rows, 1)

    def shape(dims, dtype):
        return jax.ShapeDtypeStruct(dims, dtype)

    heads = width // HD
    qkv, probs, att, keep, give = call(
        lambda *refs: fwd_kernel(frames, zs, *refs),
        (
            shape((2 * rows, half), bf),
            shape((heads, rows, rows), f32),
            shape((2 * rows, cut), bf),
            shape((cut, cut), bf),
            shape((cut, cut), bf),
        ),
        (pltpu.VMEM((width, half), bf),),
        FWD_COST,
        core, xp, gain, g_all, valid_all, *blocks,
    )

    got = swap(give, "core")
    term = jnp.where(first, jnp.concatenate([keep, got]), jnp.concatenate([got, keep]))
    row = order_of(cut, near_xs * piece)
    order = (jnp.arange(cut, dtype=jnp.int32)[:, None] == row[None, :]).astype(bf)
    att = jnp.dot(att, order, preferred_element_type=f32).astype(bf)

    own_part, other_part = call(
        lambda *refs: bwd_kernel(zs, *refs),
        (shape((rows, 2 * width), f32), shape((rows, 2 * width), bf)),
        (
            pltpu.VMEM((2 * rows, half), bf),
            pltpu.VMEM((width, half), bf),
            pltpu.VMEM((cut, width), bf),
        ),
        BWD_COST,
        g_all, valid_all, att, order, qkv, probs, *blocks, behind=(term,),
    )
    term = exchange(term.reshape(tms, piece, cut), TM)
    term = jnp.sum(term.astype(f32), axis=0).astype(bf)
    got_part = swap(other_part, "core")
    (done,) = call(
        end_kernel,
        (shape((rows, 2 * width), bf),),
        (),
        END_COST,
        x, valid_own, xp[:rows], gp, gain, own_part, got_part, perm,
    )

    low = piece // frames
    term = term.reshape(low, frames, cut).transpose(1, 0, 2).reshape(frames, low * cut)
    term = jnp.broadcast_to(term[None], (mics, frames, low * cut))
    sent = jnp.concatenate([done.reshape(mics, frames, 2 * width), term], axis=2)
    sent = exchange(sent, MIC)
    out = sent[:, :, :width].reshape(1, frame_dev, width)
    dx = sent[:, :, width : 2 * width].reshape(1, frame_dev, width)
    term = jnp.sum(sent[:, :, 2 * width :].astype(f32).reshape(ys, cores, frames, low, cut), axis=0)
    grad_wout = term.transpose(2, 1, 0, 3).reshape(piece, width)
    return (out, dx, grad_wout)


def solution(mesh):
    grid = Mesh(mesh.devices.reshape(-1, 2, 4, mesh.devices.shape[1] // 4), ("y", "core", "x", "z"))
    return jax.shard_map(
        per_device,
        mesh=grid,
        in_specs=(P(MIC, TM, None), P(MIC, TM, None), P(), P(TM, None), P(TM, None), P()),
        out_specs=(P(MIC, TM, None), P(MIC, TM, None), P(TM, None)),
        check_vma=False,
    )
```

```python
import jax
import jax.numpy as jnp
from jax import lax
from jax.experimental import pallas as pl
from jax.experimental.pallas import tpu as pltpu
from jax.sharding import Mesh, PartitionSpec as P

HD = 64
SESS = 2
XS = 4
MIC = ("y", "core")
TM = ("x", "z")
NEG = -1e30
VMEM_LIMIT = 56 * 1024 * 1024
FWD_COST, BWD_COST, END_COST = 8_000_000_000, 1000, 1000


def dot_nn(a, b):
    return lax.dot_general(a, b, (((1,), (0,)), ((), ())), preferred_element_type=jnp.float32)


def dot_nt(a, b):
    return lax.dot_general(a, b, (((1,), (1,)), ((), ())), preferred_element_type=jnp.float32)


def dot_tn(a, b):
    return lax.dot_general(a, b, (((0,), (0,)), ((), ())), preferred_element_type=jnp.float32)


def low_half(rows):
    return lax.broadcasted_iota(jnp.int32, (rows, 2 * HD), 1) < HD


def same_frame(rows, frames):
    row_at = lax.broadcasted_iota(jnp.int32, (rows, rows), 0)
    col_at = lax.broadcasted_iota(jnp.int32, (rows, rows), 1)
    return lax.rem(row_at, frames) == lax.rem(col_at, frames)


def valid_rows(rows, frames, left):
    frame = lax.rem(lax.broadcasted_iota(jnp.int32, (rows, 1), 0), frames)
    return (frame < left).astype(jnp.float32)


def masked_grad(frames, scalars, own_ref, near_ref):
    rows, width = own_ref.shape[0], own_ref.shape[1] // 2
    parts = [
        (ref[:, width:].astype(jnp.float32) * valid_rows(rows, frames, scalars[1 + i])).astype(
            jnp.bfloat16
        )
        for i, ref in enumerate((own_ref, near_ref))
    ]
    return jnp.concatenate(parts)


def pairs_of(rows, width):
    at = 0
    for start in (0, rows):
        for col in range(0, width, 2 * HD):
            yield start, col, at
            at += 2


def inv_rms_of(x):
    return lax.rsqrt(jnp.mean(x * x, axis=-1, keepdims=True) + 1e-05)


def fwd_kernel(
    frames,
    scalars,
    own_ref,
    near_ref,
    gain_ref,
    block_ref,
    up_ref,
    down_ref,
    far_low_ref,
    far_high_ref,
    qkv_ref,
    p_ref,
    att_ref,
    w_ref,
    wo_ref,
    give_ref,
    gw_ref,
    all_ref,
):
    rows, width = own_ref.shape[0], own_ref.shape[1] // 2
    mine, deep = att_ref.shape[1], block_ref.shape[0]
    core, x_at = scalars[0], scalars[3]
    first = core == 0
    far = lax.rem(x_at + 2, XS) * deep
    places = (
        (block_ref, x_at * deep),
        (up_ref, lax.rem(x_at + XS - 1, XS) * deep),
        (down_ref, lax.rem(x_at + 1, XS) * deep),
        (far_low_ref, far),
        (far_high_ref, far + deep // 2),
    )
    for ref, at in places:
        here = pl.ds(pl.multiple_of(at, deep // 2), ref.shape[0])
        w_ref[here, :] = ref[:, : 3 * mine]
        all_ref[here, :] = ref[:, 3 * mine :]
    mid = width // 2
    wo_ref[...] = all_ref[pl.ds(pl.multiple_of(core * mid, mid), mid), :]
    give_ref[mid:, :] = all_ref[pl.ds(pl.multiple_of((1 - core) * mid, mid), mid), :]

    for i, ref in enumerate((own_ref, near_ref)):
        x = ref[:, :width].astype(jnp.float32)
        normed = (x * inv_rms_of(x) * gain_ref[...]).astype(jnp.bfloat16)
        qkv_ref[i * rows : (i + 1) * rows, :] = normed_dot(normed, w_ref)
    same = same_frame(rows, frames)
    low = low_half(rows)
    for start, at, index in pairs_of(rows, mine):
        here = pl.ds(start, rows)
        q = qkv_ref[here, at : at + 2 * HD]
        k = qkv_ref[here, mine + at : mine + at + 2 * HD]
        v = qkv_ref[here, 2 * mine + at : 2 * mine + at + 2 * HD]
        mixed = []
        for i in range(2):
            qi = jnp.where(low == (i == 0), q, jnp.zeros_like(q))
            s = jnp.where(same, dot_nt(qi, k) * HD ** (-0.5), NEG)
            e = jnp.exp(s - jnp.max(s, axis=-1, keepdims=True))
            p = e / jnp.sum(e, axis=-1, keepdims=True)
            p_ref[index + i] = p
            mixed.append(dot_nn(p.astype(jnp.bfloat16), v))
        att_ref[here, at : at + 2 * HD] = jnp.where(low, mixed[0], mixed[1]).astype(jnp.bfloat16)
    gz = masked_grad(frames, scalars, own_ref, near_ref)
    low_cols, high_cols = gz[:, :mid], gz[:, mid:]
    att = att_ref[...]
    keep = dot_tn(att, jnp.where(first, low_cols, high_cols))
    gw_ref[pl.ds(pl.multiple_of(core * mid, mid), mid), :] = keep.astype(jnp.bfloat16)
    give_ref[:mid, :] = dot_tn(att, jnp.where(first, high_cols, low_cols)).astype(jnp.bfloat16)


def normed_dot(normed, w_ref):
    return dot_nn(normed, w_ref[...]).astype(jnp.bfloat16)


def bwd_kernel(
    frames,
    scalars,
    own_ref,
    near_ref,
    wo_ref,
    got_ref,
    att_ref,
    qkv_ref,
    p_ref,
    w_ref,
    _,
    sum_ref,
    other_ref,
    gqkv_ref,
):
    rows, width = own_ref.shape[0], own_ref.shape[1] // 2
    mine, mid = att_ref.shape[1], width // 2
    first = scalars[0] == 0
    att = att_ref[...]
    kept, got = dot_nn(att, wo_ref[...]), dot_nn(att, got_ref[mid:, :])
    for at, part in ((0, jnp.where(first, kept, got)), (mid, jnp.where(first, got, kept))):
        sum_ref[:, at : at + mid] = part[:rows]
        other_ref[:, at : at + mid] = part[rows:].astype(jnp.bfloat16)
    gz = masked_grad(frames, scalars, own_ref, near_ref)
    low_cols, high_cols = gz[:, :mid], gz[:, mid:]
    ga_all = dot_nt(jnp.where(first, low_cols, high_cols), wo_ref[...])
    ga_all += dot_nt(jnp.where(first, high_cols, low_cols), got_ref[mid:, :])
    ga_all = ga_all.astype(jnp.bfloat16)
    low = low_half(rows)
    for start, at, index in pairs_of(rows, mine):
        here = pl.ds(start, rows)
        q = qkv_ref[here, at : at + 2 * HD]
        k = qkv_ref[here, mine + at : mine + at + 2 * HD]
        v = qkv_ref[here, 2 * mine + at : 2 * mine + at + 2 * HD]
        ga = ga_all[start : start + rows, at : at + 2 * HD]
        dq, dk, dv = [], [], []
        for i in range(2):
            gi = jnp.where(low == (i == 0), ga, jnp.zeros_like(ga))
            p = p_ref[index + i]
            gp = dot_nt(gi, v)
            ds = p * (gp - jnp.sum(p * gp, axis=-1, keepdims=True)) * HD ** (-0.5)
            ds = ds.astype(jnp.bfloat16)
            dq.append(dot_nn(ds, k))
            dk.append(dot_tn(ds, q))
            dv.append(dot_tn(p.astype(jnp.bfloat16), ga))
        for j, grad in enumerate((dq, dk, dv)):
            gqkv_ref[here, j * mine + at : j * mine + at + 2 * HD] = jnp.where(
                low, grad[0], grad[1]
            ).astype(jnp.bfloat16)
    gh = dot_nt(gqkv_ref[...], w_ref[...])
    sum_ref[:, width:] = gh[:rows]
    other_ref[:, width:] = gh[rows:].astype(jnp.bfloat16)


def end_kernel(frames, scalars, own_ref, gain_ref, sum_ref, got_ref, both_ref):
    rows, width = own_ref.shape[0], own_ref.shape[1] // 2
    valid = valid_rows(rows, frames, scalars[1])
    x = own_ref[:, :width].astype(jnp.float32)
    mixed = sum_ref[:, :width] + got_ref[:, :width].astype(jnp.float32)
    both_ref[:, :width] = (valid * (x + mixed)).astype(jnp.bfloat16)
    gh = (sum_ref[:, width:] + got_ref[:, width:].astype(jnp.float32)) * gain_ref[...]
    inv = inv_rms_of(x)
    inner = jnp.mean(gh * x, axis=-1, keepdims=True)
    gy = own_ref[:, width:].astype(jnp.float32) * valid
    both_ref[:, width:] = (gy + inv * (gh - x * inv * inv * inner)).astype(jnp.bfloat16)


def call(kernel, outs, scratch, flops, *operands, behind=()):
    size = sum(o.size * o.dtype.itemsize for o in outs + operands)
    return pl.pallas_call(
        kernel,
        out_shape=outs,
        in_specs=[
            pl.BlockSpec(memory_space=pltpu.SMEM if o.dtype == jnp.int32 else pltpu.VMEM)
            for o in operands
        ]
        + [pl.BlockSpec(memory_space=pl.ANY)] * len(behind),
        scratch_shapes=scratch,
        compiler_params=pltpu.CompilerParams(vmem_limit_bytes=VMEM_LIMIT),
        cost_estimate=pl.CostEstimate(flops=flops, bytes_accessed=size, transcendentals=0),
    )(*operands, *behind)


def shift(v, axis, by):
    size = lax.axis_size(axis)
    return lax.ppermute(v, axis, [(i, (i + by) % size) for i in range(size)])


def exchange(v, axes):
    return lax.all_to_all(v, axes, split_axis=0, concat_axis=0, tiled=True)


def after(v, first):
    return lax.optimization_barrier((v, first))[0]


def per_device(frames_in, cotangent, norm_gain, w_qkv, w_out, lengths):
    bf, f32 = jnp.bfloat16, jnp.float32
    y_at, core_at, x_at = (lax.axis_index(axis) for axis in ("y", "core", "x"))
    ys, cores, zs = (lax.axis_size(axis) for axis in ("y", "core", "z"))
    tms, mics = XS * zs, ys * cores
    frame_dev, width = frames_in.shape[1:]
    frames = frame_dev // mics
    rows = mics * frames
    piece, wide = w_qkv.shape
    half, cut = wide // cores, width // cores

    mine = [lax.dynamic_slice(w_qkv, (0, j * width + core_at * cut), (piece, cut)) for j in range(3)]
    mine.append(lax.dynamic_slice(w_out, (0, core_at * cut), (piece, cut)))
    mine = jnp.concatenate(mine, axis=1)
    block = exchange(jnp.broadcast_to(mine[None], (zs, piece, half + cut)), "z")
    block = block.reshape(zs * piece, half + cut)
    up, down = shift(block, "x", 1), shift(block, "x", -1)
    mid = zs * piece // 2
    far_low, far_high = shift(up[:mid], "x", 1), shift(down[mid:], "x", -1)

    both = jnp.concatenate(
        [frames_in.reshape(mics, frames, width), cotangent.reshape(mics, frames, width)], axis=2
    )
    own = exchange(after(both, block), MIC).reshape(rows, 2 * width)
    near = shift(own, "core", 1)

    slot_len = frame_dev * tms // SESS
    start = lax.axis_index(TM) * frame_dev
    session = start // slot_len
    left = lengths[session] + session * slot_len - start - y_at * cores * frames
    scalars = [core_at, left - core_at * frames, left - (1 - core_at) * frames, x_at]
    scalars = jnp.stack(scalars).astype(jnp.int32)
    gain = norm_gain.reshape(1, width)

    def shape(dims, dtype):
        return jax.ShapeDtypeStruct(dims, dtype)

    heads = width // HD
    qkv, probs, att, w, wo, give, gw = call(
        lambda *refs: fwd_kernel(frames, *refs),
        (
            shape((2 * rows, half), bf),
            shape((heads, rows, rows), f32),
            shape((2 * rows, cut), bf),
            shape((width, half), bf),
            shape((cut, cut), bf),
            shape((width, cut), bf),
            shape((width, cut), bf),
        ),
        (pltpu.VMEM((width, cut), bf),),
        FWD_COST,
        scalars, own, near, gain, block, up, down, far_low, far_high,
    )

    got = shift(give, "core", 1)
    term = lax.dynamic_update_slice(gw, got[:cut], ((1 - core_at) * cut, 0))

    sum_part, other_part = call(
        lambda *refs: bwd_kernel(frames, *refs),
        (shape((rows, 2 * width), f32), shape((rows, 2 * width), bf)),
        (pltpu.VMEM((2 * rows, half), bf),),
        BWD_COST,
        scalars, own, near, wo, got, att, qkv, probs, w, behind=(term,),
    )
    term = exchange(term.reshape(tms, piece, cut), TM)
    term = jnp.sum(term.astype(f32), axis=0).astype(bf)
    got_part = shift(other_part, "core", 1)
    (done,) = call(
        lambda *refs: end_kernel(frames, *refs),
        (shape((rows, 2 * width), bf),),
        (),
        END_COST,
        scalars, own, gain, sum_part, got_part,
    )

    low = piece // frames
    term = term.reshape(low, frames, cut).transpose(1, 0, 2).reshape(frames, low * cut)
    term = jnp.broadcast_to(term[None], (mics, frames, low * cut))
    sent = jnp.concatenate([done.reshape(mics, frames, 2 * width), term], axis=2)
    sent = exchange(sent, MIC)
    out = sent[:, :, :width].reshape(1, frame_dev, width)
    dx = sent[:, :, width : 2 * width].reshape(1, frame_dev, width)
    term = jnp.sum(sent[:, :, 2 * width :].astype(f32).reshape(ys, cores, frames, low, cut), axis=0)
    grad_wout = term.transpose(2, 1, 0, 3).reshape(piece, width)
    return (out, dx, grad_wout)


def solution(mesh):
    grid = Mesh(mesh.devices.reshape(-1, 2, XS, mesh.devices.shape[1] // XS), ("y", "core", "x", "z"))
    return jax.shard_map(
        per_device,
        mesh=grid,
        in_specs=(P(MIC, TM, None), P(MIC, TM, None), P(), P(TM, None), P(TM, None), P()),
        out_specs=(P(MIC, TM, None), P(MIC, TM, None), P(TM, None)),
        check_vma=False,
    )
```

```python
import jax
import jax.numpy as jnp
from jax import lax
from jax.experimental import pallas as pl
from jax.experimental.pallas import tpu as pltpu
from jax.sharding import Mesh, PartitionSpec as P

HD = 64
SESS = 2
XS = 4
MIC = ("y", "core")
TM = ("x", "z")
NEG = -1e30
VMEM_LIMIT = 56 * 1024 * 1024
FWD_COST, BWD_COST, END_COST, HALVES_COST = 8_000_000_000, 1000, 1000, 20_000_000_000


def dot_nn(a, b):
    return lax.dot_general(a, b, (((1,), (0,)), ((), ())), preferred_element_type=jnp.float32)


def dot_nt(a, b):
    return lax.dot_general(a, b, (((1,), (1,)), ((), ())), preferred_element_type=jnp.float32)


def dot_tn(a, b):
    return lax.dot_general(a, b, (((0,), (0,)), ((), ())), preferred_element_type=jnp.float32)


def low_half(rows):
    return lax.broadcasted_iota(jnp.int32, (rows, 2 * HD), 1) < HD


def same_frame(rows, frames):
    row_at = lax.broadcasted_iota(jnp.int32, (rows, rows), 0)
    col_at = lax.broadcasted_iota(jnp.int32, (rows, rows), 1)
    return lax.rem(row_at, frames) == lax.rem(col_at, frames)


def valid_rows(rows, frames, left):
    frame = lax.rem(lax.broadcasted_iota(jnp.int32, (rows, 1), 0), frames)
    return (frame < left).astype(jnp.float32)


def masked_grad(frames, scalars, own_ref, near_ref):
    rows, width = own_ref.shape[0], own_ref.shape[1] // 2
    parts = [
        (ref[:, width:].astype(jnp.float32) * valid_rows(rows, frames, scalars[1 + i])).astype(
            jnp.bfloat16
        )
        for i, ref in enumerate((own_ref, near_ref))
    ]
    return jnp.concatenate(parts)


def inv_rms_of(x):
    return lax.rsqrt(jnp.mean(x * x, axis=-1, keepdims=True) + 1e-05)


def attend(same, qkv_ref, p_ref, att_ref):
    rows, mine = att_ref.shape
    low = low_half(rows)
    for index, at in enumerate(range(0, mine, 2 * HD)):
        q = qkv_ref[:, at : at + 2 * HD]
        k = qkv_ref[:, mine + at : mine + at + 2 * HD]
        v = qkv_ref[:, 2 * mine + at : 2 * mine + at + 2 * HD]
        mixed = []
        for i in range(2):
            qi = jnp.where(low == (i == 0), q, jnp.zeros_like(q))
            s = jnp.where(same, dot_nt(qi, k) * HD ** (-0.5), NEG)
            e = jnp.exp(s - jnp.max(s, axis=-1, keepdims=True))
            p = e / jnp.sum(e, axis=-1, keepdims=True)
            p_ref[2 * index + i] = p
            mixed.append(dot_nn(p.astype(jnp.bfloat16), v))
        att_ref[:, at : at + 2 * HD] = jnp.where(low, mixed[0], mixed[1]).astype(jnp.bfloat16)


def project(rows_ref, gain_ref, w_ref, qkv_ref):
    x = rows_ref[:, : w_ref.shape[0]].astype(jnp.float32)
    normed = (x * inv_rms_of(x) * gain_ref[...]).astype(jnp.bfloat16)
    qkv_ref[...] = dot_nn(normed, w_ref[...]).astype(jnp.bfloat16)


def own_kernel(
    frames,
    scalars,
    own_ref,
    gain_ref,
    block_ref,
    up_ref,
    down_ref,
    far_low_ref,
    far_high_ref,
    qkv_ref,
    p_ref,
    att_ref,
    w_ref,
    wo_ref,
    give_ref,
    all_ref,
):
    rows, mine = att_ref.shape
    width, deep = w_ref.shape[0], block_ref.shape[0]
    core, x_at = scalars[0], scalars[3]
    far = lax.rem(x_at + 2, XS) * deep
    places = (
        (block_ref, x_at * deep),
        (up_ref, lax.rem(x_at + XS - 1, XS) * deep),
        (down_ref, lax.rem(x_at + 1, XS) * deep),
        (far_low_ref, far),
        (far_high_ref, far + deep // 2),
    )
    for ref, at in places:
        here = pl.ds(pl.multiple_of(at, deep // 2), ref.shape[0])
        w_ref[here, :] = ref[:, : 3 * mine]
        all_ref[here, :] = ref[:, 3 * mine :]
    mid = width // 2
    wo_ref[...] = all_ref[pl.ds(pl.multiple_of(core * mid, mid), mid), :]
    give_ref[...] = all_ref[pl.ds(pl.multiple_of((1 - core) * mid, mid), mid), :]
    project(own_ref, gain_ref, w_ref, qkv_ref)
    attend(same_frame(rows, frames), qkv_ref, p_ref, att_ref)


def near_kernel(
    frames,
    scalars,
    own_ref,
    near_ref,
    gain_ref,
    w_ref,
    own_att_ref,
    qkv_ref,
    p_ref,
    att_ref,
    give_ref,
    gw_ref,
):
    project(near_ref, gain_ref, w_ref, qkv_ref)
    attend(same_frame(att_ref.shape[0], frames), qkv_ref, p_ref, att_ref)
    core, mid = scalars[0], w_ref.shape[0] // 2
    first = core == 0
    gz = masked_grad(frames, scalars, own_ref, near_ref)
    low_cols, high_cols = gz[:, :mid], gz[:, mid:]
    att = jnp.concatenate([own_att_ref[...], att_ref[...]])
    keep = dot_tn(att, jnp.where(first, low_cols, high_cols))
    gw_ref[pl.ds(pl.multiple_of(core * mid, mid), mid), :] = keep.astype(jnp.bfloat16)
    give_ref[...] = dot_tn(att, jnp.where(first, high_cols, low_cols)).astype(jnp.bfloat16)


def bwd_kernel(
    frames,
    scalars,
    own_ref,
    near_ref,
    wo_ref,
    got_ref,
    own_att_ref,
    near_att_ref,
    own_qkv_ref,
    near_qkv_ref,
    own_p_ref,
    near_p_ref,
    w_ref,
    _,
    sum_ref,
    other_ref,
    gqkv_ref,
):
    rows, width = own_ref.shape[0], own_ref.shape[1] // 2
    mine, mid = own_att_ref.shape[1], width // 2
    first = scalars[0] == 0
    att = jnp.concatenate([own_att_ref[...], near_att_ref[...]])
    kept, got = dot_nn(att, wo_ref[...]), dot_nn(att, got_ref[...])
    for at, part in ((0, jnp.where(first, kept, got)), (mid, jnp.where(first, got, kept))):
        sum_ref[:, at : at + mid] = part[:rows]
        other_ref[:, at : at + mid] = part[rows:].astype(jnp.bfloat16)
    gz = masked_grad(frames, scalars, own_ref, near_ref)
    low_cols, high_cols = gz[:, :mid], gz[:, mid:]
    ga_all = dot_nt(jnp.where(first, low_cols, high_cols), wo_ref[...])
    ga_all += dot_nt(jnp.where(first, high_cols, low_cols), got_ref[...])
    ga_all = ga_all.astype(jnp.bfloat16)
    low = low_half(rows)
    sets = ((0, own_qkv_ref, own_p_ref), (rows, near_qkv_ref, near_p_ref))
    for start, qkv_ref, p_ref in sets:
        for index, at in enumerate(range(0, mine, 2 * HD)):
            q = qkv_ref[:, at : at + 2 * HD]
            k = qkv_ref[:, mine + at : mine + at + 2 * HD]
            v = qkv_ref[:, 2 * mine + at : 2 * mine + at + 2 * HD]
            ga = ga_all[start : start + rows, at : at + 2 * HD]
            dq, dk, dv = [], [], []
            for i in range(2):
                gi = jnp.where(low == (i == 0), ga, jnp.zeros_like(ga))
                p = p_ref[2 * index + i]
                gp = dot_nt(gi, v)
                ds = p * (gp - jnp.sum(p * gp, axis=-1, keepdims=True)) * HD ** (-0.5)
                ds = ds.astype(jnp.bfloat16)
                dq.append(dot_nn(ds, k))
                dk.append(dot_tn(ds, q))
                dv.append(dot_tn(p.astype(jnp.bfloat16), ga))
            for j, grad in enumerate((dq, dk, dv)):
                gqkv_ref[start : start + rows, j * mine + at : j * mine + at + 2 * HD] = jnp.where(
                    low, grad[0], grad[1]
                ).astype(jnp.bfloat16)
    gh = dot_nt(gqkv_ref[...], w_ref[...])
    sum_ref[:, width:] = gh[:rows]
    other_ref[:, width:] = gh[rows:].astype(jnp.bfloat16)


def end_kernel(frames, scalars, own_ref, gain_ref, sum_ref, got_ref, both_ref):
    rows, width = own_ref.shape[0], own_ref.shape[1] // 2
    valid = valid_rows(rows, frames, scalars[1])
    x = own_ref[:, :width].astype(jnp.float32)
    mixed = sum_ref[:, :width] + got_ref[:, :width].astype(jnp.float32)
    both_ref[:, :width] = (valid * (x + mixed)).astype(jnp.bfloat16)
    gh = (sum_ref[:, width:] + got_ref[:, width:].astype(jnp.float32)) * gain_ref[...]
    inv = inv_rms_of(x)
    inner = jnp.mean(gh * x, axis=-1, keepdims=True)
    gy = own_ref[:, width:].astype(jnp.float32) * valid
    both_ref[:, width:] = (gy + inv * (gh - x * inv * inv * inner)).astype(jnp.bfloat16)


def call(kernel, outs, scratch, flops, *operands, behind=()):
    size = sum(o.size * o.dtype.itemsize for o in outs + operands)
    return pl.pallas_call(
        kernel,
        out_shape=outs,
        in_specs=[
            pl.BlockSpec(memory_space=pltpu.SMEM if o.dtype == jnp.int32 else pltpu.VMEM)
            for o in operands
        ]
        + [pl.BlockSpec(memory_space=pl.ANY)] * len(behind),
        scratch_shapes=scratch,
        compiler_params=pltpu.CompilerParams(vmem_limit_bytes=VMEM_LIMIT),
        cost_estimate=pl.CostEstimate(flops=flops, bytes_accessed=size, transcendentals=0),
    )(*operands, *behind)


def halves(up, down, mid):
    def kernel(up_ref, down_ref, low_ref, high_ref):
        low_ref[...] = up_ref[...]
        high_ref[...] = down_ref[...]

    cols = up.shape[1]
    return pl.pallas_call(
        kernel,
        grid=(1,),
        out_shape=[jax.ShapeDtypeStruct((mid, cols), up.dtype)] * 2,
        in_specs=[
            pl.BlockSpec((mid, cols), lambda i: (0, 0)),
            pl.BlockSpec((mid, cols), lambda i: (1, 0)),
        ],
        out_specs=[pl.BlockSpec((mid, cols), lambda i: (0, 0))] * 2,
        cost_estimate=pl.CostEstimate(
            flops=HALVES_COST, bytes_accessed=4 * mid * cols * 2, transcendentals=0
        ),
    )(up, down)


def shift(v, axis, by):
    size = lax.axis_size(axis)
    return lax.ppermute(v, axis, [(i, (i + by) % size) for i in range(size)])


def exchange(v, axes):
    return lax.all_to_all(v, axes, split_axis=0, concat_axis=0, tiled=True)


def after(v, first):
    return lax.optimization_barrier((v, first))[0]


def per_device(frames_in, cotangent, norm_gain, w_qkv, w_out, lengths):
    bf, f32 = jnp.bfloat16, jnp.float32
    y_at, core_at, x_at = (lax.axis_index(axis) for axis in ("y", "core", "x"))
    ys, cores, zs = (lax.axis_size(axis) for axis in ("y", "core", "z"))
    tms, mics = XS * zs, ys * cores
    frame_dev, width = frames_in.shape[1:]
    frames = frame_dev // mics
    rows = mics * frames
    piece, wide = w_qkv.shape
    half, cut = wide // cores, width // cores

    mine = [lax.dynamic_slice(w_qkv, (0, j * width + core_at * cut), (piece, cut)) for j in range(3)]
    mine.append(lax.dynamic_slice(w_out, (0, core_at * cut), (piece, cut)))
    mine = jnp.concatenate(mine, axis=1)
    block = exchange(jnp.broadcast_to(mine[None], (zs, piece, half + cut)), "z")
    block = block.reshape(zs * piece, half + cut)
    up, down = shift(block, "x", 1), shift(block, "x", -1)
    mid = zs * piece // 2
    far_low, far_high = halves(up, down, mid)
    far_low, far_high = shift(far_low, "x", 1), shift(far_high, "x", -1)

    both = jnp.concatenate(
        [frames_in.reshape(mics, frames, width), cotangent.reshape(mics, frames, width)], axis=2
    )
    own = exchange(after(both, block), MIC).reshape(rows, 2 * width)
    near = shift(own, "core", 1)

    slot_len = frame_dev * tms // SESS
    start = lax.axis_index(TM) * frame_dev
    session = start // slot_len
    left = lengths[session] + session * slot_len - start - y_at * cores * frames
    scalars = [core_at, left - core_at * frames, left - (1 - core_at) * frames, x_at]
    scalars = jnp.stack(scalars).astype(jnp.int32)
    gain = norm_gain.reshape(1, width)

    def shape(dims, dtype):
        return jax.ShapeDtypeStruct(dims, dtype)

    heads = width // HD // cores
    results = (
        shape((rows, half), bf),
        shape((heads, rows, rows), f32),
        shape((rows, cut), bf),
    )
    own_qkv, own_p, own_att, w, wo, wo_give = call(
        lambda *refs: own_kernel(frames, *refs),
        results + (shape((width, half), bf), shape((cut, cut), bf), shape((cut, cut), bf)),
        (pltpu.VMEM((width, cut), bf),),
        FWD_COST,
        scalars, own, gain, block, up, down, far_low, far_high,
    )
    wo_got = shift(wo_give, "core", 1)
    near_qkv, near_p, near_att, give, gw = call(
        lambda *refs: near_kernel(frames, *refs),
        results + (shape((cut, cut), bf), shape((width, cut), bf)),
        (),
        FWD_COST,
        scalars, own, near, gain, w, own_att,
    )

    got = shift(give, "core", 1)
    term = lax.dynamic_update_slice(gw, got, ((1 - core_at) * cut, 0))

    sum_part, other_part = call(
        lambda *refs: bwd_kernel(frames, *refs),
        (shape((rows, 2 * width), f32), shape((rows, 2 * width), bf)),
        (pltpu.VMEM((2 * rows, half), bf),),
        BWD_COST,
        scalars, own, near, wo, wo_got, own_att, near_att, own_qkv, near_qkv, own_p, near_p, w,
        behind=(term,),
    )
    term = exchange(term.reshape(tms, piece, cut), TM)
    term = jnp.sum(term.astype(f32), axis=0).astype(bf)
    got_part = shift(other_part, "core", 1)
    (done,) = call(
        lambda *refs: end_kernel(frames, *refs),
        (shape((rows, 2 * width), bf),),
        (),
        END_COST,
        scalars, own, gain, sum_part, got_part,
    )

    low = piece // frames
    term = term.reshape(low, frames, cut).transpose(1, 0, 2).reshape(frames, low * cut)
    term = jnp.broadcast_to(term[None], (mics, frames, low * cut))
    sent = jnp.concatenate([done.reshape(mics, frames, 2 * width), term], axis=2)
    sent = exchange(sent, MIC)
    out = sent[:, :, :width].reshape(1, frame_dev, width)
    dx = sent[:, :, width : 2 * width].reshape(1, frame_dev, width)
    term = jnp.sum(sent[:, :, 2 * width :].astype(f32).reshape(ys, cores, frames, low, cut), axis=0)
    grad_wout = term.transpose(2, 1, 0, 3).reshape(piece, width)
    return (out, dx, grad_wout)


def solution(mesh):
    grid = Mesh(mesh.devices.reshape(-1, 2, XS, mesh.devices.shape[1] // XS), ("y", "core", "x", "z"))
    return jax.shard_map(
        per_device,
        mesh=grid,
        in_specs=(P(MIC, TM, None), P(MIC, TM, None), P(), P(TM, None), P(TM, None), P()),
        out_specs=(P(MIC, TM, None), P(MIC, TM, None), P(TM, None)),
        check_vma=False,
    )
```

```python
import jax
import jax.numpy as jnp
from jax import lax
from jax.experimental import pallas as pl
from jax.experimental.pallas import tpu as pltpu
from jax.sharding import Mesh, PartitionSpec as P

HD = 64
SESS = 2
XS = 4
MIC = ("y", "core")
TM = ("x", "z")
NEG = -1e30
VMEM_LIMIT = 56 * 1024 * 1024
OWN_COST = 8_000_000_000
NEAR_COST = 8_000_000_000
PLACE_COST = 1000
STEP_COST = 20_000_000_000
BWD_COST = 1000
END_COST = 1000


def dot_nn(a, b):
    return lax.dot_general(a, b, (((1,), (0,)), ((), ())), preferred_element_type=jnp.float32)


def dot_nt(a, b):
    return lax.dot_general(a, b, (((1,), (1,)), ((), ())), preferred_element_type=jnp.float32)


def dot_tn(a, b):
    return lax.dot_general(a, b, (((0,), (0,)), ((), ())), preferred_element_type=jnp.float32)


def low_half(rows):
    return lax.broadcasted_iota(jnp.int32, (rows, 2 * HD), 1) < HD


def same_frame(rows, frames):
    row_at = lax.broadcasted_iota(jnp.int32, (rows, rows), 0)
    col_at = lax.broadcasted_iota(jnp.int32, (rows, rows), 1)
    return lax.rem(row_at, frames) == lax.rem(col_at, frames)


def valid_rows(rows, frames, left):
    frame = lax.rem(lax.broadcasted_iota(jnp.int32, (rows, 1), 0), frames)
    return (frame < left).astype(jnp.float32)


def masked_grad(frames, scalars, own_ref, near_ref):
    rows, width = own_ref.shape[0], own_ref.shape[1] // 2
    parts = [
        (ref[:, width:].astype(jnp.float32) * valid_rows(rows, frames, scalars[1 + i])).astype(
            jnp.bfloat16
        )
        for i, ref in enumerate((own_ref, near_ref))
    ]
    return jnp.concatenate(parts)


def inv_rms_of(x):
    return lax.rsqrt(jnp.mean(x * x, axis=-1, keepdims=True) + 1e-05)


def attend(same, qkv_ref, p_ref, att_ref):
    rows, mine = att_ref.shape
    low = low_half(rows)
    for index, at in enumerate(range(0, mine, 2 * HD)):
        q = qkv_ref[:, at : at + 2 * HD]
        k = qkv_ref[:, mine + at : mine + at + 2 * HD]
        v = qkv_ref[:, 2 * mine + at : 2 * mine + at + 2 * HD]
        mixed = []
        for i in range(2):
            qi = jnp.where(low == (i == 0), q, jnp.zeros_like(q))
            s = jnp.where(same, dot_nt(qi, k) * HD ** (-0.5), NEG)
            e = jnp.exp(s - jnp.max(s, axis=-1, keepdims=True))
            p = e / jnp.sum(e, axis=-1, keepdims=True)
            p_ref[2 * index + i] = p
            mixed.append(dot_nn(p.astype(jnp.bfloat16), v))
        att_ref[:, at : at + 2 * HD] = jnp.where(low, mixed[0], mixed[1]).astype(jnp.bfloat16)


def project(rows_ref, gain_ref, w_ref, qkv_ref):
    x = rows_ref[:, : w_ref.shape[0]].astype(jnp.float32)
    normed = (x * inv_rms_of(x) * gain_ref[...]).astype(jnp.bfloat16)
    qkv_ref[...] = dot_nn(normed, w_ref[...]).astype(jnp.bfloat16)


def place(ref, at, w_ref, wo_ref):
    here = pl.ds(pl.multiple_of(at, ref.shape[0]), ref.shape[0])
    w_ref[here, :] = ref[:, : w_ref.shape[1]]
    wo_ref[here, :] = ref[:, w_ref.shape[1] :]


def near_blocks_kernel(
    scalars, low_ref, high_ref, up_low, up_high, down_low, down_high, w_ref, wo_ref
):
    x_at, deep = scalars[3], 2 * low_ref.shape[0]
    pairs = ((low_ref, high_ref, 0), (up_low, up_high, XS - 1), (down_low, down_high, 1))
    for low, high, step in pairs:
        at = lax.rem(x_at + step, XS) * deep
        place(low, at, w_ref, wo_ref)
        place(high, at + deep // 2, w_ref, wo_ref)


def own_kernel(
    frames,
    scalars,
    own_ref,
    gain_ref,
    far_low_ref,
    far_high_ref,
    some_w_ref,
    some_wo_ref,
    qkv_ref,
    p_ref,
    att_ref,
    w_ref,
    wo_ref,
    give_ref,
    all_ref,
):
    rows, mid = att_ref.shape
    core, x_at = scalars[0], scalars[3]
    deep = far_low_ref.shape[0]
    far = lax.rem(x_at + 2, XS) * (2 * deep)
    w_ref[...] = some_w_ref[...]
    all_ref[...] = some_wo_ref[...]
    place(far_low_ref, far, w_ref, all_ref)
    place(far_high_ref, far + deep, w_ref, all_ref)
    wo_ref[...] = all_ref[pl.ds(pl.multiple_of(core * mid, mid), mid), :]
    give_ref[...] = all_ref[pl.ds(pl.multiple_of((1 - core) * mid, mid), mid), :]
    project(own_ref, gain_ref, w_ref, qkv_ref)
    attend(same_frame(rows, frames), qkv_ref, p_ref, att_ref)


def near_kernel(
    frames,
    scalars,
    own_ref,
    near_ref,
    gain_ref,
    w_ref,
    own_att_ref,
    qkv_ref,
    p_ref,
    att_ref,
    give_ref,
    gw_ref,
):
    project(near_ref, gain_ref, w_ref, qkv_ref)
    attend(same_frame(att_ref.shape[0], frames), qkv_ref, p_ref, att_ref)
    core, mid = scalars[0], w_ref.shape[0] // 2
    first = core == 0
    gz = masked_grad(frames, scalars, own_ref, near_ref)
    low_cols, high_cols = gz[:, :mid], gz[:, mid:]
    att = jnp.concatenate([own_att_ref[...], att_ref[...]])
    keep = dot_tn(att, jnp.where(first, low_cols, high_cols))
    gw_ref[pl.ds(pl.multiple_of(core * mid, mid), mid), :] = keep.astype(jnp.bfloat16)
    give_ref[...] = dot_tn(att, jnp.where(first, high_cols, low_cols)).astype(jnp.bfloat16)


def bwd_kernel(
    frames,
    scalars,
    own_ref,
    near_ref,
    wo_ref,
    got_ref,
    own_att_ref,
    near_att_ref,
    own_qkv_ref,
    near_qkv_ref,
    own_p_ref,
    near_p_ref,
    w_ref,
    _,
    sum_ref,
    other_ref,
    gqkv_ref,
):
    rows, width = own_ref.shape[0], own_ref.shape[1] // 2
    mine, mid = own_att_ref.shape[1], width // 2
    first = scalars[0] == 0
    att = jnp.concatenate([own_att_ref[...], near_att_ref[...]])
    kept, got = dot_nn(att, wo_ref[...]), dot_nn(att, got_ref[...])
    for at, part in ((0, jnp.where(first, kept, got)), (mid, jnp.where(first, got, kept))):
        sum_ref[:, at : at + mid] = part[:rows]
        other_ref[:, at : at + mid] = part[rows:].astype(jnp.bfloat16)
    gz = masked_grad(frames, scalars, own_ref, near_ref)
    low_cols, high_cols = gz[:, :mid], gz[:, mid:]
    ga_all = dot_nt(jnp.where(first, low_cols, high_cols), wo_ref[...])
    ga_all += dot_nt(jnp.where(first, high_cols, low_cols), got_ref[...])
    ga_all = ga_all.astype(jnp.bfloat16)
    low = low_half(rows)
    sets = ((0, own_qkv_ref, own_p_ref), (rows, near_qkv_ref, near_p_ref))
    for start, qkv_ref, p_ref in sets:
        for index, at in enumerate(range(0, mine, 2 * HD)):
            q = qkv_ref[:, at : at + 2 * HD]
            k = qkv_ref[:, mine + at : mine + at + 2 * HD]
            v = qkv_ref[:, 2 * mine + at : 2 * mine + at + 2 * HD]
            ga = ga_all[start : start + rows, at : at + 2 * HD]
            dq, dk, dv = [], [], []
            for i in range(2):
                gi = jnp.where(low == (i == 0), ga, jnp.zeros_like(ga))
                p = p_ref[2 * index + i]
                gp = dot_nt(gi, v)
                ds = p * (gp - jnp.sum(p * gp, axis=-1, keepdims=True)) * HD ** (-0.5)
                ds = ds.astype(jnp.bfloat16)
                dq.append(dot_nn(ds, k))
                dk.append(dot_tn(ds, q))
                dv.append(dot_tn(p.astype(jnp.bfloat16), ga))
            for j, grad in enumerate((dq, dk, dv)):
                gqkv_ref[start : start + rows, j * mine + at : j * mine + at + 2 * HD] = jnp.where(
                    low, grad[0], grad[1]
                ).astype(jnp.bfloat16)
    gh = dot_nt(gqkv_ref[...], w_ref[...])
    sum_ref[:, width:] = gh[:rows]
    other_ref[:, width:] = gh[rows:].astype(jnp.bfloat16)


def end_kernel(frames, scalars, own_ref, gain_ref, sum_ref, got_ref, both_ref):
    rows, width = own_ref.shape[0], own_ref.shape[1] // 2
    valid = valid_rows(rows, frames, scalars[1])
    x = own_ref[:, :width].astype(jnp.float32)
    mixed = sum_ref[:, :width] + got_ref[:, :width].astype(jnp.float32)
    both_ref[:, :width] = (valid * (x + mixed)).astype(jnp.bfloat16)
    gh = (sum_ref[:, width:] + got_ref[:, width:].astype(jnp.float32)) * gain_ref[...]
    inv = inv_rms_of(x)
    inner = jnp.mean(gh * x, axis=-1, keepdims=True)
    gy = own_ref[:, width:].astype(jnp.float32) * valid
    both_ref[:, width:] = (gy + inv * (gh - x * inv * inv * inner)).astype(jnp.bfloat16)


def call(kernel, outs, scratch, flops, *operands, behind=()):
    size = sum(o.size * o.dtype.itemsize for o in outs + operands)
    return pl.pallas_call(
        kernel,
        out_shape=outs,
        in_specs=[
            pl.BlockSpec(memory_space=pltpu.SMEM if o.dtype == jnp.int32 else pltpu.VMEM)
            for o in operands
        ]
        + [pl.BlockSpec(memory_space=pl.ANY)] * len(behind),
        scratch_shapes=scratch,
        compiler_params=pltpu.CompilerParams(vmem_limit_bytes=VMEM_LIMIT),
        cost_estimate=pl.CostEstimate(flops=flops, bytes_accessed=size, transcendentals=0),
    )(*operands, *behind)


def as_they_are(*arrays):
    return pl.pallas_call(
        lambda *refs: None,
        out_shape=[jax.ShapeDtypeStruct(v.shape, v.dtype) for v in arrays],
        in_specs=[pl.BlockSpec(memory_space=pl.ANY)] * len(arrays),
        out_specs=[pl.BlockSpec(memory_space=pl.ANY)] * len(arrays),
        input_output_aliases={i: i for i in range(len(arrays))},
        cost_estimate=pl.CostEstimate(flops=STEP_COST, bytes_accessed=0, transcendentals=0),
    )(*arrays)


def shift(v, axis, by):
    size = lax.axis_size(axis)
    return lax.ppermute(v, axis, [(i, (i + by) % size) for i in range(size)])


def exchange(v, axes):
    return lax.all_to_all(v, axes, split_axis=0, concat_axis=0, tiled=True)


def after(v, first):
    return lax.optimization_barrier((v, first))[0]


def per_device(frames_in, cotangent, norm_gain, w_qkv, w_out, lengths):
    bf, f32 = jnp.bfloat16, jnp.float32
    y_at, core_at, x_at = (lax.axis_index(axis) for axis in ("y", "core", "x"))
    ys, cores, zs = (lax.axis_size(axis) for axis in ("y", "core", "z"))
    tms, mics = XS * zs, ys * cores
    frame_dev, width = frames_in.shape[1:]
    frames = frame_dev // mics
    rows = mics * frames
    piece, wide = w_qkv.shape
    half, cut = wide // cores, width // cores

    mine = [lax.dynamic_slice(w_qkv, (0, j * width + core_at * cut), (piece, cut)) for j in range(3)]
    mine.append(lax.dynamic_slice(w_out, (0, core_at * cut), (piece, cut)))
    mine = jnp.concatenate(mine, axis=1)
    block = exchange(jnp.broadcast_to(mine[None], (zs, piece, half + cut)), "z")
    block = block.reshape(zs * piece, half + cut)
    mid = zs * piece // 2
    low, high = block[:mid], block[mid:]
    up_low, down_high = shift(low, "x", 1), shift(high, "x", -1)
    up_high, down_low = shift(high, "x", 1), shift(low, "x", -1)
    up_low, down_high = as_they_are(up_low, down_high)
    far_low, far_high = shift(up_low, "x", 1), shift(down_high, "x", -1)

    both = jnp.concatenate(
        [frames_in.reshape(mics, frames, width), cotangent.reshape(mics, frames, width)], axis=2
    )
    own = exchange(after(both, block), MIC).reshape(rows, 2 * width)
    near = shift(own, "core", 1)

    slot_len = frame_dev * tms // SESS
    start = lax.axis_index(TM) * frame_dev
    session = start // slot_len
    left = lengths[session] + session * slot_len - start - y_at * cores * frames
    scalars = [core_at, left - core_at * frames, left - (1 - core_at) * frames, x_at]
    scalars = jnp.stack(scalars).astype(jnp.int32)
    gain = norm_gain.reshape(1, width)

    def shape(dims, dtype):
        return jax.ShapeDtypeStruct(dims, dtype)

    some_w, some_wo = call(
        near_blocks_kernel,
        (shape((width, half), bf), shape((width, cut), bf)),
        (),
        PLACE_COST,
        scalars, low, high, up_low, up_high, down_low, down_high,
    )
    heads = width // HD // cores
    results = (
        shape((rows, half), bf),
        shape((heads, rows, rows), f32),
        shape((rows, cut), bf),
    )
    own_qkv, own_p, own_att, w, wo, wo_give = call(
        lambda *refs: own_kernel(frames, *refs),
        results + (shape((width, half), bf), shape((cut, cut), bf), shape((cut, cut), bf)),
        (pltpu.VMEM((width, cut), bf),),
        OWN_COST,
        scalars, own, gain, far_low, far_high, some_w, some_wo,
    )
    wo_got = shift(wo_give, "core", 1)
    near_qkv, near_p, near_att, give, gw = call(
        lambda *refs: near_kernel(frames, *refs),
        results + (shape((cut, cut), bf), shape((width, cut), bf)),
        (),
        NEAR_COST,
        scalars, own, near, gain, w, own_att,
    )

    got = shift(give, "core", 1)
    term = lax.dynamic_update_slice(gw, got, ((1 - core_at) * cut, 0))

    sum_part, other_part = call(
        lambda *refs: bwd_kernel(frames, *refs),
        (shape((rows, 2 * width), f32), shape((rows, 2 * width), bf)),
        (pltpu.VMEM((2 * rows, half), bf),),
        BWD_COST,
        scalars, own, near, wo, wo_got, own_att, near_att, own_qkv, near_qkv, own_p, near_p, w,
        behind=(term,),
    )
    term = exchange(term.reshape(tms, piece, cut), TM)
    term = jnp.sum(term.astype(f32), axis=0).astype(bf)
    got_part = shift(other_part, "core", 1)
    (done,) = call(
        lambda *refs: end_kernel(frames, *refs),
        (shape((rows, 2 * width), bf),),
        (),
        END_COST,
        scalars, own, gain, sum_part, got_part,
    )

    low = piece // frames
    term = term.reshape(low, frames, cut).transpose(1, 0, 2).reshape(frames, low * cut)
    term = jnp.broadcast_to(term[None], (mics, frames, low * cut))
    sent = jnp.concatenate([done.reshape(mics, frames, 2 * width), term], axis=2)
    sent = exchange(sent, MIC)
    out = sent[:, :, :width].reshape(1, frame_dev, width)
    dx = sent[:, :, width : 2 * width].reshape(1, frame_dev, width)
    term = jnp.sum(sent[:, :, 2 * width :].astype(f32).reshape(ys, cores, frames, low, cut), axis=0)
    grad_wout = term.transpose(2, 1, 0, 3).reshape(piece, width)
    return (out, dx, grad_wout)


def solution(mesh):
    grid = Mesh(mesh.devices.reshape(-1, 2, XS, mesh.devices.shape[1] // XS), ("y", "core", "x", "z"))
    return jax.shard_map(
        per_device,
        mesh=grid,
        in_specs=(P(MIC, TM, None), P(MIC, TM, None), P(), P(TM, None), P(TM, None), P()),
        out_specs=(P(MIC, TM, None), P(MIC, TM, None), P(TM, None)),
        check_vma=False,
    )
```

```python
import jax
import jax.numpy as jnp
from jax import lax
from jax.experimental import pallas as pl
from jax.experimental.pallas import tpu as pltpu
from jax.sharding import Mesh, PartitionSpec as P

HD = 64
SESS = 2
XS = 4
MIC = ("y", "core")
TM = ("x", "z")
NEG = -1e30
VMEM_LIMIT = 56 * 1024 * 1024
OWN_COST = 8_000_000_000
NEAR_COST = 8_000_000_000
STEP_COST = 20_000_000_000
BWD_COST = 1000
END_COST = 1000


def dot_nn(a, b):
    return lax.dot_general(a, b, (((1,), (0,)), ((), ())), preferred_element_type=jnp.float32)


def dot_nt(a, b):
    return lax.dot_general(a, b, (((1,), (1,)), ((), ())), preferred_element_type=jnp.float32)


def dot_tn(a, b):
    return lax.dot_general(a, b, (((0,), (0,)), ((), ())), preferred_element_type=jnp.float32)


def by_head(pair):
    low = lax.broadcasted_iota(jnp.int32, pair.shape, 1) < HD
    zero = jnp.zeros_like(pair)
    return jnp.concatenate([jnp.where(low, pair, zero), jnp.where(low, zero, pair)])


def side_by_side(stacked):
    half = stacked.shape[0] // 2
    return jnp.concatenate([stacked[:half], stacked[half:]], axis=1)


def same_frame(rows, frames):
    row_at = lax.broadcasted_iota(jnp.int32, (2 * rows, rows), 0)
    col_at = lax.broadcasted_iota(jnp.int32, (2 * rows, rows), 1)
    return lax.rem(row_at, frames) == lax.rem(col_at, frames)


def valid_rows(rows, frames, left):
    frame = lax.rem(lax.broadcasted_iota(jnp.int32, (rows, 1), 0), frames)
    return (frame < left).astype(jnp.float32)


def masked_grad(frames, scalars, own_ref, near_ref):
    rows, width = own_ref.shape[0], own_ref.shape[1] // 2
    parts = [
        (ref[:, width:].astype(jnp.float32) * valid_rows(rows, frames, scalars[1 + i])).astype(
            jnp.bfloat16
        )
        for i, ref in enumerate((own_ref, near_ref))
    ]
    return jnp.concatenate(parts)


def inv_rms_of(x):
    return lax.rsqrt(jnp.mean(x * x, axis=-1, keepdims=True) + 1e-05)


def attend(same, qkv_ref, p_ref, att_ref):
    mine = att_ref.shape[1]
    for index, at in enumerate(range(0, mine, 2 * HD)):
        q = qkv_ref[:, at : at + 2 * HD]
        k = qkv_ref[:, mine + at : mine + at + 2 * HD]
        v = qkv_ref[:, 2 * mine + at : 2 * mine + at + 2 * HD]
        s = jnp.where(same, dot_nt(by_head(q), k) * HD ** (-0.5), NEG)
        e = jnp.exp(s - jnp.max(s, axis=-1, keepdims=True))
        p = e / jnp.sum(e, axis=-1, keepdims=True)
        p_ref[index] = p
        mixed = dot_nn(side_by_side(p.astype(jnp.bfloat16)), by_head(v))
        att_ref[:, at : at + 2 * HD] = mixed.astype(jnp.bfloat16)


def project(rows_ref, gain_ref, w_ref, qkv_ref):
    x = rows_ref[:, : w_ref.shape[0]].astype(jnp.float32)
    normed = (x * inv_rms_of(x) * gain_ref[...]).astype(jnp.bfloat16)
    qkv_ref[...] = dot_nn(normed, w_ref[...]).astype(jnp.bfloat16)


def own_kernel(
    frames,
    scalars,
    own_ref,
    gain_ref,
    block_ref,
    up_ref,
    down_ref,
    far_low_ref,
    far_high_ref,
    qkv_ref,
    p_ref,
    att_ref,
    w_ref,
    wo_ref,
    give_ref,
    all_ref,
):
    rows, mine = att_ref.shape
    width, deep = w_ref.shape[0], block_ref.shape[0]
    core, x_at = scalars[0], scalars[3]
    far = lax.rem(x_at + 2, XS) * deep
    places = (
        (block_ref, x_at * deep),
        (up_ref, lax.rem(x_at + XS - 1, XS) * deep),
        (down_ref, lax.rem(x_at + 1, XS) * deep),
        (far_low_ref, far),
        (far_high_ref, far + deep // 2),
    )
    for ref, at in places:
        here = pl.ds(pl.multiple_of(at, deep // 2), ref.shape[0])
        w_ref[here, :] = ref[:, : 3 * mine]
        all_ref[here, :] = ref[:, 3 * mine :]
    mid = width // 2
    wo_ref[...] = all_ref[pl.ds(pl.multiple_of(core * mid, mid), mid), :]
    give_ref[...] = all_ref[pl.ds(pl.multiple_of((1 - core) * mid, mid), mid), :]
    project(own_ref, gain_ref, w_ref, qkv_ref)
    attend(same_frame(rows, frames), qkv_ref, p_ref, att_ref)


def near_kernel(
    frames,
    scalars,
    own_ref,
    near_ref,
    gain_ref,
    w_ref,
    own_att_ref,
    wo_give_ref,
    qkv_ref,
    p_ref,
    att_ref,
    give_ref,
    gw_ref,
):
    project(near_ref, gain_ref, w_ref, qkv_ref)
    attend(same_frame(att_ref.shape[0], frames), qkv_ref, p_ref, att_ref)
    core, mid = scalars[0], w_ref.shape[0] // 2
    first = core == 0
    gz = masked_grad(frames, scalars, own_ref, near_ref)
    low_cols, high_cols = gz[:, :mid], gz[:, mid:]
    att = jnp.concatenate([own_att_ref[...], att_ref[...]])
    keep = dot_tn(att, jnp.where(first, low_cols, high_cols))
    gw_ref[pl.ds(pl.multiple_of(core * mid, mid), mid), :] = keep.astype(jnp.bfloat16)
    give_ref[:mid, :] = dot_tn(att, jnp.where(first, high_cols, low_cols)).astype(jnp.bfloat16)
    give_ref[mid:, :] = wo_give_ref[...]


def bwd_kernel(
    frames,
    scalars,
    own_ref,
    near_ref,
    wo_ref,
    got_ref,
    own_att_ref,
    near_att_ref,
    own_qkv_ref,
    near_qkv_ref,
    own_p_ref,
    near_p_ref,
    w_ref,
    _,
    sum_ref,
    other_ref,
    gqkv_ref,
):
    rows, width = own_ref.shape[0], own_ref.shape[1] // 2
    mine, mid = own_att_ref.shape[1], width // 2
    first = scalars[0] == 0
    att = jnp.concatenate([own_att_ref[...], near_att_ref[...]])
    kept, got = dot_nn(att, wo_ref[...]), dot_nn(att, got_ref[mid:, :])
    for at, part in ((0, jnp.where(first, kept, got)), (mid, jnp.where(first, got, kept))):
        sum_ref[:, at : at + mid] = part[:rows]
        other_ref[:, at : at + mid] = part[rows:].astype(jnp.bfloat16)
    gz = masked_grad(frames, scalars, own_ref, near_ref)
    low_cols, high_cols = gz[:, :mid], gz[:, mid:]
    ga_all = dot_nt(jnp.where(first, low_cols, high_cols), wo_ref[...])
    ga_all += dot_nt(jnp.where(first, high_cols, low_cols), got_ref[mid:, :])
    ga_all = ga_all.astype(jnp.bfloat16)
    sets = ((0, own_qkv_ref, own_p_ref), (rows, near_qkv_ref, near_p_ref))
    for start, qkv_ref, p_ref in sets:
        for index, at in enumerate(range(0, mine, 2 * HD)):
            q = qkv_ref[:, at : at + 2 * HD]
            k = qkv_ref[:, mine + at : mine + at + 2 * HD]
            v = qkv_ref[:, 2 * mine + at : 2 * mine + at + 2 * HD]
            ga = by_head(ga_all[start : start + rows, at : at + 2 * HD])
            p = p_ref[index]
            gp = dot_nt(ga, v)
            ds = p * (gp - jnp.sum(p * gp, axis=-1, keepdims=True)) * HD ** (-0.5)
            ds = ds.astype(jnp.bfloat16)
            dq = dot_nn(side_by_side(ds), by_head(k))
            dk = dot_tn(ds, by_head(q))
            dv = dot_tn(p.astype(jnp.bfloat16), ga)
            for j, grad in enumerate((dq, dk, dv)):
                to = j * mine + at
                gqkv_ref[start : start + rows, to : to + 2 * HD] = grad.astype(jnp.bfloat16)
    gh = dot_nt(gqkv_ref[...], w_ref[...])
    sum_ref[:, width:] = gh[:rows]
    other_ref[:, width:] = gh[rows:].astype(jnp.bfloat16)


def end_kernel(frames, scalars, own_ref, gain_ref, sum_ref, got_ref, term_ref, both_ref):
    rows, width = own_ref.shape[0], own_ref.shape[1] // 2
    valid = valid_rows(rows, frames, scalars[1])
    x = own_ref[:, :width].astype(jnp.float32)
    mixed = sum_ref[:, :width] + got_ref[:, :width].astype(jnp.float32)
    both_ref[:, :width] = (valid * (x + mixed)).astype(jnp.bfloat16)
    gh = (sum_ref[:, width:] + got_ref[:, width:].astype(jnp.float32)) * gain_ref[...]
    inv = inv_rms_of(x)
    inner = jnp.mean(gh * x, axis=-1, keepdims=True)
    gy = own_ref[:, width:].astype(jnp.float32) * valid
    dx = gy + inv * (gh - x * inv * inv * inner)
    both_ref[:, width : 2 * width] = dx.astype(jnp.bfloat16)
    term = jnp.sum(term_ref[...].astype(jnp.float32), axis=0)
    cols = term.shape[1]
    for i in range(term.shape[0] // frames):
        part = jnp.tile(term[i * frames : (i + 1) * frames], (rows // frames, 1))
        to = 2 * width + i * cols
        both_ref[:, to : to + cols] = part.astype(jnp.bfloat16)


def call(kernel, outs, scratch, flops, *operands, behind=()):
    size = sum(o.size * o.dtype.itemsize for o in outs + operands)
    return pl.pallas_call(
        kernel,
        out_shape=outs,
        in_specs=[
            pl.BlockSpec(memory_space=pltpu.SMEM if o.dtype == jnp.int32 else pltpu.VMEM)
            for o in operands
        ]
        + [pl.BlockSpec(memory_space=pl.ANY)] * len(behind),
        scratch_shapes=scratch,
        compiler_params=pltpu.CompilerParams(vmem_limit_bytes=VMEM_LIMIT),
        cost_estimate=pl.CostEstimate(flops=flops, bytes_accessed=size, transcendentals=0),
    )(*operands, *behind)


def step(arrays, *behind):
    return pl.pallas_call(
        lambda *refs: None,
        out_shape=[jax.ShapeDtypeStruct(v.shape, v.dtype) for v in arrays],
        in_specs=[pl.BlockSpec(memory_space=pl.ANY)] * (len(arrays) + len(behind)),
        out_specs=[pl.BlockSpec(memory_space=pl.ANY)] * len(arrays),
        input_output_aliases={i: i for i in range(len(arrays))},
        cost_estimate=pl.CostEstimate(flops=STEP_COST, bytes_accessed=0, transcendentals=0),
    )(*arrays, *behind)


def shift(v, axis, by):
    size = lax.axis_size(axis)
    return lax.ppermute(v, axis, [(i, (i + by) % size) for i in range(size)])


def exchange(v, axes):
    return lax.all_to_all(v, axes, split_axis=0, concat_axis=0, tiled=True)


def after(v, first):
    return lax.optimization_barrier((v, first))[0]


def per_device(frames_in, cotangent, norm_gain, w_qkv, w_out, lengths):
    bf, f32 = jnp.bfloat16, jnp.float32
    y_at, core_at, x_at = (lax.axis_index(axis) for axis in ("y", "core", "x"))
    ys, cores, zs = (lax.axis_size(axis) for axis in ("y", "core", "z"))
    tms, mics = XS * zs, ys * cores
    frame_dev, width = frames_in.shape[1:]
    frames = frame_dev // mics
    rows = mics * frames
    piece, wide = w_qkv.shape
    half, cut = wide // cores, width // cores

    slot_len = frame_dev * tms // SESS
    start = lax.axis_index(TM) * frame_dev
    session = start // slot_len
    left = lengths[session] + session * slot_len - start - y_at * cores * frames
    scalars = [core_at, left - core_at * frames, left - (1 - core_at) * frames, x_at]
    scalars = jnp.stack(scalars).astype(jnp.int32)
    gain = norm_gain.reshape(1, width)

    mine = [lax.dynamic_slice(w_qkv, (0, j * width + core_at * cut), (piece, cut)) for j in range(3)]
    mine.append(lax.dynamic_slice(w_out, (0, core_at * cut), (piece, cut)))
    mine = jnp.concatenate(mine, axis=1)
    block = exchange(jnp.broadcast_to(mine[None], (zs, piece, half + cut)), "z")
    block = block.reshape(zs * piece, half + cut)
    up, down = shift(block, "x", 1), shift(block, "x", -1)
    mid = zs * piece // 2
    up, down = step((up, down), scalars, gain)
    far_low, far_high = shift(up[:mid], "x", 1), shift(down[mid:], "x", -1)

    both = jnp.concatenate(
        [frames_in.reshape(mics, frames, width), cotangent.reshape(mics, frames, width)], axis=2
    )
    own = exchange(after(both, block), MIC).reshape(rows, 2 * width)
    near = shift(own, "core", 1)

    def shape(dims, dtype):
        return jax.ShapeDtypeStruct(dims, dtype)

    heads = width // HD // cores
    results = (
        shape((rows, half), bf),
        shape((heads // 2, 2 * rows, rows), f32),
        shape((rows, cut), bf),
    )
    own_qkv, own_p, own_att, w, wo, wo_give = call(
        lambda *refs: own_kernel(frames, *refs),
        results + (shape((width, half), bf), shape((cut, cut), bf), shape((cut, cut), bf)),
        (pltpu.VMEM((width, cut), bf),),
        OWN_COST,
        scalars, own, gain, block, up, down, far_low, far_high,
    )
    near_qkv, near_p, near_att, give, gw = call(
        lambda *refs: near_kernel(frames, *refs),
        results + (shape((width, cut), bf), shape((width, cut), bf)),
        (),
        NEAR_COST,
        scalars, own, near, gain, w, own_att, wo_give,
    )

    got = shift(give, "core", 1)
    term = lax.dynamic_update_slice(gw, got[:cut], ((1 - core_at) * cut, 0))

    sum_part, other_part = call(
        lambda *refs: bwd_kernel(frames, *refs),
        (shape((rows, 2 * width), f32), shape((rows, 2 * width), bf)),
        (pltpu.VMEM((2 * rows, half), bf),),
        BWD_COST,
        scalars, own, near, wo, got, own_att, near_att, own_qkv, near_qkv, own_p, near_p, w,
        behind=(term,),
    )
    term = exchange(term.reshape(tms, piece, cut), TM)
    got_part = shift(other_part, "core", 1)
    low = piece // frames
    (done,) = call(
        lambda *refs: end_kernel(frames, *refs),
        (shape((rows, 2 * width + low * cut), bf),),
        (),
        END_COST,
        scalars, own, gain, sum_part, got_part, term,
    )

    sent = exchange(done.reshape(mics, frames, 2 * width + low * cut), MIC)
    out = sent[:, :, :width].reshape(1, frame_dev, width)
    dx = sent[:, :, width : 2 * width].reshape(1, frame_dev, width)
    term = jnp.sum(sent[:, :, 2 * width :].astype(f32).reshape(ys, cores, frames, low, cut), axis=0)
    grad_wout = term.transpose(2, 1, 0, 3).reshape(piece, width)
    return (out, dx, grad_wout)


def solution(mesh):
    grid = Mesh(mesh.devices.reshape(-1, 2, XS, mesh.devices.shape[1] // XS), ("y", "core", "x", "z"))
    return jax.shard_map(
        per_device,
        mesh=grid,
        in_specs=(P(MIC, TM, None), P(MIC, TM, None), P(), P(TM, None), P(TM, None), P()),
        out_specs=(P(MIC, TM, None), P(MIC, TM, None), P(TM, None)),
        check_vma=False,
    )
```

```python
import jax
import jax.numpy as jnp
from jax import lax
from jax.experimental import pallas as pl
from jax.experimental.pallas import tpu as pltpu
from jax.sharding import Mesh, PartitionSpec as P

HD = 64
SESS = 2
XS = 4
MIC = ("y", "core")
TM = ("x", "z")
NEG = -1e30
VMEM_LIMIT = 56 * 1024 * 1024
OWN_COST = 8_000_000_000
NEAR_COST = 8_000_000_000
BWD_COST = 1000
END_COST = 1000


def dot_nn(a, b):
    return lax.dot_general(a, b, (((1,), (0,)), ((), ())), preferred_element_type=jnp.float32)


def dot_nt(a, b):
    return lax.dot_general(a, b, (((1,), (1,)), ((), ())), preferred_element_type=jnp.float32)


def dot_tn(a, b):
    return lax.dot_general(a, b, (((0,), (0,)), ((), ())), preferred_element_type=jnp.float32)


def by_head(pair):
    low = lax.broadcasted_iota(jnp.int32, pair.shape, 1) < HD
    zero = jnp.zeros_like(pair)
    return jnp.concatenate([jnp.where(low, pair, zero), jnp.where(low, zero, pair)])


def side_by_side(stacked):
    half = stacked.shape[0] // 2
    return jnp.concatenate([stacked[:half], stacked[half:]], axis=1)


def same_frame(rows, frames):
    row_at = lax.broadcasted_iota(jnp.int32, (2 * rows, rows), 0)
    col_at = lax.broadcasted_iota(jnp.int32, (2 * rows, rows), 1)
    return lax.rem(row_at, frames) == lax.rem(col_at, frames)


def valid_rows(rows, frames, slot_len, lengths, other):
    start = (lax.axis_index("x") * lax.axis_size("z") + lax.axis_index("z")) * lax.axis_size("y")
    core = lax.axis_index("core")
    core = 1 - core if other else core
    start = ((start + lax.axis_index("y")) * lax.axis_size("core") + core) * frames
    session = start // slot_len
    left = lengths[session] + session * slot_len - start
    frame = lax.rem(lax.broadcasted_iota(jnp.int32, (rows, 1), 0), frames)
    return (frame < left).astype(jnp.float32)


def masked_grad(frames, slot_len, lengths, own_ref, near_ref):
    rows, width = own_ref.shape[0], own_ref.shape[1] // 2
    parts = [
        ref[:, width:].astype(jnp.float32) * valid_rows(rows, frames, slot_len, lengths, other)
        for other, ref in ((False, own_ref), (True, near_ref))
    ]
    return jnp.concatenate(parts).astype(jnp.bfloat16)


def inv_rms_of(x):
    return lax.rsqrt(jnp.mean(x * x, axis=-1, keepdims=True) + 1e-05)


def attend(same, qkv_ref, p_ref, att_ref):
    mine = att_ref.shape[1]
    for index, at in enumerate(range(0, mine, 2 * HD)):
        q = qkv_ref[:, at : at + 2 * HD]
        k = qkv_ref[:, mine + at : mine + at + 2 * HD]
        v = qkv_ref[:, 2 * mine + at : 2 * mine + at + 2 * HD]
        s = jnp.where(same, dot_nt(by_head(q), k) * HD ** (-0.5), NEG)
        e = jnp.exp(s - jnp.max(s, axis=-1, keepdims=True))
        p = e / jnp.sum(e, axis=-1, keepdims=True)
        p_ref[index] = p
        mixed = dot_nn(side_by_side(p.astype(jnp.bfloat16)), by_head(v))
        att_ref[:, at : at + 2 * HD] = mixed.astype(jnp.bfloat16)


def project(rows_ref, gain_ref, w_ref, qkv_ref):
    x = rows_ref[:, : w_ref.shape[0]].astype(jnp.float32)
    normed = (x * inv_rms_of(x) * gain_ref[...].reshape(1, -1)).astype(jnp.bfloat16)
    qkv_ref[...] = dot_nn(normed, w_ref[...]).astype(jnp.bfloat16)


def own_kernel(
    frames,
    slot_len,
    lengths,
    own_ref,
    gain_ref,
    block_ref,
    up_ref,
    down_ref,
    far_low_ref,
    far_high_ref,
    qkv_ref,
    p_ref,
    att_ref,
    w_ref,
    wo_ref,
    give_ref,
    all_ref,
):
    rows, mine = att_ref.shape
    width, deep = w_ref.shape[0], block_ref.shape[0]
    core, x_at = lax.axis_index("core"), lax.axis_index("x")
    far = lax.rem(x_at + 2, XS) * deep
    places = (
        (block_ref, x_at * deep),
        (up_ref, lax.rem(x_at + XS - 1, XS) * deep),
        (down_ref, lax.rem(x_at + 1, XS) * deep),
        (far_low_ref, far),
        (far_high_ref, far + deep // 2),
    )
    for ref, at in places:
        here = pl.ds(pl.multiple_of(at, deep // 2), ref.shape[0])
        w_ref[here, :] = ref[:, : 3 * mine]
        all_ref[here, :] = ref[:, 3 * mine :]
    mid = width // 2
    wo_ref[...] = all_ref[pl.ds(pl.multiple_of(core * mid, mid), mid), :]
    give_ref[...] = all_ref[pl.ds(pl.multiple_of((1 - core) * mid, mid), mid), :]
    project(own_ref, gain_ref, w_ref, qkv_ref)
    attend(same_frame(rows, frames), qkv_ref, p_ref, att_ref)


def near_kernel(
    frames,
    slot_len,
    lengths,
    own_ref,
    near_ref,
    gain_ref,
    w_ref,
    own_att_ref,
    wo_give_ref,
    qkv_ref,
    p_ref,
    att_ref,
    give_ref,
    gw_ref,
):
    project(near_ref, gain_ref, w_ref, qkv_ref)
    attend(same_frame(att_ref.shape[0], frames), qkv_ref, p_ref, att_ref)
    core, mid = lax.axis_index("core"), w_ref.shape[0] // 2
    first = core == 0
    gz = masked_grad(frames, slot_len, lengths, own_ref, near_ref)
    low_cols, high_cols = gz[:, :mid], gz[:, mid:]
    att = jnp.concatenate([own_att_ref[...], att_ref[...]])
    keep = dot_tn(att, jnp.where(first, low_cols, high_cols))
    gw_ref[pl.ds(pl.multiple_of(core * mid, mid), mid), :] = keep.astype(jnp.bfloat16)
    give_ref[:mid, :] = dot_tn(att, jnp.where(first, high_cols, low_cols)).astype(jnp.bfloat16)
    give_ref[mid:, :] = wo_give_ref[...]


def bwd_kernel(
    frames,
    slot_len,
    lengths,
    own_ref,
    near_ref,
    wo_ref,
    got_ref,
    own_att_ref,
    near_att_ref,
    own_qkv_ref,
    near_qkv_ref,
    own_p_ref,
    near_p_ref,
    w_ref,
    _,
    sum_ref,
    other_ref,
    gqkv_ref,
):
    rows, width = own_ref.shape[0], own_ref.shape[1] // 2
    mine, mid = own_att_ref.shape[1], width // 2
    first = lax.axis_index("core") == 0
    att = jnp.concatenate([own_att_ref[...], near_att_ref[...]])
    kept, got = dot_nn(att, wo_ref[...]), dot_nn(att, got_ref[mid:, :])
    for at, part in ((0, jnp.where(first, kept, got)), (mid, jnp.where(first, got, kept))):
        sum_ref[:, at : at + mid] = part[:rows]
        other_ref[:, at : at + mid] = part[rows:].astype(jnp.bfloat16)
    gz = masked_grad(frames, slot_len, lengths, own_ref, near_ref)
    low_cols, high_cols = gz[:, :mid], gz[:, mid:]
    ga_all = dot_nt(jnp.where(first, low_cols, high_cols), wo_ref[...])
    ga_all += dot_nt(jnp.where(first, high_cols, low_cols), got_ref[mid:, :])
    ga_all = ga_all.astype(jnp.bfloat16)
    sets = ((0, own_qkv_ref, own_p_ref), (rows, near_qkv_ref, near_p_ref))
    for start, qkv_ref, p_ref in sets:
        for index, at in enumerate(range(0, mine, 2 * HD)):
            q = qkv_ref[:, at : at + 2 * HD]
            k = qkv_ref[:, mine + at : mine + at + 2 * HD]
            v = qkv_ref[:, 2 * mine + at : 2 * mine + at + 2 * HD]
            ga = by_head(ga_all[start : start + rows, at : at + 2 * HD])
            p = p_ref[index]
            gp = dot_nt(ga, v)
            ds = p * (gp - jnp.sum(p * gp, axis=-1, keepdims=True)) * HD ** (-0.5)
            ds = ds.astype(jnp.bfloat16)
            dq = dot_nn(side_by_side(ds), by_head(k))
            dk = dot_tn(ds, by_head(q))
            dv = dot_tn(p.astype(jnp.bfloat16), ga)
            for j, grad in enumerate((dq, dk, dv)):
                to = j * mine + at
                gqkv_ref[start : start + rows, to : to + 2 * HD] = grad.astype(jnp.bfloat16)
    gh = dot_nt(gqkv_ref[...], w_ref[...])
    sum_ref[:, width:] = gh[:rows]
    other_ref[:, width:] = gh[rows:].astype(jnp.bfloat16)


def end_kernel(frames, slot_len, lengths, own_ref, gain_ref, sum_ref, got_ref, both_ref):
    rows, width = own_ref.shape[0], own_ref.shape[1] // 2
    valid = valid_rows(rows, frames, slot_len, lengths, False)
    x = own_ref[:, :width].astype(jnp.float32)
    mixed = sum_ref[:, :width] + got_ref[:, :width].astype(jnp.float32)
    both_ref[:, :width] = (valid * (x + mixed)).astype(jnp.bfloat16)
    gh = (sum_ref[:, width:] + got_ref[:, width:].astype(jnp.float32)) * gain_ref[...].reshape(1, -1)
    inv = inv_rms_of(x)
    inner = jnp.mean(gh * x, axis=-1, keepdims=True)
    gy = own_ref[:, width:].astype(jnp.float32) * valid
    dx = gy + inv * (gh - x * inv * inv * inner)
    both_ref[:, width:] = dx.astype(jnp.bfloat16)


def call(kernel, outs, scratch, flops, *operands, behind=()):
    size = sum(o.size * o.dtype.itemsize for o in outs + operands)
    return pl.pallas_call(
        kernel,
        out_shape=outs,
        in_specs=[
            pl.BlockSpec(memory_space=pltpu.SMEM if o.dtype == jnp.int32 else pltpu.VMEM)
            for o in operands
        ]
        + [pl.BlockSpec(memory_space=pl.ANY)] * len(behind),
        scratch_shapes=scratch,
        compiler_params=pltpu.CompilerParams(vmem_limit_bytes=VMEM_LIMIT),
        cost_estimate=pl.CostEstimate(flops=flops, bytes_accessed=size, transcendentals=0),
    )(*operands, *behind)


def shift(v, axis, by):
    size = lax.axis_size(axis)
    return lax.ppermute(v, axis, [(i, (i + by) % size) for i in range(size)])


def exchange(v, axes):
    return lax.all_to_all(v, axes, split_axis=0, concat_axis=0, tiled=True)


def after(v, first):
    return lax.optimization_barrier((v, first))[0]


def per_device(frames_in, cotangent, norm_gain, w_qkv, w_out, lengths):
    bf, f32 = jnp.bfloat16, jnp.float32
    core_at = lax.axis_index("core")
    ys, cores, zs = (lax.axis_size(axis) for axis in ("y", "core", "z"))
    tms, mics = XS * zs, ys * cores
    frame_dev, width = frames_in.shape[1:]
    frames = frame_dev // mics
    rows = mics * frames
    piece, wide = w_qkv.shape
    half, cut = wide // cores, width // cores
    spots = (frames, frame_dev * tms // SESS)

    mine = [lax.dynamic_slice(w_qkv, (0, j * width + core_at * cut), (piece, cut)) for j in range(3)]
    mine.append(lax.dynamic_slice(w_out, (0, core_at * cut), (piece, cut)))
    mine = jnp.concatenate(mine, axis=1)
    block = exchange(jnp.broadcast_to(mine[None], (zs, piece, half + cut)), "z")
    block = block.reshape(zs * piece, half + cut)
    up, down = shift(block, "x", 1), shift(block, "x", -1)
    mid = zs * piece // 2
    far_low, far_high = shift(up[:mid], "x", 1), shift(down[mid:], "x", -1)

    both = jnp.concatenate(
        [frames_in.reshape(mics, frames, width), cotangent.reshape(mics, frames, width)], axis=2
    )
    own = exchange(after(both, block), MIC).reshape(rows, 2 * width)
    near = shift(own, "core", 1)

    def shape(dims, dtype):
        return jax.ShapeDtypeStruct(dims, dtype)

    heads = width // HD // cores
    results = (
        shape((rows, half), bf),
        shape((heads // 2, 2 * rows, rows), f32),
        shape((rows, cut), bf),
    )
    own_qkv, own_p, own_att, w, wo, wo_give = call(
        lambda *refs: own_kernel(*spots, *refs),
        results + (shape((width, half), bf), shape((cut, cut), bf), shape((cut, cut), bf)),
        (pltpu.VMEM((width, cut), bf),),
        OWN_COST,
        lengths, own, norm_gain, block, up, down, far_low, far_high,
    )
    near_qkv, near_p, near_att, give, gw = call(
        lambda *refs: near_kernel(*spots, *refs),
        results + (shape((width, cut), bf), shape((width, cut), bf)),
        (),
        NEAR_COST,
        lengths, own, near, norm_gain, w, own_att, wo_give,
    )

    got = shift(give, "core", 1)
    term = lax.dynamic_update_slice(gw, got[:cut], ((1 - core_at) * cut, 0))

    sum_part, other_part = call(
        lambda *refs: bwd_kernel(*spots, *refs),
        (shape((rows, 2 * width), f32), shape((rows, 2 * width), bf)),
        (pltpu.VMEM((2 * rows, half), bf),),
        BWD_COST,
        lengths, own, near, wo, got, own_att, near_att, own_qkv, near_qkv, own_p, near_p, w,
        behind=(term,),
    )
    term = exchange(term.reshape(tms, piece, cut), TM)
    term = jnp.sum(term.astype(f32), axis=0).astype(bf)
    got_part = shift(other_part, "core", 1)
    low = piece // frames
    (done,) = call(
        lambda *refs: end_kernel(*spots, *refs),
        (shape((rows, 2 * width), bf),),
        (),
        END_COST,
        lengths, own, norm_gain, sum_part, got_part,
    )

    term = term.reshape(low, frames, cut).transpose(1, 0, 2).reshape(frames, low * cut)
    term = jnp.broadcast_to(term[None], (mics, frames, low * cut))
    sent = jnp.concatenate([done.reshape(mics, frames, 2 * width), term], axis=2)
    sent = exchange(sent, MIC)
    out = sent[:, :, :width].reshape(1, frame_dev, width)
    dx = sent[:, :, width : 2 * width].reshape(1, frame_dev, width)
    term = jnp.sum(sent[:, :, 2 * width :].astype(f32).reshape(ys, cores, frames, low, cut), axis=0)
    grad_wout = term.transpose(2, 1, 0, 3).reshape(piece, width)
    return (out, dx, grad_wout)


def solution(mesh):
    grid = Mesh(mesh.devices.reshape(-1, 2, XS, mesh.devices.shape[1] // XS), ("y", "core", "x", "z"))
    return jax.shard_map(
        per_device,
        mesh=grid,
        in_specs=(P(MIC, TM, None), P(MIC, TM, None), P(), P(TM, None), P(TM, None), P()),
        out_specs=(P(MIC, TM, None), P(MIC, TM, None), P(TM, None)),
        check_vma=False,
    )
```

```python
import jax
import jax.numpy as jnp
from jax import lax
from jax.experimental import pallas as pl
from jax.experimental.pallas import tpu as pltpu
from jax.sharding import Mesh, PartitionSpec as P

HD = 64
SESS = 2
XS = 4
MIC = ("y", "core")
TM = ("x", "z")
NEG = -1e30
VMEM_LIMIT = 56 * 1024 * 1024
OWN_COST = 8_000_000_000
NEAR_COST = 8_000_000_000
BWD_COST = 1000
END_COST = 1000


def dot_nn(a, b):
    return lax.dot_general(a, b, (((1,), (0,)), ((), ())), preferred_element_type=jnp.float32)


def dot_nt(a, b):
    return lax.dot_general(a, b, (((1,), (1,)), ((), ())), preferred_element_type=jnp.float32)


def dot_tn(a, b):
    return lax.dot_general(a, b, (((0,), (0,)), ((), ())), preferred_element_type=jnp.float32)


def by_head(pair):
    low = lax.broadcasted_iota(jnp.int32, pair.shape, 1) < HD
    zero = jnp.zeros_like(pair)
    return jnp.concatenate([jnp.where(low, pair, zero), jnp.where(low, zero, pair)])


def side_by_side(stacked):
    half = stacked.shape[0] // 2
    return jnp.concatenate([stacked[:half], stacked[half:]], axis=1)


def same_frame(rows, frames):
    row_at = lax.broadcasted_iota(jnp.int32, (2 * rows, rows), 0)
    col_at = lax.broadcasted_iota(jnp.int32, (2 * rows, rows), 1)
    return lax.rem(row_at, frames) == lax.rem(col_at, frames)


def valid_rows(rows, frames, slot_len, lengths, other):
    start = (lax.axis_index("x") * lax.axis_size("z") + lax.axis_index("z")) * lax.axis_size("y")
    core = lax.axis_index("core")
    core = 1 - core if other else core
    start = ((start + lax.axis_index("y")) * lax.axis_size("core") + core) * frames
    session = start // slot_len
    left = lengths[session] + session * slot_len - start
    frame = lax.rem(lax.broadcasted_iota(jnp.int32, (rows, 1), 0), frames)
    return (frame < left).astype(jnp.float32)


def masked_grad(frames, slot_len, lengths, own_ref, near_ref):
    rows, width = own_ref.shape[0], own_ref.shape[1] // 2
    parts = [
        ref[:, width:].astype(jnp.float32) * valid_rows(rows, frames, slot_len, lengths, other)
        for other, ref in ((False, own_ref), (True, near_ref))
    ]
    return jnp.concatenate(parts).astype(jnp.bfloat16)


def inv_rms_of(x):
    return lax.rsqrt(jnp.mean(x * x, axis=-1, keepdims=True) + 1e-05)


def attend(same, qkv_ref, p_ref, att_ref):
    mine = att_ref.shape[1]
    for index, at in enumerate(range(0, mine, 2 * HD)):
        q = qkv_ref[:, at : at + 2 * HD]
        k = qkv_ref[:, mine + at : mine + at + 2 * HD]
        v = qkv_ref[:, 2 * mine + at : 2 * mine + at + 2 * HD]
        s = jnp.where(same, dot_nt(by_head(q), k) * HD ** (-0.5), NEG)
        e = jnp.exp(s - jnp.max(s, axis=-1, keepdims=True))
        p = e / jnp.sum(e, axis=-1, keepdims=True)
        p_ref[index] = p
        mixed = dot_nn(side_by_side(p.astype(jnp.bfloat16)), by_head(v))
        att_ref[:, at : at + 2 * HD] = mixed.astype(jnp.bfloat16)


def project(rows_ref, gain_ref, w_ref, qkv_ref):
    x = rows_ref[:, : w_ref.shape[0]].astype(jnp.float32)
    normed = (x * inv_rms_of(x) * gain_ref[...].reshape(1, -1)).astype(jnp.bfloat16)
    qkv_ref[...] = dot_nn(normed, w_ref[...]).astype(jnp.bfloat16)


def own_kernel(
    frames,
    slot_len,
    lengths,
    own_ref,
    gain_ref,
    block_ref,
    up_ref,
    down_ref,
    far_low_ref,
    far_high_ref,
    qkv_ref,
    p_ref,
    att_ref,
    w_ref,
    wo_ref,
    give_ref,
    all_ref,
):
    rows, mine = att_ref.shape
    width, deep = w_ref.shape[0], block_ref.shape[0]
    core, x_at = lax.axis_index("core"), lax.axis_index("x")
    far = lax.rem(x_at + 2, XS) * deep
    places = (
        (block_ref, x_at * deep),
        (up_ref, lax.rem(x_at + XS - 1, XS) * deep),
        (down_ref, lax.rem(x_at + 1, XS) * deep),
        (far_low_ref, far),
        (far_high_ref, far + deep // 2),
    )
    for ref, at in places:
        here = pl.ds(pl.multiple_of(at, deep // 2), ref.shape[0])
        w_ref[here, :] = ref[:, : 3 * mine]
        all_ref[here, :] = ref[:, 3 * mine :]
    mid = width // 2
    wo_ref[...] = all_ref[pl.ds(pl.multiple_of(core * mid, mid), mid), :]
    give_ref[...] = all_ref[pl.ds(pl.multiple_of((1 - core) * mid, mid), mid), :]
    project(own_ref, gain_ref, w_ref, qkv_ref)
    attend(same_frame(rows, frames), qkv_ref, p_ref, att_ref)


def near_kernel(
    frames,
    slot_len,
    lengths,
    own_ref,
    near_ref,
    gain_ref,
    w_ref,
    own_att_ref,
    wo_give_ref,
    qkv_ref,
    p_ref,
    att_ref,
    give_ref,
    gw_ref,
):
    project(near_ref, gain_ref, w_ref, qkv_ref)
    attend(same_frame(att_ref.shape[0], frames), qkv_ref, p_ref, att_ref)
    core, mid = lax.axis_index("core"), w_ref.shape[0] // 2
    first = core == 0
    gz = masked_grad(frames, slot_len, lengths, own_ref, near_ref)
    low_cols, high_cols = gz[:, :mid], gz[:, mid:]
    att = jnp.concatenate([own_att_ref[...], att_ref[...]])
    keep = dot_tn(att, jnp.where(first, low_cols, high_cols))
    gw_ref[pl.ds(pl.multiple_of(core * mid, mid), mid), :] = keep.astype(jnp.bfloat16)
    give_ref[:mid, :] = dot_tn(att, jnp.where(first, high_cols, low_cols)).astype(jnp.bfloat16)
    give_ref[mid:, :] = wo_give_ref[...]


def bwd_kernel(
    frames,
    slot_len,
    lengths,
    own_ref,
    near_ref,
    wo_ref,
    got_ref,
    own_att_ref,
    near_att_ref,
    own_qkv_ref,
    near_qkv_ref,
    own_p_ref,
    near_p_ref,
    w_ref,
    _,
    sum_ref,
    other_ref,
    gqkv_ref,
):
    rows, width = own_ref.shape[0], own_ref.shape[1] // 2
    mine, mid = own_att_ref.shape[1], width // 2
    first = lax.axis_index("core") == 0
    att = jnp.concatenate([own_att_ref[...], near_att_ref[...]])
    kept, got = dot_nn(att, wo_ref[...]), dot_nn(att, got_ref[mid:, :])
    for at, part in ((0, jnp.where(first, kept, got)), (mid, jnp.where(first, got, kept))):
        sum_ref[:, at : at + mid] = part[:rows]
        other_ref[:, at : at + mid] = part[rows:].astype(jnp.bfloat16)
    gz = masked_grad(frames, slot_len, lengths, own_ref, near_ref)
    low_cols, high_cols = gz[:, :mid], gz[:, mid:]
    ga_all = dot_nt(jnp.where(first, low_cols, high_cols), wo_ref[...])
    ga_all += dot_nt(jnp.where(first, high_cols, low_cols), got_ref[mid:, :])
    ga_all = ga_all.astype(jnp.bfloat16)
    sets = ((0, own_qkv_ref, own_p_ref), (rows, near_qkv_ref, near_p_ref))
    for start, qkv_ref, p_ref in sets:
        for index, at in enumerate(range(0, mine, 2 * HD)):
            q = qkv_ref[:, at : at + 2 * HD]
            k = qkv_ref[:, mine + at : mine + at + 2 * HD]
            v = qkv_ref[:, 2 * mine + at : 2 * mine + at + 2 * HD]
            ga = by_head(ga_all[start : start + rows, at : at + 2 * HD])
            p = p_ref[index]
            gp = dot_nt(ga, v)
            ds = p * (gp - jnp.sum(p * gp, axis=-1, keepdims=True)) * HD ** (-0.5)
            ds = ds.astype(jnp.bfloat16)
            dq = dot_nn(side_by_side(ds), by_head(k))
            dk = dot_tn(ds, by_head(q))
            dv = dot_tn(p.astype(jnp.bfloat16), ga)
            for j, grad in enumerate((dq, dk, dv)):
                to = j * mine + at
                gqkv_ref[start : start + rows, to : to + 2 * HD] = grad.astype(jnp.bfloat16)
    gh = dot_nt(gqkv_ref[...], w_ref[...])
    sum_ref[:, width:] = gh[:rows]
    other_ref[:, width:] = gh[rows:].astype(jnp.bfloat16)


def end_kernel(frames, slot_len, lengths, own_ref, gain_ref, sum_ref, got_ref, both_ref):
    rows, width = own_ref.shape[0], own_ref.shape[1] // 2
    valid = valid_rows(rows, frames, slot_len, lengths, False)
    x = own_ref[:, :width].astype(jnp.float32)
    mixed = sum_ref[:, :width] + got_ref[:, :width].astype(jnp.float32)
    both_ref[:, :width] = (valid * (x + mixed)).astype(jnp.bfloat16)
    gh = (sum_ref[:, width:] + got_ref[:, width:].astype(jnp.float32)) * gain_ref[...].reshape(1, -1)
    inv = inv_rms_of(x)
    inner = jnp.mean(gh * x, axis=-1, keepdims=True)
    gy = own_ref[:, width:].astype(jnp.float32) * valid
    dx = gy + inv * (gh - x * inv * inv * inner)
    both_ref[:, width : 2 * width] = dx.astype(jnp.bfloat16)


def call(kernel, outs, scratch, flops, *operands, behind=()):
    size = sum(o.size * o.dtype.itemsize for o in outs + operands)
    return pl.pallas_call(
        kernel,
        out_shape=outs,
        in_specs=[
            pl.BlockSpec(memory_space=pltpu.SMEM if o.dtype == jnp.int32 else pltpu.VMEM)
            for o in operands
        ]
        + [pl.BlockSpec(memory_space=pl.ANY)] * len(behind),
        scratch_shapes=scratch,
        compiler_params=pltpu.CompilerParams(vmem_limit_bytes=VMEM_LIMIT),
        cost_estimate=pl.CostEstimate(flops=flops, bytes_accessed=size, transcendentals=0),
    )(*operands, *behind)


def shift(v, axis, by):
    size = lax.axis_size(axis)
    return lax.ppermute(v, axis, [(i, (i + by) % size) for i in range(size)])


def exchange(v, axes):
    return lax.all_to_all(v, axes, split_axis=0, concat_axis=0, tiled=True)


def after(v, first):
    return lax.optimization_barrier((v, first))[0]


def per_device(frames_in, cotangent, norm_gain, w_qkv, w_out, lengths):
    bf, f32 = jnp.bfloat16, jnp.float32
    core_at = lax.axis_index("core")
    ys, cores, zs = (lax.axis_size(axis) for axis in ("y", "core", "z"))
    tms, mics = XS * zs, ys * cores
    frame_dev, width = frames_in.shape[1:]
    frames = frame_dev // mics
    rows = mics * frames
    piece, wide = w_qkv.shape
    half, cut = wide // cores, width // cores
    spots = (frames, frame_dev * tms // SESS)

    mine = [lax.dynamic_slice(w_qkv, (0, j * width + core_at * cut), (piece, cut)) for j in range(3)]
    mine.append(lax.dynamic_slice(w_out, (0, core_at * cut), (piece, cut)))
    mine = jnp.concatenate(mine, axis=1)
    block = exchange(jnp.broadcast_to(mine[None], (zs, piece, half + cut)), "z")
    block = block.reshape(zs * piece, half + cut)
    up, down = shift(block, "x", 1), shift(block, "x", -1)
    mid = zs * piece // 2
    far_low, far_high = shift(up[:mid], "x", 1), shift(down[mid:], "x", -1)

    both = jnp.concatenate(
        [frames_in.reshape(mics, frames, width), cotangent.reshape(mics, frames, width)], axis=2
    )
    own = exchange(after(both, block), MIC).reshape(rows, 2 * width)
    near = shift(own, "core", 1)

    def shape(dims, dtype):
        return jax.ShapeDtypeStruct(dims, dtype)

    heads = width // HD // cores
    results = (
        shape((rows, half), bf),
        shape((heads // 2, 2 * rows, rows), f32),
        shape((rows, cut), bf),
    )
    own_qkv, own_p, own_att, w, wo, wo_give = call(
        lambda *refs: own_kernel(*spots, *refs),
        results + (shape((width, half), bf), shape((cut, cut), bf), shape((cut, cut), bf)),
        (pltpu.VMEM((width, cut), bf),),
        OWN_COST,
        lengths, own, norm_gain, block, up, down, far_low, far_high,
    )
    near_qkv, near_p, near_att, give, gw = call(
        lambda *refs: near_kernel(*spots, *refs),
        results + (shape((width, cut), bf), shape((width, cut), bf)),
        (),
        NEAR_COST,
        lengths, own, near, norm_gain, w, own_att, wo_give,
    )

    got = shift(give, "core", 1)
    term = lax.dynamic_update_slice(gw, got[:cut], ((1 - core_at) * cut, 0))

    sum_part, other_part = call(
        lambda *refs: bwd_kernel(*spots, *refs),
        (shape((rows, 2 * width), f32), shape((rows, 2 * width), bf)),
        (pltpu.VMEM((2 * rows, half), bf),),
        BWD_COST,
        lengths, own, near, wo, got, own_att, near_att, own_qkv, near_qkv, own_p, near_p, w,
        behind=(term,),
    )
    term = exchange(term.reshape(tms, piece, cut), TM)
    term = jnp.sum(term.astype(f32), axis=0).astype(bf)
    got_part = shift(other_part, "core", 1)
    low = piece // frames
    (done,) = call(
        lambda *refs: end_kernel(*spots, *refs),
        (shape((rows, 2 * width + low * cut), bf),),
        (),
        END_COST,
        lengths, own, norm_gain, sum_part, got_part,
    )

    term = term.reshape(low, frames, cut).transpose(1, 0, 2).reshape(frames, low * cut)
    term = jnp.broadcast_to(term[None], (mics, frames, low * cut))
    sent = done.reshape(mics, frames, 2 * width + low * cut)
    sent = exchange(lax.dynamic_update_slice(sent, term, (0, 0, 2 * width)), MIC)
    out = sent[:, :, :width].reshape(1, frame_dev, width)
    dx = sent[:, :, width : 2 * width].reshape(1, frame_dev, width)
    term = jnp.sum(sent[:, :, 2 * width :].astype(f32).reshape(ys, cores, frames, low, cut), axis=0)
    grad_wout = term.transpose(2, 1, 0, 3).reshape(piece, width)
    return (out, dx, grad_wout)


def solution(mesh):
    grid = Mesh(mesh.devices.reshape(-1, 2, XS, mesh.devices.shape[1] // XS), ("y", "core", "x", "z"))
    return jax.shard_map(
        per_device,
        mesh=grid,
        in_specs=(P(MIC, TM, None), P(MIC, TM, None), P(), P(TM, None), P(TM, None), P()),
        out_specs=(P(MIC, TM, None), P(MIC, TM, None), P(TM, None)),
        check_vma=False,
    )
```

```python
import jax
import jax.numpy as jnp
from jax import lax
from jax.experimental import pallas as pl
from jax.experimental.pallas import tpu as pltpu
from jax.sharding import Mesh, PartitionSpec as P

HD = 64
SESS = 2
XS = 4
MIC = ("y", "core")
TM = ("x", "z")
NEG = -1e30
VMEM_LIMIT = 56 * 1024 * 1024
OWN_COST = 8_000_000_000
NEAR_COST = 8_000_000_000
BWD_COST = 1000
END_COST = 1000


def dot_nn(a, b):
    return lax.dot_general(a, b, (((1,), (0,)), ((), ())), preferred_element_type=jnp.float32)


def dot_nt(a, b):
    return lax.dot_general(a, b, (((1,), (1,)), ((), ())), preferred_element_type=jnp.float32)


def dot_tn(a, b):
    return lax.dot_general(a, b, (((0,), (0,)), ((), ())), preferred_element_type=jnp.float32)


def by_head(pair):
    low = lax.broadcasted_iota(jnp.int32, pair.shape, 1) < HD
    zero = jnp.zeros_like(pair)
    return jnp.concatenate([jnp.where(low, pair, zero), jnp.where(low, zero, pair)])


def side_by_side(stacked):
    half = stacked.shape[0] // 2
    return jnp.concatenate([stacked[:half], stacked[half:]], axis=1)


def same_frame(rows, frames):
    row_at = lax.broadcasted_iota(jnp.int32, (2 * rows, rows), 0)
    col_at = lax.broadcasted_iota(jnp.int32, (2 * rows, rows), 1)
    return lax.rem(row_at, frames) == lax.rem(col_at, frames)


def valid_rows(rows, frames, slot_len, lengths, other):
    start = (lax.axis_index("x") * lax.axis_size("z") + lax.axis_index("z")) * lax.axis_size("y")
    core = lax.axis_index("core")
    core = 1 - core if other else core
    start = ((start + lax.axis_index("y")) * lax.axis_size("core") + core) * frames
    session = start // slot_len
    left = lengths[session] + session * slot_len - start
    frame = lax.rem(lax.broadcasted_iota(jnp.int32, (rows, 1), 0), frames)
    return (frame < left).astype(jnp.float32)


def masked_grad(frames, slot_len, lengths, own_ref, near_ref):
    rows, width = own_ref.shape[0], own_ref.shape[1] // 2
    parts = [
        ref[:, width:].astype(jnp.float32) * valid_rows(rows, frames, slot_len, lengths, other)
        for other, ref in ((False, own_ref), (True, near_ref))
    ]
    return jnp.concatenate(parts).astype(jnp.bfloat16)


def inv_rms_of(x):
    return lax.rsqrt(jnp.mean(x * x, axis=-1, keepdims=True) + 1e-05)


def attend(same, qkv_ref, p_ref, att_ref):
    mine = att_ref.shape[1]
    for index, at in enumerate(range(0, mine, 2 * HD)):
        q = qkv_ref[:, at : at + 2 * HD]
        k = qkv_ref[:, mine + at : mine + at + 2 * HD]
        v = qkv_ref[:, 2 * mine + at : 2 * mine + at + 2 * HD]
        s = jnp.where(same, dot_nt(by_head(q), k) * HD ** (-0.5), NEG)
        e = jnp.exp(s - jnp.max(s, axis=-1, keepdims=True))
        p = e / jnp.sum(e, axis=-1, keepdims=True)
        p_ref[index] = p
        mixed = dot_nn(side_by_side(p.astype(jnp.bfloat16)), by_head(v))
        att_ref[:, at : at + 2 * HD] = mixed.astype(jnp.bfloat16)


def normalised(rows_ref, gain_ref):
    x = rows_ref[:, : rows_ref.shape[1] // 2].astype(jnp.float32)
    return (x * inv_rms_of(x) * gain_ref[...].reshape(1, -1)).astype(jnp.bfloat16)


def own_kernel(
    frames,
    slot_len,
    lengths,
    own_ref,
    gain_ref,
    block_ref,
    up_ref,
    down_ref,
    far_low_ref,
    far_high_ref,
    qkv_ref,
    p_ref,
    att_ref,
    w_ref,
    wo_ref,
    give_ref,
    all_ref,
    sems,
):
    rows, mine = att_ref.shape
    width, deep = w_ref.shape[0], block_ref.shape[0]
    core, x_at = lax.axis_index("core"), lax.axis_index("x")
    far = lax.rem(x_at + 2, XS) * deep
    places = (
        (block_ref, x_at * deep),
        (up_ref, lax.rem(x_at + XS - 1, XS) * deep),
        (down_ref, lax.rem(x_at + 1, XS) * deep),
        (far_low_ref, far),
        (far_high_ref, far + deep // 2),
    )
    copies = []
    for i, (ref, at) in enumerate(places):
        here = pl.ds(pl.multiple_of(at, deep // 2), ref.shape[0])
        for j, (cols, to) in enumerate(
            ((pl.ds(0, 3 * mine), w_ref), (pl.ds(3 * mine, mine), all_ref))
        ):
            copies.append(
                pltpu.make_async_copy(ref.at[:, cols], to.at[here, :], sems.at[2 * i + j])
            )
    for copy in copies:
        copy.start()
    mid = width // 2
    normed = normalised(own_ref, gain_ref)
    for copy in copies:
        copy.wait()
    wo_ref[...] = all_ref[pl.ds(pl.multiple_of(core * mid, mid), mid), :]
    give_ref[...] = all_ref[pl.ds(pl.multiple_of((1 - core) * mid, mid), mid), :]
    qkv_ref[...] = dot_nn(normed, w_ref[...]).astype(jnp.bfloat16)
    attend(same_frame(rows, frames), qkv_ref, p_ref, att_ref)


def near_kernel(
    frames,
    slot_len,
    lengths,
    own_ref,
    near_ref,
    gain_ref,
    own_att_ref,
    wo_give_ref,
    w_ref,
    qkv_ref,
    p_ref,
    att_ref,
    give_ref,
    gw_ref,
    held_ref,
    sem,
):
    copy = pltpu.make_async_copy(w_ref, held_ref, sem)
    copy.start()
    normed = normalised(near_ref, gain_ref)
    copy.wait()
    qkv_ref[...] = dot_nn(normed, held_ref[...]).astype(jnp.bfloat16)
    attend(same_frame(att_ref.shape[0], frames), qkv_ref, p_ref, att_ref)
    core, mid = lax.axis_index("core"), w_ref.shape[0] // 2
    first = core == 0
    gz = masked_grad(frames, slot_len, lengths, own_ref, near_ref)
    low_cols, high_cols = gz[:, :mid], gz[:, mid:]
    att = jnp.concatenate([own_att_ref[...], att_ref[...]])
    keep = dot_tn(att, jnp.where(first, low_cols, high_cols))
    gw_ref[pl.ds(pl.multiple_of(core * mid, mid), mid), :] = keep.astype(jnp.bfloat16)
    give_ref[:mid, :] = dot_tn(att, jnp.where(first, high_cols, low_cols)).astype(jnp.bfloat16)
    give_ref[mid:, :] = wo_give_ref[...]


def bwd_kernel(
    frames,
    slot_len,
    lengths,
    own_ref,
    near_ref,
    wo_ref,
    got_ref,
    own_att_ref,
    near_att_ref,
    own_qkv_ref,
    near_qkv_ref,
    own_p_ref,
    near_p_ref,
    w_ref,
    _,
    sum_ref,
    other_ref,
    gqkv_ref,
):
    rows, width = own_ref.shape[0], own_ref.shape[1] // 2
    mine, mid = own_att_ref.shape[1], width // 2
    first = lax.axis_index("core") == 0
    att = jnp.concatenate([own_att_ref[...], near_att_ref[...]])
    kept, got = dot_nn(att, wo_ref[...]), dot_nn(att, got_ref[mid:, :])
    for at, part in ((0, jnp.where(first, kept, got)), (mid, jnp.where(first, got, kept))):
        sum_ref[:, at : at + mid] = part[:rows]
        other_ref[:, at : at + mid] = part[rows:].astype(jnp.bfloat16)
    gz = masked_grad(frames, slot_len, lengths, own_ref, near_ref)
    low_cols, high_cols = gz[:, :mid], gz[:, mid:]
    ga_all = dot_nt(jnp.where(first, low_cols, high_cols), wo_ref[...])
    ga_all += dot_nt(jnp.where(first, high_cols, low_cols), got_ref[mid:, :])
    ga_all = ga_all.astype(jnp.bfloat16)
    sets = ((0, own_qkv_ref, own_p_ref), (rows, near_qkv_ref, near_p_ref))
    for start, qkv_ref, p_ref in sets:
        for index, at in enumerate(range(0, mine, 2 * HD)):
            q = qkv_ref[:, at : at + 2 * HD]
            k = qkv_ref[:, mine + at : mine + at + 2 * HD]
            v = qkv_ref[:, 2 * mine + at : 2 * mine + at + 2 * HD]
            ga = by_head(ga_all[start : start + rows, at : at + 2 * HD])
            p = p_ref[index]
            gp = dot_nt(ga, v)
            ds = p * (gp - jnp.sum(p * gp, axis=-1, keepdims=True)) * HD ** (-0.5)
            ds = ds.astype(jnp.bfloat16)
            dq = dot_nn(side_by_side(ds), by_head(k))
            dk = dot_tn(ds, by_head(q))
            dv = dot_tn(p.astype(jnp.bfloat16), ga)
            for j, grad in enumerate((dq, dk, dv)):
                to = j * mine + at
                gqkv_ref[start : start + rows, to : to + 2 * HD] = grad.astype(jnp.bfloat16)
    gh = dot_nt(gqkv_ref[...], w_ref[...])
    sum_ref[:, width:] = gh[:rows]
    other_ref[:, width:] = gh[rows:].astype(jnp.bfloat16)


def end_kernel(frames, slot_len, lengths, own_ref, gain_ref, sum_ref, got_ref, both_ref):
    rows, width = own_ref.shape[0], own_ref.shape[1] // 2
    valid = valid_rows(rows, frames, slot_len, lengths, False)
    x = own_ref[:, :width].astype(jnp.float32)
    mixed = sum_ref[:, :width] + got_ref[:, :width].astype(jnp.float32)
    both_ref[:, :width] = (valid * (x + mixed)).astype(jnp.bfloat16)
    gh = (sum_ref[:, width:] + got_ref[:, width:].astype(jnp.float32)) * gain_ref[...].reshape(1, -1)
    inv = inv_rms_of(x)
    inner = jnp.mean(gh * x, axis=-1, keepdims=True)
    gy = own_ref[:, width:].astype(jnp.float32) * valid
    dx = gy + inv * (gh - x * inv * inv * inner)
    both_ref[:, width : 2 * width] = dx.astype(jnp.bfloat16)


def call(kernel, outs, scratch, flops, *operands, behind=()):
    size = sum(o.size * o.dtype.itemsize for o in outs + operands)
    return pl.pallas_call(
        kernel,
        out_shape=outs,
        in_specs=[
            pl.BlockSpec(memory_space=pltpu.SMEM if o.dtype == jnp.int32 else pltpu.VMEM)
            for o in operands
        ]
        + [pl.BlockSpec(memory_space=pl.ANY)] * len(behind),
        scratch_shapes=scratch,
        compiler_params=pltpu.CompilerParams(vmem_limit_bytes=VMEM_LIMIT),
        cost_estimate=pl.CostEstimate(flops=flops, bytes_accessed=size, transcendentals=0),
    )(*operands, *behind)


def shift(v, axis, by):
    size = lax.axis_size(axis)
    return lax.ppermute(v, axis, [(i, (i + by) % size) for i in range(size)])


def exchange(v, axes):
    return lax.all_to_all(v, axes, split_axis=0, concat_axis=0, tiled=True)


def after(v, first):
    return lax.optimization_barrier((v, first))[0]


def per_device(frames_in, cotangent, norm_gain, w_qkv, w_out, lengths):
    bf, f32 = jnp.bfloat16, jnp.float32
    core_at = lax.axis_index("core")
    ys, cores, zs = (lax.axis_size(axis) for axis in ("y", "core", "z"))
    tms, mics = XS * zs, ys * cores
    frame_dev, width = frames_in.shape[1:]
    frames = frame_dev // mics
    rows = mics * frames
    piece, wide = w_qkv.shape
    half, cut = wide // cores, width // cores
    spots = (frames, frame_dev * tms // SESS)

    mine = [lax.dynamic_slice(w_qkv, (0, j * width + core_at * cut), (piece, cut)) for j in range(3)]
    mine.append(lax.dynamic_slice(w_out, (0, core_at * cut), (piece, cut)))
    mine = jnp.concatenate(mine, axis=1)
    block = exchange(jnp.broadcast_to(mine[None], (zs, piece, half + cut)), "z")
    block = block.reshape(zs * piece, half + cut)
    up, down = shift(block, "x", 1), shift(block, "x", -1)
    mid = zs * piece // 2
    far_low, far_high = shift(up[:mid], "x", 1), shift(down[mid:], "x", -1)

    both = jnp.concatenate(
        [frames_in.reshape(mics, frames, width), cotangent.reshape(mics, frames, width)], axis=2
    )
    own = exchange(after(both, block), MIC).reshape(rows, 2 * width)
    near = shift(own, "core", 1)

    def shape(dims, dtype):
        return jax.ShapeDtypeStruct(dims, dtype)

    heads = width // HD // cores
    results = (
        shape((rows, half), bf),
        shape((heads // 2, 2 * rows, rows), f32),
        shape((rows, cut), bf),
    )
    own_qkv, own_p, own_att, w, wo, wo_give = call(
        lambda *refs: own_kernel(*spots, *refs),
        results + (shape((width, half), bf), shape((cut, cut), bf), shape((cut, cut), bf)),
        (pltpu.VMEM((width, cut), bf), pltpu.SemaphoreType.DMA((10,))),
        OWN_COST,
        lengths, own, norm_gain, behind=(block, up, down, far_low, far_high),
    )
    near_qkv, near_p, near_att, give, gw = call(
        lambda *refs: near_kernel(*spots, *refs),
        results + (shape((width, cut), bf), shape((width, cut), bf)),
        (pltpu.VMEM((width, half), bf), pltpu.SemaphoreType.DMA),
        NEAR_COST,
        lengths, own, near, norm_gain, own_att, wo_give, behind=(w,),
    )

    got = shift(give, "core", 1)
    term = lax.dynamic_update_slice(gw, got[:cut], ((1 - core_at) * cut, 0))

    sum_part, other_part = call(
        lambda *refs: bwd_kernel(*spots, *refs),
        (shape((rows, 2 * width), f32), shape((rows, 2 * width), bf)),
        (pltpu.VMEM((2 * rows, half), bf),),
        BWD_COST,
        lengths, own, near, wo, got, own_att, near_att, own_qkv, near_qkv, own_p, near_p, w,
        behind=(term,),
    )
    term = exchange(term.reshape(tms, piece, cut), TM)
    term = jnp.sum(term.astype(f32), axis=0).astype(bf)
    got_part = shift(other_part, "core", 1)
    low = piece // frames
    (done,) = call(
        lambda *refs: end_kernel(*spots, *refs),
        (shape((rows, 2 * width + low * cut), bf),),
        (),
        END_COST,
        lengths, own, norm_gain, sum_part, got_part,
    )

    term = term.reshape(low, frames, cut).transpose(1, 0, 2).reshape(frames, low * cut)
    term = jnp.broadcast_to(term[None], (mics, frames, low * cut))
    sent = done.reshape(mics, frames, 2 * width + low * cut)
    sent = exchange(lax.dynamic_update_slice(sent, term, (0, 0, 2 * width)), MIC)
    out = sent[:, :, :width].reshape(1, frame_dev, width)
    dx = sent[:, :, width : 2 * width].reshape(1, frame_dev, width)
    term = jnp.sum(sent[:, :, 2 * width :].astype(f32).reshape(ys, cores, frames, low, cut), axis=0)
    grad_wout = term.transpose(2, 1, 0, 3).reshape(piece, width)
    return (out, dx, grad_wout)


def solution(mesh):
    grid = Mesh(mesh.devices.reshape(-1, 2, XS, mesh.devices.shape[1] // XS), ("y", "core", "x", "z"))
    return jax.shard_map(
        per_device,
        mesh=grid,
        in_specs=(P(MIC, TM, None), P(MIC, TM, None), P(), P(TM, None), P(TM, None), P()),
        out_specs=(P(MIC, TM, None), P(MIC, TM, None), P(TM, None)),
        check_vma=False,
    )
```

```python
import jax
import jax.numpy as jnp
from jax import lax
from jax.experimental import pallas as pl
from jax.experimental.pallas import tpu as pltpu
from jax.sharding import Mesh, PartitionSpec as P

HD = 64
SESS = 2
XS = 4
MIC = ("y", "core")
TM = ("x", "z")
NEG = -1e30
VMEM_LIMIT = 56 * 1024 * 1024
OWN_COST = 8_000_000_000
NEAR_COST = 8_000_000_000
BWD_COST = 1000
END_COST = 1000


def dot_nn(a, b):
    return lax.dot_general(a, b, (((1,), (0,)), ((), ())), preferred_element_type=jnp.float32)


def dot_nt(a, b):
    return lax.dot_general(a, b, (((1,), (1,)), ((), ())), preferred_element_type=jnp.float32)


def dot_tn(a, b):
    return lax.dot_general(a, b, (((0,), (0,)), ((), ())), preferred_element_type=jnp.float32)


def by_head(pair):
    low = lax.broadcasted_iota(jnp.int32, pair.shape, 1) < HD
    zero = jnp.zeros_like(pair)
    return jnp.concatenate([jnp.where(low, pair, zero), jnp.where(low, zero, pair)])


def side_by_side(stacked):
    half = stacked.shape[0] // 2
    return jnp.concatenate([stacked[:half], stacked[half:]], axis=1)


def same_frame(rows, frames):
    row_at = lax.broadcasted_iota(jnp.int32, (2 * rows, rows), 0)
    col_at = lax.broadcasted_iota(jnp.int32, (2 * rows, rows), 1)
    return lax.rem(row_at, frames) == lax.rem(col_at, frames)


def valid_rows(rows, frames, slot_len, lengths, other):
    start = (lax.axis_index("x") * lax.axis_size("z") + lax.axis_index("z")) * lax.axis_size("y")
    core = lax.axis_index("core")
    core = 1 - core if other else core
    start = ((start + lax.axis_index("y")) * lax.axis_size("core") + core) * frames
    session = start // slot_len
    left = lengths[session] + session * slot_len - start
    frame = lax.rem(lax.broadcasted_iota(jnp.int32, (rows, 1), 0), frames)
    return (frame < left).astype(jnp.float32)


def masked_grad(frames, slot_len, lengths, own_ref, near_ref):
    rows, width = own_ref.shape[0], own_ref.shape[1] // 2
    parts = [
        ref[:, width:].astype(jnp.float32) * valid_rows(rows, frames, slot_len, lengths, other)
        for other, ref in ((False, own_ref), (True, near_ref))
    ]
    return jnp.concatenate(parts).astype(jnp.bfloat16)


def inv_rms_of(x):
    return lax.rsqrt(jnp.mean(x * x, axis=-1, keepdims=True) + 1e-05)


def attend(same, qkv_ref, p_ref, att_ref):
    mine = att_ref.shape[1]
    for index, at in enumerate(range(0, mine, 2 * HD)):
        q = qkv_ref[:, at : at + 2 * HD]
        k = qkv_ref[:, mine + at : mine + at + 2 * HD]
        v = qkv_ref[:, 2 * mine + at : 2 * mine + at + 2 * HD]
        s = jnp.where(same, dot_nt(by_head(q), k) * HD ** (-0.5), NEG)
        e = jnp.exp(s - jnp.max(s, axis=-1, keepdims=True))
        p = e / jnp.sum(e, axis=-1, keepdims=True)
        p_ref[index] = p
        mixed = dot_nn(side_by_side(p.astype(jnp.bfloat16)), by_head(v))
        att_ref[:, at : at + 2 * HD] = mixed.astype(jnp.bfloat16)


def project(rows_ref, gain_ref, w_ref, qkv_ref):
    x = rows_ref[:, : w_ref.shape[0]].astype(jnp.float32)
    normed = (x * inv_rms_of(x) * gain_ref[...].reshape(1, -1)).astype(jnp.bfloat16)
    qkv_ref[...] = dot_nn(normed, w_ref[...]).astype(jnp.bfloat16)


def own_kernel(
    frames,
    slot_len,
    lengths,
    own_ref,
    gain_ref,
    block_ref,
    up_ref,
    down_ref,
    far_low_ref,
    far_high_ref,
    qkv_ref,
    p_ref,
    att_ref,
    w_ref,
    wo_ref,
    give_ref,
    all_ref,
):
    rows, mine = att_ref.shape
    width, deep = w_ref.shape[0], block_ref.shape[0]
    core, x_at = lax.axis_index("core"), lax.axis_index("x")
    far = lax.rem(x_at + 2, XS) * deep
    places = (
        (block_ref, x_at * deep),
        (up_ref, lax.rem(x_at + XS - 1, XS) * deep),
        (down_ref, lax.rem(x_at + 1, XS) * deep),
        (far_low_ref, far),
        (far_high_ref, far + deep // 2),
    )
    for ref, at in places:
        here = pl.ds(pl.multiple_of(at, deep // 2), ref.shape[0])
        w_ref[here, :] = ref[:, : 3 * mine]
        all_ref[here, :] = ref[:, 3 * mine :]
    mid = width // 2
    wo_ref[...] = all_ref[pl.ds(pl.multiple_of(core * mid, mid), mid), :]
    give_ref[...] = all_ref[pl.ds(pl.multiple_of((1 - core) * mid, mid), mid), :]
    project(own_ref, gain_ref, w_ref, qkv_ref)
    attend(same_frame(rows, frames), qkv_ref, p_ref, att_ref)


def near_kernel(
    frames,
    slot_len,
    lengths,
    own_ref,
    near_ref,
    gain_ref,
    w_ref,
    own_att_ref,
    qkv_ref,
    p_ref,
    att_ref,
    give_ref,
    gw_ref,
):
    project(near_ref, gain_ref, w_ref, qkv_ref)
    attend(same_frame(att_ref.shape[0], frames), qkv_ref, p_ref, att_ref)
    core, mid = lax.axis_index("core"), w_ref.shape[0] // 2
    first = core == 0
    gz = masked_grad(frames, slot_len, lengths, own_ref, near_ref)
    low_cols, high_cols = gz[:, :mid], gz[:, mid:]
    att = jnp.concatenate([own_att_ref[...], att_ref[...]])
    keep = dot_tn(att, jnp.where(first, low_cols, high_cols))
    gw_ref[pl.ds(pl.multiple_of(core * mid, mid), mid), :] = keep.astype(jnp.bfloat16)
    give_ref[...] = dot_tn(att, jnp.where(first, high_cols, low_cols)).astype(jnp.bfloat16)


def bwd_kernel(
    frames,
    slot_len,
    lengths,
    own_ref,
    near_ref,
    wo_ref,
    got_ref,
    own_att_ref,
    near_att_ref,
    own_qkv_ref,
    near_qkv_ref,
    own_p_ref,
    near_p_ref,
    w_ref,
    _,
    sum_ref,
    other_ref,
    gqkv_ref,
):
    rows, width = own_ref.shape[0], own_ref.shape[1] // 2
    mine, mid = own_att_ref.shape[1], width // 2
    first = lax.axis_index("core") == 0
    att = jnp.concatenate([own_att_ref[...], near_att_ref[...]])
    kept, got = dot_nn(att, wo_ref[...]), dot_nn(att, got_ref[...])
    for at, part in ((0, jnp.where(first, kept, got)), (mid, jnp.where(first, got, kept))):
        sum_ref[:, at : at + mid] = part[:rows]
        other_ref[:, at : at + mid] = part[rows:].astype(jnp.bfloat16)
    gz = masked_grad(frames, slot_len, lengths, own_ref, near_ref)
    low_cols, high_cols = gz[:, :mid], gz[:, mid:]
    ga_all = dot_nt(jnp.where(first, low_cols, high_cols), wo_ref[...])
    ga_all += dot_nt(jnp.where(first, high_cols, low_cols), got_ref[...])
    ga_all = ga_all.astype(jnp.bfloat16)
    sets = ((0, own_qkv_ref, own_p_ref), (rows, near_qkv_ref, near_p_ref))
    for start, qkv_ref, p_ref in sets:
        for index, at in enumerate(range(0, mine, 2 * HD)):
            q = qkv_ref[:, at : at + 2 * HD]
            k = qkv_ref[:, mine + at : mine + at + 2 * HD]
            v = qkv_ref[:, 2 * mine + at : 2 * mine + at + 2 * HD]
            ga = by_head(ga_all[start : start + rows, at : at + 2 * HD])
            p = p_ref[index]
            gp = dot_nt(ga, v)
            ds = p * (gp - jnp.sum(p * gp, axis=-1, keepdims=True)) * HD ** (-0.5)
            ds = ds.astype(jnp.bfloat16)
            dq = dot_nn(side_by_side(ds), by_head(k))
            dk = dot_tn(ds, by_head(q))
            dv = dot_tn(p.astype(jnp.bfloat16), ga)
            for j, grad in enumerate((dq, dk, dv)):
                to = j * mine + at
                gqkv_ref[start : start + rows, to : to + 2 * HD] = grad.astype(jnp.bfloat16)
    gh = dot_nt(gqkv_ref[...], w_ref[...])
    sum_ref[:, width:] = gh[:rows]
    other_ref[:, width:] = gh[rows:].astype(jnp.bfloat16)


def end_kernel(frames, slot_len, lengths, own_ref, gain_ref, sum_ref, got_ref, both_ref):
    rows, width = own_ref.shape[0], own_ref.shape[1] // 2
    valid = valid_rows(rows, frames, slot_len, lengths, False)
    x = own_ref[:, :width].astype(jnp.float32)
    mixed = sum_ref[:, :width] + got_ref[:, :width].astype(jnp.float32)
    both_ref[:, :width] = (valid * (x + mixed)).astype(jnp.bfloat16)
    gh = (sum_ref[:, width:] + got_ref[:, width:].astype(jnp.float32)) * gain_ref[...].reshape(1, -1)
    inv = inv_rms_of(x)
    inner = jnp.mean(gh * x, axis=-1, keepdims=True)
    gy = own_ref[:, width:].astype(jnp.float32) * valid
    dx = gy + inv * (gh - x * inv * inv * inner)
    both_ref[:, width : 2 * width] = dx.astype(jnp.bfloat16)


def call(kernel, outs, scratch, flops, *operands, behind=()):
    size = sum(o.size * o.dtype.itemsize for o in outs + operands)
    return pl.pallas_call(
        kernel,
        out_shape=outs,
        in_specs=[
            pl.BlockSpec(memory_space=pltpu.SMEM if o.dtype == jnp.int32 else pltpu.VMEM)
            for o in operands
        ]
        + [pl.BlockSpec(memory_space=pl.ANY)] * len(behind),
        scratch_shapes=scratch,
        compiler_params=pltpu.CompilerParams(vmem_limit_bytes=VMEM_LIMIT),
        cost_estimate=pl.CostEstimate(flops=flops, bytes_accessed=size, transcendentals=0),
    )(*operands, *behind)


def shift(v, axis, by):
    size = lax.axis_size(axis)
    return lax.ppermute(v, axis, [(i, (i + by) % size) for i in range(size)])


def exchange(v, axes):
    return lax.all_to_all(v, axes, split_axis=0, concat_axis=0, tiled=True)


def after(v, first):
    return lax.optimization_barrier((v, first))[0]


def per_device(frames_in, cotangent, norm_gain, w_qkv, w_out, lengths):
    bf, f32 = jnp.bfloat16, jnp.float32
    core_at = lax.axis_index("core")
    ys, cores, zs = (lax.axis_size(axis) for axis in ("y", "core", "z"))
    tms, mics = XS * zs, ys * cores
    frame_dev, width = frames_in.shape[1:]
    frames = frame_dev // mics
    rows = mics * frames
    piece, wide = w_qkv.shape
    half, cut = wide // cores, width // cores
    spots = (frames, frame_dev * tms // SESS)

    mine = [lax.dynamic_slice(w_qkv, (0, j * width + core_at * cut), (piece, cut)) for j in range(3)]
    mine.append(lax.dynamic_slice(w_out, (0, core_at * cut), (piece, cut)))
    mine = jnp.concatenate(mine, axis=1)
    block = exchange(jnp.broadcast_to(mine[None], (zs, piece, half + cut)), "z")
    block = block.reshape(zs * piece, half + cut)
    up, down = shift(block, "x", 1), shift(block, "x", -1)
    mid = zs * piece // 2
    far_low, far_high = shift(up[:mid], "x", 1), shift(down[mid:], "x", -1)

    both = jnp.concatenate(
        [frames_in.reshape(mics, frames, width), cotangent.reshape(mics, frames, width)], axis=2
    )
    own = exchange(after(both, block), MIC).reshape(rows, 2 * width)
    near = shift(own, "core", 1)

    def shape(dims, dtype):
        return jax.ShapeDtypeStruct(dims, dtype)

    heads = width // HD // cores
    results = (
        shape((rows, half), bf),
        shape((heads // 2, 2 * rows, rows), f32),
        shape((rows, cut), bf),
    )
    own_qkv, own_p, own_att, w, wo, wo_give = call(
        lambda *refs: own_kernel(*spots, *refs),
        results + (shape((width, half), bf), shape((cut, cut), bf), shape((cut, cut), bf)),
        (pltpu.VMEM((width, cut), bf),),
        OWN_COST,
        lengths, own, norm_gain, block, up, down, far_low, far_high,
    )
    near_qkv, near_p, near_att, give, gw = call(
        lambda *refs: near_kernel(*spots, *refs),
        results + (shape((cut, cut), bf), shape((width, cut), bf)),
        (),
        NEAR_COST,
        lengths, own, near, norm_gain, w, own_att,
    )

    got = shift(give, "core", 1)
    wo_got = shift(wo_give, "core", 1)
    term = lax.dynamic_update_slice(gw, got, ((1 - core_at) * cut, 0))

    sum_part, other_part = call(
        lambda *refs: bwd_kernel(*spots, *refs),
        (shape((rows, 2 * width), f32), shape((rows, 2 * width), bf)),
        (pltpu.VMEM((2 * rows, half), bf),),
        BWD_COST,
        lengths, own, near, wo, wo_got, own_att, near_att, own_qkv, near_qkv, own_p, near_p, w,
        behind=(term,),
    )
    term = exchange(term.reshape(tms, piece, cut), TM)
    term = jnp.sum(term.astype(f32), axis=0).astype(bf)
    got_part = shift(other_part, "core", 1)
    low = piece // frames
    (done,) = call(
        lambda *refs: end_kernel(*spots, *refs),
        (shape((rows, 2 * width + low * cut), bf),),
        (),
        END_COST,
        lengths, own, norm_gain, sum_part, got_part,
    )

    term = term.reshape(low, frames, cut).transpose(1, 0, 2).reshape(frames, low * cut)
    term = jnp.broadcast_to(term[None], (mics, frames, low * cut))
    sent = done.reshape(mics, frames, 2 * width + low * cut)
    sent = exchange(lax.dynamic_update_slice(sent, term, (0, 0, 2 * width)), MIC)
    out = sent[:, :, :width].reshape(1, frame_dev, width)
    dx = sent[:, :, width : 2 * width].reshape(1, frame_dev, width)
    term = jnp.sum(sent[:, :, 2 * width :].astype(f32).reshape(ys, cores, frames, low, cut), axis=0)
    grad_wout = term.transpose(2, 1, 0, 3).reshape(piece, width)
    return (out, dx, grad_wout)


def solution(mesh):
    grid = Mesh(mesh.devices.reshape(-1, 2, XS, mesh.devices.shape[1] // XS), ("y", "core", "x", "z"))
    return jax.shard_map(
        per_device,
        mesh=grid,
        in_specs=(P(MIC, TM, None), P(MIC, TM, None), P(), P(TM, None), P(TM, None), P()),
        out_specs=(P(MIC, TM, None), P(MIC, TM, None), P(TM, None)),
        check_vma=False,
    )
```

```python
import jax
import jax.numpy as jnp
from jax import lax
from jax.experimental import pallas as pl
from jax.experimental.pallas import tpu as pltpu
from jax.sharding import Mesh, PartitionSpec as P

HD = 64
SESS = 2
XS = 4
MIC = ("y", "core")
TM = ("x", "z")
NEG = -1e30
VMEM_LIMIT = 56 * 1024 * 1024
OWN_COST = 8_000_000_000
NEAR_COST = 8_000_000_000
BWD_COST = 8_000_000_000
END_COST = 1000


def dot_nn(a, b):
    return lax.dot_general(a, b, (((1,), (0,)), ((), ())), preferred_element_type=jnp.float32)


def dot_nt(a, b):
    return lax.dot_general(a, b, (((1,), (1,)), ((), ())), preferred_element_type=jnp.float32)


def dot_tn(a, b):
    return lax.dot_general(a, b, (((0,), (0,)), ((), ())), preferred_element_type=jnp.float32)


def by_head(pair):
    low = lax.broadcasted_iota(jnp.int32, pair.shape, 1) < HD
    zero = jnp.zeros_like(pair)
    return jnp.concatenate([jnp.where(low, pair, zero), jnp.where(low, zero, pair)])


def side_by_side(stacked):
    half = stacked.shape[0] // 2
    return jnp.concatenate([stacked[:half], stacked[half:]], axis=1)


def same_frame(rows, frames):
    row_at = lax.broadcasted_iota(jnp.int32, (2 * rows, rows), 0)
    col_at = lax.broadcasted_iota(jnp.int32, (2 * rows, rows), 1)
    return lax.rem(row_at, frames) == lax.rem(col_at, frames)


def valid_rows(rows, frames, slot_len, lengths, other):
    start = (lax.axis_index("x") * lax.axis_size("z") + lax.axis_index("z")) * lax.axis_size("y")
    core = lax.axis_index("core")
    core = 1 - core if other else core
    start = ((start + lax.axis_index("y")) * lax.axis_size("core") + core) * frames
    session = start // slot_len
    left = lengths[session] + session * slot_len - start
    frame = lax.rem(lax.broadcasted_iota(jnp.int32, (rows, 1), 0), frames)
    return (frame < left).astype(jnp.float32)


def masked_grad(frames, slot_len, lengths, own_ref, near_ref):
    rows, width = own_ref.shape[0], own_ref.shape[1] // 2
    parts = [
        ref[:, width:].astype(jnp.float32) * valid_rows(rows, frames, slot_len, lengths, other)
        for other, ref in ((False, own_ref), (True, near_ref))
    ]
    return jnp.concatenate(parts).astype(jnp.bfloat16)


def inv_rms_of(x):
    return lax.rsqrt(jnp.mean(x * x, axis=-1, keepdims=True) + 1e-05)


def attend(same, qkv_ref, p_ref, att_ref):
    mine = att_ref.shape[1]
    for index, at in enumerate(range(0, mine, 2 * HD)):
        q = qkv_ref[:, at : at + 2 * HD]
        k = qkv_ref[:, mine + at : mine + at + 2 * HD]
        v = qkv_ref[:, 2 * mine + at : 2 * mine + at + 2 * HD]
        s = jnp.where(same, dot_nt(by_head(q), k) * HD ** (-0.5), NEG)
        e = jnp.exp(s - jnp.max(s, axis=-1, keepdims=True))
        p = e / jnp.sum(e, axis=-1, keepdims=True)
        p_ref[index] = p
        mixed = dot_nn(side_by_side(p.astype(jnp.bfloat16)), by_head(v))
        att_ref[:, at : at + 2 * HD] = mixed.astype(jnp.bfloat16)


def project(rows_ref, gain_ref, w_ref, qkv_ref):
    x = rows_ref[:, : w_ref.shape[0]].astype(jnp.float32)
    normed = (x * inv_rms_of(x) * gain_ref[...].reshape(1, -1)).astype(jnp.bfloat16)
    qkv_ref[...] = dot_nn(normed, w_ref[...]).astype(jnp.bfloat16)


def own_kernel(
    frames,
    slot_len,
    lengths,
    own_ref,
    gain_ref,
    block_ref,
    up_ref,
    down_ref,
    far_low_ref,
    far_high_ref,
    qkv_ref,
    p_ref,
    att_ref,
    w_ref,
    wo_ref,
    give_ref,
    all_ref,
):
    rows, mine = att_ref.shape
    width, deep = w_ref.shape[0], block_ref.shape[0]
    core, x_at = lax.axis_index("core"), lax.axis_index("x")
    far = lax.rem(x_at + 2, XS) * deep
    places = (
        (block_ref, x_at * deep),
        (up_ref, lax.rem(x_at + XS - 1, XS) * deep),
        (down_ref, lax.rem(x_at + 1, XS) * deep),
        (far_low_ref, far),
        (far_high_ref, far + deep // 2),
    )
    for ref, at in places:
        here = pl.ds(pl.multiple_of(at, deep // 2), ref.shape[0])
        w_ref[here, :] = ref[:, : 3 * mine]
        all_ref[here, :] = ref[:, 3 * mine :]
    mid = width // 2
    wo_ref[...] = all_ref[pl.ds(pl.multiple_of(core * mid, mid), mid), :]
    give_ref[...] = all_ref[pl.ds(pl.multiple_of((1 - core) * mid, mid), mid), :]
    project(own_ref, gain_ref, w_ref, qkv_ref)
    attend(same_frame(rows, frames), qkv_ref, p_ref, att_ref)


def near_kernel(
    frames,
    slot_len,
    lengths,
    own_ref,
    near_ref,
    gain_ref,
    w_ref,
    own_att_ref,
    qkv_ref,
    p_ref,
    att_ref,
    give_ref,
    gw_ref,
):
    project(near_ref, gain_ref, w_ref, qkv_ref)
    attend(same_frame(att_ref.shape[0], frames), qkv_ref, p_ref, att_ref)
    core, mid = lax.axis_index("core"), w_ref.shape[0] // 2
    first = core == 0
    gz = masked_grad(frames, slot_len, lengths, own_ref, near_ref)
    low_cols, high_cols = gz[:, :mid], gz[:, mid:]
    att = jnp.concatenate([own_att_ref[...], att_ref[...]])
    keep = dot_tn(att, jnp.where(first, low_cols, high_cols))
    gw_ref[pl.ds(pl.multiple_of(core * mid, mid), mid), :] = keep.astype(jnp.bfloat16)
    give_ref[...] = dot_tn(att, jnp.where(first, high_cols, low_cols)).astype(jnp.bfloat16)


def bwd_kernel(
    frames,
    slot_len,
    lengths,
    own_ref,
    near_ref,
    wo_ref,
    got_ref,
    own_att_ref,
    near_att_ref,
    own_qkv_ref,
    near_qkv_ref,
    own_p_ref,
    near_p_ref,
    w_ref,
    _,
    sum_ref,
    other_ref,
    gqkv_ref,
):
    rows, width = own_ref.shape[0], own_ref.shape[1] // 2
    mine, mid = own_att_ref.shape[1], width // 2
    first = lax.axis_index("core") == 0
    att = jnp.concatenate([own_att_ref[...], near_att_ref[...]])
    kept, got = dot_nn(att, wo_ref[...]), dot_nn(att, got_ref[...])
    for at, part in ((0, jnp.where(first, kept, got)), (mid, jnp.where(first, got, kept))):
        sum_ref[:, at : at + mid] = part[:rows]
        other_ref[:, at : at + mid] = part[rows:].astype(jnp.bfloat16)
    gz = masked_grad(frames, slot_len, lengths, own_ref, near_ref)
    low_cols, high_cols = gz[:, :mid], gz[:, mid:]
    ga_all = dot_nt(jnp.where(first, low_cols, high_cols), wo_ref[...])
    ga_all += dot_nt(jnp.where(first, high_cols, low_cols), got_ref[...])
    ga_all = ga_all.astype(jnp.bfloat16)
    sets = ((0, own_qkv_ref, own_p_ref), (rows, near_qkv_ref, near_p_ref))
    for start, qkv_ref, p_ref in sets:
        for index, at in enumerate(range(0, mine, 2 * HD)):
            q = qkv_ref[:, at : at + 2 * HD]
            k = qkv_ref[:, mine + at : mine + at + 2 * HD]
            v = qkv_ref[:, 2 * mine + at : 2 * mine + at + 2 * HD]
            ga = by_head(ga_all[start : start + rows, at : at + 2 * HD])
            p = p_ref[index]
            gp = dot_nt(ga, v)
            ds = p * (gp - jnp.sum(p * gp, axis=-1, keepdims=True)) * HD ** (-0.5)
            ds = ds.astype(jnp.bfloat16)
            dq = dot_nn(side_by_side(ds), by_head(k))
            dk = dot_tn(ds, by_head(q))
            dv = dot_tn(p.astype(jnp.bfloat16), ga)
            for j, grad in enumerate((dq, dk, dv)):
                to = j * mine + at
                gqkv_ref[start : start + rows, to : to + 2 * HD] = grad.astype(jnp.bfloat16)
    gh = dot_nt(gqkv_ref[...], w_ref[...])
    sum_ref[:, width:] = gh[:rows]
    other_ref[:, width:] = gh[rows:].astype(jnp.bfloat16)


def end_kernel(frames, slot_len, lengths, own_ref, gain_ref, sum_ref, got_ref, both_ref):
    rows, width = own_ref.shape[0], own_ref.shape[1] // 2
    valid = valid_rows(rows, frames, slot_len, lengths, False)
    x = own_ref[:, :width].astype(jnp.float32)
    mixed = sum_ref[:, :width] + got_ref[:, :width].astype(jnp.float32)
    both_ref[:, :width] = (valid * (x + mixed)).astype(jnp.bfloat16)
    gh = (sum_ref[:, width:] + got_ref[:, width:].astype(jnp.float32)) * gain_ref[...].reshape(1, -1)
    inv = inv_rms_of(x)
    inner = jnp.mean(gh * x, axis=-1, keepdims=True)
    gy = own_ref[:, width:].astype(jnp.float32) * valid
    dx = gy + inv * (gh - x * inv * inv * inner)
    both_ref[:, width : 2 * width] = dx.astype(jnp.bfloat16)


def call(kernel, outs, scratch, flops, *operands, behind=()):
    size = sum(o.size * o.dtype.itemsize for o in outs + operands)
    return pl.pallas_call(
        kernel,
        out_shape=outs,
        in_specs=[
            pl.BlockSpec(memory_space=pltpu.SMEM if o.dtype == jnp.int32 else pltpu.VMEM)
            for o in operands
        ]
        + [pl.BlockSpec(memory_space=pl.ANY)] * len(behind),
        scratch_shapes=scratch,
        compiler_params=pltpu.CompilerParams(vmem_limit_bytes=VMEM_LIMIT),
        cost_estimate=pl.CostEstimate(flops=flops, bytes_accessed=size, transcendentals=0),
    )(*operands, *behind)


def shift(v, axis, by):
    size = lax.axis_size(axis)
    return lax.ppermute(v, axis, [(i, (i + by) % size) for i in range(size)])


def exchange(v, axes):
    return lax.all_to_all(v, axes, split_axis=0, concat_axis=0, tiled=True)


def after(v, first):
    return lax.optimization_barrier((v, first))[0]


def per_device(frames_in, cotangent, norm_gain, w_qkv, w_out, lengths):
    bf, f32 = jnp.bfloat16, jnp.float32
    core_at = lax.axis_index("core")
    ys, cores, zs = (lax.axis_size(axis) for axis in ("y", "core", "z"))
    tms, mics = XS * zs, ys * cores
    frame_dev, width = frames_in.shape[1:]
    frames = frame_dev // mics
    rows = mics * frames
    piece, wide = w_qkv.shape
    half, cut = wide // cores, width // cores
    spots = (frames, frame_dev * tms // SESS)

    mine = [lax.dynamic_slice(w_qkv, (0, j * width + core_at * cut), (piece, cut)) for j in range(3)]
    mine.append(lax.dynamic_slice(w_out, (0, core_at * cut), (piece, cut)))
    mine = jnp.concatenate(mine, axis=1)
    block = exchange(jnp.broadcast_to(mine[None], (zs, piece, half + cut)), "z")
    block = block.reshape(zs * piece, half + cut)
    up, down = shift(block, "x", 1), shift(block, "x", -1)
    mid = zs * piece // 2
    far_low, far_high = shift(up[:mid], "x", 1), shift(down[mid:], "x", -1)

    both = jnp.concatenate(
        [frames_in.reshape(mics, frames, width), cotangent.reshape(mics, frames, width)], axis=2
    )
    own = exchange(after(both, block), MIC).reshape(rows, 2 * width)
    near = shift(own, "core", 1)

    def shape(dims, dtype):
        return jax.ShapeDtypeStruct(dims, dtype)

    heads = width // HD // cores
    results = (
        shape((rows, half), bf),
        shape((heads // 2, 2 * rows, rows), f32),
        shape((rows, cut), bf),
    )
    own_qkv, own_p, own_att, w, wo, wo_give = call(
        lambda *refs: own_kernel(*spots, *refs),
        results + (shape((width, half), bf), shape((cut, cut), bf), shape((cut, cut), bf)),
        (pltpu.VMEM((width, cut), bf),),
        OWN_COST,
        lengths, own, norm_gain, block, up, down, far_low, far_high,
    )
    near_qkv, near_p, near_att, give, gw = call(
        lambda *refs: near_kernel(*spots, *refs),
        results + (shape((cut, cut), bf), shape((width, cut), bf)),
        (),
        NEAR_COST,
        lengths, own, near, norm_gain, w, own_att,
    )

    got = shift(give, "core", 1)
    wo_got = shift(wo_give, "core", 1)
    term = lax.dynamic_update_slice(gw, got, ((1 - core_at) * cut, 0))

    sum_part, other_part = call(
        lambda *refs: bwd_kernel(*spots, *refs),
        (shape((rows, 2 * width), f32), shape((rows, 2 * width), bf)),
        (pltpu.VMEM((2 * rows, half), bf),),
        BWD_COST,
        lengths, own, near, wo, wo_got, own_att, near_att, own_qkv, near_qkv, own_p, near_p, w,
        behind=(term,),
    )
    term = exchange(term.reshape(tms, piece, cut), TM)
    term = jnp.sum(term.astype(f32), axis=0).astype(bf)
    got_part = shift(other_part, "core", 1)
    low = piece // frames
    (done,) = call(
        lambda *refs: end_kernel(*spots, *refs),
        (shape((rows, 2 * width + low * cut), bf),),
        (),
        END_COST,
        lengths, own, norm_gain, sum_part, got_part,
    )

    term = term.reshape(low, frames, cut).transpose(1, 0, 2).reshape(frames, low * cut)
    term = jnp.broadcast_to(term[None], (mics, frames, low * cut))
    sent = done.reshape(mics, frames, 2 * width + low * cut)
    sent = exchange(lax.dynamic_update_slice(sent, term, (0, 0, 2 * width)), MIC)
    out = sent[:, :, :width].reshape(1, frame_dev, width)
    dx = sent[:, :, width : 2 * width].reshape(1, frame_dev, width)
    term = jnp.sum(sent[:, :, 2 * width :].astype(f32).reshape(ys, cores, frames, low, cut), axis=0)
    grad_wout = term.transpose(2, 1, 0, 3).reshape(piece, width)
    return (out, dx, grad_wout)


def solution(mesh):
    grid = Mesh(mesh.devices.reshape(-1, 2, XS, mesh.devices.shape[1] // XS), ("y", "core", "x", "z"))
    return jax.shard_map(
        per_device,
        mesh=grid,
        in_specs=(P(MIC, TM, None), P(MIC, TM, None), P(), P(TM, None), P(TM, None), P()),
        out_specs=(P(MIC, TM, None), P(MIC, TM, None), P(TM, None)),
        check_vma=False,
    )
```

```python
import jax
import jax.numpy as jnp
from jax import lax
from jax.experimental import pallas as pl
from jax.experimental.pallas import tpu as pltpu
from jax.sharding import Mesh, PartitionSpec as P

HD = 64
SESS = 2
XS = 4
MIC = ("y", "core")
TM = ("x", "z")
NEG = -1e30
VMEM_LIMIT = 56 * 1024 * 1024
OWN_COST = 8_000_000_000
NEAR_COST = 8_000_000_000
BWD_COST = 1000
END_COST = 1000


def dot_nn(a, b):
    return lax.dot_general(a, b, (((1,), (0,)), ((), ())), preferred_element_type=jnp.float32)


def dot_nt(a, b):
    return lax.dot_general(a, b, (((1,), (1,)), ((), ())), preferred_element_type=jnp.float32)


def dot_tn(a, b):
    return lax.dot_general(a, b, (((0,), (0,)), ((), ())), preferred_element_type=jnp.float32)


def by_head(pair):
    low = lax.broadcasted_iota(jnp.int32, pair.shape, 1) < HD
    zero = jnp.zeros_like(pair)
    return jnp.concatenate([jnp.where(low, pair, zero), jnp.where(low, zero, pair)])


def side_by_side(stacked):
    half = stacked.shape[0] // 2
    return jnp.concatenate([stacked[:half], stacked[half:]], axis=1)


def same_frame(rows, frames):
    row_at = lax.broadcasted_iota(jnp.int32, (2 * rows, rows), 0)
    col_at = lax.broadcasted_iota(jnp.int32, (2 * rows, rows), 1)
    return lax.rem(row_at, frames) == lax.rem(col_at, frames)


def valid_rows(rows, frames, slot_len, lengths, other):
    start = (lax.axis_index("x") * lax.axis_size("z") + lax.axis_index("z")) * lax.axis_size("y")
    core = lax.axis_index("core")
    core = 1 - core if other else core
    start = ((start + lax.axis_index("y")) * lax.axis_size("core") + core) * frames
    session = start // slot_len
    left = lengths[session] + session * slot_len - start
    frame = lax.rem(lax.broadcasted_iota(jnp.int32, (rows, 1), 0), frames)
    return (frame < left).astype(jnp.float32)


def masked_grad(frames, slot_len, lengths, own_ref, near_ref):
    rows, width = own_ref.shape[0], own_ref.shape[1] // 2
    parts = [
        ref[:, width:].astype(jnp.float32) * valid_rows(rows, frames, slot_len, lengths, other)
        for other, ref in ((False, own_ref), (True, near_ref))
    ]
    return jnp.concatenate(parts).astype(jnp.bfloat16)


def inv_rms_of(x):
    return lax.rsqrt(jnp.mean(x * x, axis=-1, keepdims=True) + 1e-05)


def attend(same, qkv_ref, p_ref, att_ref):
    mine = att_ref.shape[1]
    for index, at in enumerate(range(0, mine, 2 * HD)):
        q = qkv_ref[:, at : at + 2 * HD]
        k = qkv_ref[:, mine + at : mine + at + 2 * HD]
        v = qkv_ref[:, 2 * mine + at : 2 * mine + at + 2 * HD]
        s = jnp.where(same, dot_nt(by_head(q), k) * HD ** (-0.5), NEG)
        e = jnp.exp(s - jnp.max(s, axis=-1, keepdims=True))
        p = e / jnp.sum(e, axis=-1, keepdims=True)
        p_low = p.astype(jnp.bfloat16)
        p_ref[index] = p_low
        mixed = dot_nn(side_by_side(p_low), by_head(v))
        att_ref[:, at : at + 2 * HD] = mixed.astype(jnp.bfloat16)


def project(rows_ref, gain_ref, w_ref, qkv_ref):
    x = rows_ref[:, : w_ref.shape[0]].astype(jnp.float32)
    normed = (x * inv_rms_of(x) * gain_ref[...].reshape(1, -1)).astype(jnp.bfloat16)
    qkv_ref[...] = dot_nn(normed, w_ref[...]).astype(jnp.bfloat16)


def own_kernel(
    frames,
    slot_len,
    lengths,
    own_ref,
    gain_ref,
    block_ref,
    up_ref,
    down_ref,
    far_low_ref,
    far_high_ref,
    qkv_ref,
    p_ref,
    att_ref,
    w_ref,
    wo_ref,
    give_ref,
    all_ref,
):
    rows, mine = att_ref.shape
    width, deep = w_ref.shape[0], block_ref.shape[0]
    core, x_at = lax.axis_index("core"), lax.axis_index("x")
    far = lax.rem(x_at + 2, XS) * deep
    places = (
        (block_ref, x_at * deep),
        (up_ref, lax.rem(x_at + XS - 1, XS) * deep),
        (down_ref, lax.rem(x_at + 1, XS) * deep),
        (far_low_ref, far),
        (far_high_ref, far + deep // 2),
    )
    for ref, at in places:
        here = pl.ds(pl.multiple_of(at, deep // 2), ref.shape[0])
        w_ref[here, :] = ref[:, : 3 * mine]
        all_ref[here, :] = ref[:, 3 * mine :]
    mid = width // 2
    wo_ref[...] = all_ref[pl.ds(pl.multiple_of(core * mid, mid), mid), :]
    give_ref[...] = all_ref[pl.ds(pl.multiple_of((1 - core) * mid, mid), mid), :]
    project(own_ref, gain_ref, w_ref, qkv_ref)
    attend(same_frame(rows, frames), qkv_ref, p_ref, att_ref)


def near_kernel(
    frames,
    slot_len,
    lengths,
    own_ref,
    near_ref,
    gain_ref,
    w_ref,
    own_att_ref,
    qkv_ref,
    p_ref,
    att_ref,
    give_ref,
    gw_ref,
):
    project(near_ref, gain_ref, w_ref, qkv_ref)
    attend(same_frame(att_ref.shape[0], frames), qkv_ref, p_ref, att_ref)
    core, mid = lax.axis_index("core"), w_ref.shape[0] // 2
    first = core == 0
    gz = masked_grad(frames, slot_len, lengths, own_ref, near_ref)
    low_cols, high_cols = gz[:, :mid], gz[:, mid:]
    att = jnp.concatenate([own_att_ref[...], att_ref[...]])
    keep = dot_tn(att, jnp.where(first, low_cols, high_cols))
    gw_ref[pl.ds(pl.multiple_of(core * mid, mid), mid), :] = keep.astype(jnp.bfloat16)
    give_ref[...] = dot_tn(att, jnp.where(first, high_cols, low_cols)).astype(jnp.bfloat16)


def bwd_kernel(
    frames,
    slot_len,
    lengths,
    own_ref,
    near_ref,
    wo_ref,
    got_ref,
    own_att_ref,
    near_att_ref,
    own_qkv_ref,
    near_qkv_ref,
    own_p_ref,
    near_p_ref,
    w_ref,
    _,
    sum_ref,
    other_ref,
    gqkv_ref,
):
    rows, width = own_ref.shape[0], own_ref.shape[1] // 2
    mine, mid = own_att_ref.shape[1], width // 2
    first = lax.axis_index("core") == 0
    att = jnp.concatenate([own_att_ref[...], near_att_ref[...]])
    kept, got = dot_nn(att, wo_ref[...]), dot_nn(att, got_ref[...])
    for at, part in ((0, jnp.where(first, kept, got)), (mid, jnp.where(first, got, kept))):
        sum_ref[:, at : at + mid] = part[:rows]
        other_ref[:, at : at + mid] = part[rows:].astype(jnp.bfloat16)
    gz = masked_grad(frames, slot_len, lengths, own_ref, near_ref)
    low_cols, high_cols = gz[:, :mid], gz[:, mid:]
    ga_all = dot_nt(jnp.where(first, low_cols, high_cols), wo_ref[...])
    ga_all += dot_nt(jnp.where(first, high_cols, low_cols), got_ref[...])
    ga_all = ga_all.astype(jnp.bfloat16)
    sets = ((0, own_qkv_ref, own_p_ref), (rows, near_qkv_ref, near_p_ref))
    for start, qkv_ref, p_ref in sets:
        for index, at in enumerate(range(0, mine, 2 * HD)):
            q = qkv_ref[:, at : at + 2 * HD]
            k = qkv_ref[:, mine + at : mine + at + 2 * HD]
            v = qkv_ref[:, 2 * mine + at : 2 * mine + at + 2 * HD]
            ga = by_head(ga_all[start : start + rows, at : at + 2 * HD])
            p_low = p_ref[index]
            p = p_low.astype(jnp.float32)
            gp = dot_nt(ga, v)
            ds = p * (gp - jnp.sum(p * gp, axis=-1, keepdims=True)) * HD ** (-0.5)
            ds = ds.astype(jnp.bfloat16)
            dq = dot_nn(side_by_side(ds), by_head(k))
            dk = dot_tn(ds, by_head(q))
            dv = dot_tn(p_low, ga)
            for j, grad in enumerate((dq, dk, dv)):
                to = j * mine + at
                gqkv_ref[start : start + rows, to : to + 2 * HD] = grad.astype(jnp.bfloat16)
    gh = dot_nt(gqkv_ref[...], w_ref[...])
    sum_ref[:, width:] = gh[:rows]
    other_ref[:, width:] = gh[rows:].astype(jnp.bfloat16)


def end_kernel(frames, slot_len, lengths, own_ref, gain_ref, sum_ref, got_ref, both_ref):
    rows, width = own_ref.shape[0], own_ref.shape[1] // 2
    valid = valid_rows(rows, frames, slot_len, lengths, False)
    x = own_ref[:, :width].astype(jnp.float32)
    mixed = sum_ref[:, :width] + got_ref[:, :width].astype(jnp.float32)
    both_ref[:, :width] = (valid * (x + mixed)).astype(jnp.bfloat16)
    gh = (sum_ref[:, width:] + got_ref[:, width:].astype(jnp.float32)) * gain_ref[...].reshape(1, -1)
    inv = inv_rms_of(x)
    inner = jnp.mean(gh * x, axis=-1, keepdims=True)
    gy = own_ref[:, width:].astype(jnp.float32) * valid
    dx = gy + inv * (gh - x * inv * inv * inner)
    both_ref[:, width : 2 * width] = dx.astype(jnp.bfloat16)


def call(kernel, outs, scratch, flops, *operands, behind=()):
    size = sum(o.size * o.dtype.itemsize for o in outs + operands)
    return pl.pallas_call(
        kernel,
        out_shape=outs,
        in_specs=[
            pl.BlockSpec(memory_space=pltpu.SMEM if o.dtype == jnp.int32 else pltpu.VMEM)
            for o in operands
        ]
        + [pl.BlockSpec(memory_space=pl.ANY)] * len(behind),
        scratch_shapes=scratch,
        compiler_params=pltpu.CompilerParams(vmem_limit_bytes=VMEM_LIMIT),
        cost_estimate=pl.CostEstimate(flops=flops, bytes_accessed=size, transcendentals=0),
    )(*operands, *behind)


def shift(v, axis, by):
    size = lax.axis_size(axis)
    return lax.ppermute(v, axis, [(i, (i + by) % size) for i in range(size)])


def exchange(v, axes):
    return lax.all_to_all(v, axes, split_axis=0, concat_axis=0, tiled=True)


def after(v, first):
    return lax.optimization_barrier((v, first))[0]


def per_device(frames_in, cotangent, norm_gain, w_qkv, w_out, lengths):
    bf, f32 = jnp.bfloat16, jnp.float32
    core_at = lax.axis_index("core")
    ys, cores, zs = (lax.axis_size(axis) for axis in ("y", "core", "z"))
    tms, mics = XS * zs, ys * cores
    frame_dev, width = frames_in.shape[1:]
    frames = frame_dev // mics
    rows = mics * frames
    piece, wide = w_qkv.shape
    half, cut = wide // cores, width // cores
    spots = (frames, frame_dev * tms // SESS)

    mine = [lax.dynamic_slice(w_qkv, (0, j * width + core_at * cut), (piece, cut)) for j in range(3)]
    mine.append(lax.dynamic_slice(w_out, (0, core_at * cut), (piece, cut)))
    mine = jnp.concatenate(mine, axis=1)
    block = exchange(jnp.broadcast_to(mine[None], (zs, piece, half + cut)), "z")
    block = block.reshape(zs * piece, half + cut)
    up, down = shift(block, "x", 1), shift(block, "x", -1)
    mid = zs * piece // 2
    far_low, far_high = shift(up[:mid], "x", 1), shift(down[mid:], "x", -1)

    both = jnp.concatenate(
        [frames_in.reshape(mics, frames, width), cotangent.reshape(mics, frames, width)], axis=2
    )
    own = exchange(after(both, block), MIC).reshape(rows, 2 * width)
    near = shift(own, "core", 1)

    def shape(dims, dtype):
        return jax.ShapeDtypeStruct(dims, dtype)

    heads = width // HD // cores
    results = (
        shape((rows, half), bf),
        shape((heads // 2, 2 * rows, rows), bf),
        shape((rows, cut), bf),
    )
    own_qkv, own_p, own_att, w, wo, wo_give = call(
        lambda *refs: own_kernel(*spots, *refs),
        results + (shape((width, half), bf), shape((cut, cut), bf), shape((cut, cut), bf)),
        (pltpu.VMEM((width, cut), bf),),
        OWN_COST,
        lengths, own, norm_gain, block, up, down, far_low, far_high,
    )
    near_qkv, near_p, near_att, give, gw = call(
        lambda *refs: near_kernel(*spots, *refs),
        results + (shape((cut, cut), bf), shape((width, cut), bf)),
        (),
        NEAR_COST,
        lengths, own, near, norm_gain, w, own_att,
    )

    got = shift(give, "core", 1)
    wo_got = shift(wo_give, "core", 1)
    term = lax.dynamic_update_slice(gw, got, ((1 - core_at) * cut, 0))

    sum_part, other_part = call(
        lambda *refs: bwd_kernel(*spots, *refs),
        (shape((rows, 2 * width), f32), shape((rows, 2 * width), bf)),
        (pltpu.VMEM((2 * rows, half), bf),),
        BWD_COST,
        lengths, own, near, wo, wo_got, own_att, near_att, own_qkv, near_qkv, own_p, near_p, w,
        behind=(term,),
    )
    term = exchange(term.reshape(tms, piece, cut), TM)
    term = jnp.sum(term.astype(f32), axis=0).astype(bf)
    got_part = shift(other_part, "core", 1)
    low = piece // frames
    (done,) = call(
        lambda *refs: end_kernel(*spots, *refs),
        (shape((rows, 2 * width + low * cut), bf),),
        (),
        END_COST,
        lengths, own, norm_gain, sum_part, got_part,
    )

    term = term.reshape(low, frames, cut).transpose(1, 0, 2).reshape(frames, low * cut)
    term = jnp.broadcast_to(term[None], (mics, frames, low * cut))
    sent = done.reshape(mics, frames, 2 * width + low * cut)
    sent = exchange(lax.dynamic_update_slice(sent, term, (0, 0, 2 * width)), MIC)
    out = sent[:, :, :width].reshape(1, frame_dev, width)
    dx = sent[:, :, width : 2 * width].reshape(1, frame_dev, width)
    term = jnp.sum(sent[:, :, 2 * width :].astype(f32).reshape(ys, cores, frames, low, cut), axis=0)
    grad_wout = term.transpose(2, 1, 0, 3).reshape(piece, width)
    return (out, dx, grad_wout)


def solution(mesh):
    grid = Mesh(mesh.devices.reshape(-1, 2, XS, mesh.devices.shape[1] // XS), ("y", "core", "x", "z"))
    return jax.shard_map(
        per_device,
        mesh=grid,
        in_specs=(P(MIC, TM, None), P(MIC, TM, None), P(), P(TM, None), P(TM, None), P()),
        out_specs=(P(MIC, TM, None), P(MIC, TM, None), P(TM, None)),
        check_vma=False,
    )
```
